32 devices in a mesh: segment: 2 (over x), expert: 16 (over z, y, core).
Axes of the slice: x: 2, y: 2, z: 4, core: 2. Of those that a mesh axis runs over, the one named last changes fastest.
Arguments:
- states: bfloat16 [2, 64, 7168], P('segment', 'expert'), may hold values from -6 to 6
- routing: int32 [2, 2, 64, 2], P('segment', None, 'expert'), may hold values from 0 to 3, all different within a row; in each aligned block of 4 rows (0 to 3, 4 to 7, ..., all dimensions but the last counted through in order) at most 4 rows name the same one
- route_weight: bfloat16 [2, 2, 64, 2], P('segment', None, 'expert'), may hold values from 0.19921875 to 1
- norm_gain: float32 [2, 7168], P('segment'), may hold values from 0.1 to 1.9
- gate_proj: bfloat16 [2, 7168, 4096], P('segment', None, 'expert'), may hold values from -0.0625 to 0.0625
- up_proj: bfloat16 [2, 7168, 4096], P('segment', None, 'expert'), may hold values from -0.0625 to 0.0625
- down_proj: bfloat16 [2, 4096, 7168], P('segment', 'expert'), may hold values from -0.1875 to 0.1875
Outputs:
- new_states: bfloat16 [2, 64, 7168], P('segment', 'expert')
The draws below stay inside these ranges and needn't reach their ends.
Inputs may be any that keep to these rules, and one draw needn't show every extreme that they name: `routing`: in each aligned block of 4 rows (the rows of one device for one layer and pass) no expert is named by more than 4 rows, and some block reaches 4; each row names 2 different experts.
All inputs are finite; a program needn't handle non-finite values.
Results may differ from the reference program's by a relative error of at most 0.015.
Values may be sent and summed in bfloat16 or wider, within the bound.
No kernel may reach another device: no remote copies, remote signals or barrier semaphores. Data moves between devices by JAX's collectives and lax.ppermute only.
A program may use at most 64 MiB of HBM per device.

```python
import math
import jax
import jax.numpy as jnp
import numpy as np
from jax import lax

D = 7168
HID_DEV = 256
GROUP = 4
TOP = 2
PASSES = 2
RD = 4
EXPERT_HID = 1024
EXPERTS = 4
CAP = 4
ROWS = 64
MB = 2
N_SEGMENT = 2
N_EXPERT = 16


def level_of(rng, extent, cuts, least, top_value):
    def one(dim, blocks):
        steps = jax.random.uniform(jax.random.fold_in(jax.random.fold_in(rng, 6), dim), (blocks,), jnp.float32, least / len(cuts), top_value / len(cuts))
        return jnp.repeat(jnp.exp(steps), extent[dim] // blocks).reshape((-1,) + (1,) * (len(extent) - dim - 1))

    factor_of = one(*cuts[0])
    for cut in cuts[1:]:
        factor_of = factor_of * one(*cut)
    return factor_of


def assign_block(rng, own, number, rows, amount, top, reach, lean):
    ranking = jax.random.permutation(rng, amount)
    packed, usual = load_shares(amount, rows * top, reach, lean, True), load_shares(amount, rows * top, reach, lean, False)
    places = jnp.arange(amount)

    def named(lengths, turn):
        used = int((lengths > 0).sum())
        fixed = max(1, used // 4)
        shifted = fixed + (places - fixed + turn * (used - fixed)) % max(1, amount - fixed)
        return jnp.zeros((amount,), jnp.int32).at[ranking[jnp.where(places < fixed, places, shifted)]].set(jnp.asarray(lengths, jnp.int32))

    lengths = jnp.where(number % 4 == 0, named(packed, number // 4), named(usual, number - number // 4 - 1))
    mixed = jax.random.permutation(jax.random.fold_in(own, 3), amount)
    donor, taker = mixed[0:amount // 2 * 2:2], mixed[1:amount // 2 * 2:2]
    margin = jnp.minimum(lengths[donor] - 1, reach - lengths[taker]) // 2
    margin = jnp.where((donor == ranking[0]) | (taker == ranking[0]) | (lengths[taker] == 0), 0, jnp.maximum(margin, 0))
    shifted = jax.random.randint(jax.random.fold_in(own, 4), (amount // 2,), 0, 1 << 20) % (margin + 1)
    lengths = lengths.at[donor].add(-shifted).at[taker].add(shifted)
    members = jnp.searchsorted(jnp.cumsum(lengths), jnp.arange(rows * top), side="right").astype(jnp.int32)
    table = members.reshape(top, rows).T
    table = table[jax.random.permutation(jax.random.fold_in(own, 1), rows)]
    turn = jax.random.randint(jax.random.fold_in(own, 2), (rows, 1), 0, top)
    return jnp.take_along_axis(table, (jnp.arange(top)[None, :] + turn) % top, axis=1)


def load_shares(count, total, reach, skew, full):
    weights = [(1 << 20) // math.isqrt(standing ** skew) + 1 for standing in range(1, count + 1)]
    largest = reach if full else min(reach, max(-(-total // count), total * weights[0] // sum(weights)))
    least = 1 if total - largest >= count - 1 else 0
    given, surplus = [largest] + [least] * (count - 1), total - largest - least * (count - 1)
    while surplus > 0:
        movable = [i for i in range(1, count) if given[i] < largest] or [i for i in range(1, count) if given[i] < reach]
        whole, left = sum([weights[i] for i in movable]), surplus
        for i in movable:
            addition = min(reach - given[i], max(1, left * weights[i] // whole), surplus)
            given[i] = given[i] + addition
            surplus = surplus - addition
    return np.array(given)


def gaussian(own_key, extent, width, bound, cuts=(), held_as=jnp.bfloat16):
    entries = width * jax.random.normal(own_key, extent, jnp.float32)
    if cuts:
        entries = entries * level_of(own_key, extent, cuts, -0.22, 0.18)
    return jnp.clip(entries, -bound, bound).astype(held_as)


def setup_inputs(seed: int = 0) -> dict:
    keys = jax.random.split(jax.random.key(seed), 8)
    states = gaussian(keys[0], (MB, ROWS, D), 1.0, 6.0, ((0, 2), (1, 16)))
    routing_keys = jax.random.split(jax.random.fold_in(keys[1], 1), MB * PASSES * ROWS // RD)
    routing_turns = jax.random.permutation(jax.random.fold_in(keys[1], 3), MB * PASSES * ROWS // RD)
    routing = jax.vmap(lambda own, number: assign_block(jax.random.fold_in(keys[1], 2), own, number, RD, EXPERTS, TOP, CAP, 2))(routing_keys, routing_turns).reshape((MB, PASSES, ROWS, TOP))
    route_weight = jnp.clip(0.19921875 + 0.80078125 * jax.random.uniform(keys[2], (MB, PASSES, ROWS, TOP), jnp.float32) ** level_of(keys[2], (MB, PASSES, ROWS, TOP), ((0, 2), (2, 16)), -0.2, 0.2), 0.19921875, 1.0).astype(jnp.bfloat16)
    norm_gain = jnp.clip(1.0 + 0.18 * jax.random.normal(keys[3], (MB, D), jnp.float32), 0.1, 1.9)
    gate_proj = gaussian(keys[4], (MB, D, EXPERTS * EXPERT_HID), D ** -0.5, 0.0625, ((0, 2), (2, 16)))
    up_proj = gaussian(keys[5], (MB, D, EXPERTS * EXPERT_HID), D ** -0.5, 0.0625, ((0, 2), (2, 16)))
    down_proj = gaussian(keys[6], (MB, EXPERTS * EXPERT_HID, D), EXPERT_HID ** -0.5, 0.1875, ((0, 2), (1, 16)))
    return {"states": states, "routing": routing, "route_weight": route_weight, "norm_gain": norm_gain, "gate_proj": gate_proj, "up_proj": up_proj, "down_proj": down_proj}


def apply_layer(current, routes, weights_now, gain_row, gate_mat, up_mat, down_mat):
    hidden_f = current.astype(jnp.float32)
    inv_rms = lax.rsqrt(lax.optimization_barrier(jnp.mean(hidden_f * hidden_f, axis=1, keepdims=True)) + 1e-06)
    normed = (hidden_f * inv_rms * gain_row).astype(jnp.bfloat16)
    slot_count = N_EXPERT * CAP
    summed = jnp.zeros(hidden_f.shape, jnp.float32)
    for expert in range(EXPERTS):
        picked = routes == expert
        member = jnp.any(picked, axis=1)
        weight_row = lax.optimization_barrier(jnp.sum(jnp.where(picked, weights_now.astype(jnp.float32), jnp.float32(0.0)), axis=1))
        where_rows = jnp.nonzero(member, size=slot_count, fill_value=0)[0]
        is_valid = jnp.arange(slot_count) < jnp.sum(member.astype(jnp.int32))
        chosen = normed[where_rows]
        first_col = expert * EXPERT_HID
        gate_cols = gate_mat[:, first_col:first_col + EXPERT_HID]
        up_cols = up_mat[:, first_col:first_col + EXPERT_HID]
        down_rows = down_mat[first_col:first_col + EXPERT_HID, :]
        gated = jnp.dot(chosen, gate_cols, preferred_element_type=jnp.float32)
        up_part = jnp.dot(chosen, up_cols, preferred_element_type=jnp.float32)
        inner_act = (jax.nn.silu(gated) * up_part).astype(jnp.bfloat16)
        slice_terms = jnp.einsum('sgh,ghd->sgd', inner_act.reshape(slot_count, GROUP, HID_DEV).astype(jnp.float32), down_rows.reshape(GROUP, HID_DEV, D).astype(jnp.float32))
        slot_weight = jnp.where(is_valid, weight_row[where_rows], jnp.float32(0.0))
        term_vals = (slot_weight[:, None, None] * slice_terms).astype(jnp.bfloat16).astype(jnp.float32)
        summed = summed.at[where_rows].add(lax.optimization_barrier(jnp.sum(term_vals, axis=1)))
    return (hidden_f + summed).astype(jnp.bfloat16)

def reference(states, routing, route_weight, norm_gain, gate_proj, up_proj, down_proj):
    outputs = []
    for micro_idx in range(N_SEGMENT):
        current = states[micro_idx]
        for offset in range(PASSES):
            layer_no = (micro_idx + offset) % N_SEGMENT
            current = apply_layer(current, routing[layer_no, offset], route_weight[layer_no, offset], norm_gain[layer_no], gate_proj[layer_no], up_proj[layer_no], down_proj[layer_no])
        outputs.append(current)
    return jnp.roll(jnp.stack(outputs), PASSES, axis=0)
```

```python
import jax
import jax.numpy as jnp
from jax import lax
from jax.sharding import PartitionSpec as P

GROUP = 4


def shifted(value, axis, steps):
    count = lax.axis_size(axis)
    pairs = [(source, (source + steps) % count) for source in range(count)]
    return lax.ppermute(value, axis, pairs)


def on_device(states, routing, route_weight, norm_gain, gate_proj, up_proj, down_proj):
    owners = lax.axis_size("expert")
    experts = owners // GROUP
    passes_count = routing.shape[1]
    gain_row = norm_gain[0]
    gate_mat = gate_proj[0]
    up_mat = up_proj[0]
    down_mat = down_proj[0]
    expert_ids = jnp.arange(experts, dtype=jnp.int32)

    picked = routing[0][..., None] == expert_ids
    dense = jnp.sum(jnp.where(picked, route_weight[0][..., None].astype(jnp.float32), 0.0), axis=2)
    dense = lax.all_gather(dense.astype(jnp.bfloat16), "expert", axis=1, tiled=True)
    mine = lax.axis_index("expert") // GROUP
    row_weight = lax.dynamic_index_in_dim(dense, mine, 2, keepdims=True).astype(jnp.float32)

    current = states[0]
    for step_no in range(passes_count):
        current_f = current.astype(jnp.float32)
        inv_rms = lax.rsqrt(jnp.mean(current_f * current_f, axis=1, keepdims=True) + 1e-06)
        normed = (current_f * inv_rms * gain_row).astype(jnp.bfloat16)
        rows = lax.all_gather(normed, "expert", axis=0, tiled=True)
        gated = jnp.dot(rows, gate_mat, preferred_element_type=jnp.float32)
        up_part = jnp.dot(rows, up_mat, preferred_element_type=jnp.float32)
        inner_act = (jax.nn.silu(gated) * up_part).astype(jnp.bfloat16)
        partial_out = jnp.dot(inner_act, down_mat, preferred_element_type=jnp.float32)
        weight = row_weight[step_no]
        terms = jnp.where(weight > 0.0, weight * partial_out, 0.0).astype(jnp.bfloat16)
        branch_sum = lax.psum_scatter(terms, "expert", scatter_dimension=0, tiled=True)
        updated = (current_f + branch_sum.astype(jnp.float32)).astype(jnp.bfloat16)
        current = shifted(updated, "segment", 1)
    return current[None]


def solution(mesh):
    return jax.shard_map(
        on_device,
        mesh=mesh,
        in_specs=(
            P("segment", "expert", None),
            P("segment", None, "expert", None),
            P("segment", None, "expert", None),
            P("segment", None),
            P("segment", None, "expert"),
            P("segment", None, "expert"),
            P("segment", "expert", None),
        ),
        out_specs=P("segment", "expert", None),
        check_vma=False,
    )
```

```python
import jax
import jax.numpy as jnp
from jax import lax
from jax.sharding import PartitionSpec as P

GROUP = 4
LANES = 128


def exchange(value, flip, hop):
    segments, owners = lax.axis_size("segment"), lax.axis_size("expert")
    if flip == 0 and hop % segments == 0:
        return value
    pairs = []
    for seg in range(segments):
        for own in range(owners):
            target = (seg + hop) % segments * owners + (own ^ flip)
            pairs.append((seg * owners + own, target))
    return lax.ppermute(value, ("segment", "expert"), pairs)


def gather(block, hop):
    depth = lax.axis_size("expert") // GROUP
    columns = [exchange(block, dz * GROUP, hop) for dz in range(depth)]
    planes = []
    for got in columns:
        planes.append((got, exchange(got, 2, 0)))
    blocks = []
    for near, far in planes:
        blocks += [near, exchange(near, 1, 0), far, exchange(far, 1, 0)]
    return blocks


def on_device(states, routing, route_weight, norm_gain, gate_proj, up_proj, down_proj):
    owners = lax.axis_size("expert")
    experts = owners // GROUP
    depth = owners // GROUP
    row_dev = states.shape[1]
    model_dim = states.shape[2]
    passes_count = routing.shape[1]
    gain_row = norm_gain[0]
    gate_mat = gate_proj[0]
    up_mat = up_proj[0]
    down_mat = down_proj[0]
    expert_ids = jnp.arange(experts, dtype=jnp.int32)

    picked = routing[0][..., None] == expert_ids
    dense = jnp.sum(jnp.where(picked, route_weight[0][..., None].astype(jnp.float32), 0.0), axis=2)
    dense = jnp.moveaxis(dense, 0, 1).reshape(row_dev, passes_count * experts).astype(jnp.bfloat16)
    dense = jnp.pad(dense, ((0, 0), (0, LANES - passes_count * experts)))
    mine = lax.axis_index("expert") // GROUP

    current = states[0]
    blocks = gather(jnp.concatenate([current, dense], axis=1), 0)
    tail = jnp.concatenate([block[:, model_dim:] for block in blocks], axis=0)
    blocks = [block[:, :model_dim] for block in blocks]

    for step_no in range(passes_count):
        if step_no > 0:
            blocks = gather(current, 1)
            current = blocks[0]
        hidden = jnp.concatenate(blocks, axis=0).astype(jnp.float32)
        inv_rms = lax.rsqrt(jnp.mean(hidden * hidden, axis=1, keepdims=True) + 1e-06)
        rows = (hidden * inv_rms * gain_row).astype(jnp.bfloat16)
        gated = jnp.dot(rows, gate_mat, preferred_element_type=jnp.float32)
        up_part = jnp.dot(rows, up_mat, preferred_element_type=jnp.float32)
        inner_act = (jax.nn.silu(gated) * up_part).astype(jnp.bfloat16)
        partial_out = jnp.dot(inner_act, down_mat, preferred_element_type=jnp.float32)
        weight = lax.dynamic_slice_in_dim(tail, step_no * experts + mine, 1, 1).astype(jnp.float32)
        terms = jnp.where(weight > 0.0, weight * partial_out, 0.0).astype(jnp.bfloat16)

        terms = terms.reshape(depth, 2, 2, row_dev, model_dim)
        other = exchange(terms[:, :, 1], 1, 0)
        chip = terms[:, :, 0].astype(jnp.float32) + other.astype(jnp.float32)
        other = exchange(chip[:, 1].astype(jnp.bfloat16), 2, 0)
        plane = chip[:, 0] + other.astype(jnp.float32)
        last = step_no == passes_count - 1
        if last:
            current = exchange(current, 0, 1)
        total = current.astype(jnp.float32)
        for dz in range(depth):
            part = plane[dz] if dz == 0 and not last else plane[dz].astype(jnp.bfloat16)
            total = total + exchange(part, dz * GROUP, 1 if last else 0).astype(jnp.float32)
        current = total.astype(jnp.bfloat16)
    return current[None]


def solution(mesh):
    return jax.shard_map(
        on_device,
        mesh=mesh,
        in_specs=(
            P("segment", "expert", None),
            P("segment", None, "expert", None),
            P("segment", None, "expert", None),
            P("segment", None),
            P("segment", None, "expert"),
            P("segment", None, "expert"),
            P("segment", "expert", None),
        ),
        out_specs=P("segment", "expert", None),
        check_vma=False,
    )
```

```python
import jax
import jax.numpy as jnp
from jax import lax
from jax.experimental import pallas as pl
from jax.experimental.pallas import tpu as pltpu
from jax.sharding import PartitionSpec as P

GROUP = 4
LANES = 128
CHUNK = 1024


def step_flips(owners):
    bits = [1 << place for place in range(1, owners.bit_length() - 1)]
    even = bits[::-1]
    odd = bits[:1] + bits[:0:-1]
    return list(zip(even, odd))


def exchange(value, flips, hop):
    segments, owners = lax.axis_size("segment"), lax.axis_size("expert")
    if flips == (0, 0) and hop % segments == 0:
        return value
    pairs = []
    for seg in range(segments):
        for own in range(owners):
            target = (seg + hop) % segments * owners + (own ^ flips[own % 2])
            pairs.append((seg * owners + own, target))
    return lax.ppermute(value, ("segment", "expert"), pairs)


def mlp_kernel(col_ref, own_ref, far_ref, own_w_ref, far_w_ref, gain_ref, gate_ref, up_ref, down_ref,
               own_out, far_out, rows_ref):
    half = own_ref.shape[0]
    dim = gate_ref.shape[1]
    for part, ref in enumerate((own_ref, far_ref)):
        square = jnp.zeros((half, LANES), jnp.float32)
        for start in range(0, dim, LANES):
            piece = ref[:, start:start + LANES].astype(jnp.float32)
            square += piece * piece
        inv = lax.rsqrt(jnp.sum(square, axis=1, keepdims=True) / dim + 1e-06)
        for start in range(0, dim, CHUNK):
            piece = ref[:, start:start + CHUNK].astype(jnp.float32)
            scaled = piece * inv * gain_ref[:, start:start + CHUNK]
            rows_ref[part * half:(part + 1) * half, start:start + CHUNK] = scaled.astype(jnp.bfloat16)
    gated = jnp.zeros((2 * half, gate_ref.shape[2]), jnp.float32)
    up_part = jnp.zeros((2 * half, gate_ref.shape[2]), jnp.float32)
    for start in range(0, dim, CHUNK):
        rows = rows_ref[:, start:start + CHUNK]
        gated += jnp.dot(rows, gate_ref[0, start:start + CHUNK, :], preferred_element_type=jnp.float32)
        up_part += jnp.dot(rows, up_ref[0, start:start + CHUNK, :], preferred_element_type=jnp.float32)
    inner = (gated / (1.0 + jnp.exp(-gated)) * up_part).astype(jnp.bfloat16)
    lane = lax.broadcasted_iota(jnp.int32, (half, LANES), 1)
    weights = []
    for ref in (own_w_ref, far_w_ref):
        here = jnp.where(lane == col_ref[0], ref[...].astype(jnp.float32), 0.0)
        weights.append(jnp.sum(here, axis=1, keepdims=True))
    for start in range(0, dim, CHUNK):
        terms = jnp.dot(inner, down_ref[0, :, start:start + CHUNK], preferred_element_type=jnp.float32)
        for part, out in enumerate((own_out, far_out)):
            weight = weights[part]
            chosen = jnp.where(weight > 0.0, weight * terms[part * half:(part + 1) * half], 0.0)
            out[:, start:start + CHUNK] = chosen.astype(jnp.bfloat16)


def mlp(col, own, far, own_w, far_w, gain, gate, up, down):
    half, dim = own.shape[0], gate.shape[1]
    vmem = pl.BlockSpec(memory_space=pltpu.VMEM)
    return pl.pallas_call(
        mlp_kernel,
        out_shape=[jax.ShapeDtypeStruct((half, dim), jnp.bfloat16)] * 2,
        in_specs=[pl.BlockSpec(memory_space=pltpu.SMEM)] + [vmem] * 8,
        out_specs=[vmem] * 2,
        scratch_shapes=[pltpu.VMEM((2 * half, dim), jnp.bfloat16)],
        compiler_params=pltpu.CompilerParams(vmem_limit_bytes=24 * 1024 * 1024),
        cost_estimate=pl.CostEstimate(
            flops=12 * half * dim * gate.shape[2], bytes_accessed=6 * dim * gate.shape[2], transcendentals=0
        ),
    )(col, own, far, own_w, far_w, gain, gate, up, down)


def on_device(states, routing, route_weight, norm_gain, gate_proj, up_proj, down_proj):
    owners = lax.axis_size("expert")
    experts = owners // GROUP
    row_dev = states.shape[1]
    model_dim = states.shape[2]
    passes_count = routing.shape[1]
    expert_ids = jnp.arange(experts, dtype=jnp.int32)
    steps = step_flips(owners)
    gate, up, down = [
        pltpu.with_memory_space_constraint(w, pltpu.VMEM) for w in (gate_proj, up_proj, down_proj)
    ]

    picked = routing[0][..., None] == expert_ids
    dense = jnp.sum(jnp.where(picked, route_weight[0][..., None].astype(jnp.float32), 0.0), axis=2)
    dense = jnp.moveaxis(dense, 0, 1).reshape(row_dev, passes_count * experts).astype(jnp.bfloat16)
    dense = jnp.pad(dense, ((0, 0), (0, LANES - passes_count * experts)))
    mine = lax.axis_index("expert") // GROUP

    current = states[0]
    for step_no in range(passes_count):
        hop = 1 if step_no > 0 else 0
        last = step_no == passes_count - 1
        block = exchange(current, (0, 0), hop)
        own = jnp.concatenate([block, exchange(current, steps[0], hop)], axis=0)
        if step_no == 0:
            tail = jnp.concatenate([dense, exchange(dense, steps[0], 0)], axis=0)
            own = jnp.concatenate([own, tail], axis=1)
        for flips in steps[1:]:
            own = jnp.concatenate([own, exchange(own, flips, 0)], axis=0)
        far = exchange(own, (1, 1), 0)
        if step_no == 0:
            own_w, far_w = own[:, model_dim:], far[:, model_dim:]
        col = (step_no * experts + mine).astype(jnp.int32).reshape(1)
        kept, sent = mlp(col, own, far, own_w, far_w, norm_gain, gate, up, down)

        kept = kept.astype(jnp.float32) + exchange(sent, (1, 1), 0).astype(jnp.float32)
        for flips in steps[:0:-1]:
            middle = kept.shape[0] // 2
            sent = kept[middle:].astype(jnp.bfloat16)
            kept = kept[:middle] + exchange(sent, flips, 0).astype(jnp.float32)
        if last:
            block = exchange(block, (0, 0), 1)
            near = exchange(kept[:row_dev].astype(jnp.bfloat16), (0, 0), 1)
        else:
            near = kept[:row_dev]
        other = exchange(kept[row_dev:].astype(jnp.bfloat16), steps[0], 1 if last else 0)
        total = block.astype(jnp.float32) + near.astype(jnp.float32) + other.astype(jnp.float32)
        current = total.astype(jnp.bfloat16)
    return current[None]


def solution(mesh):
    return jax.shard_map(
        on_device,
        mesh=mesh,
        in_specs=(
            P("segment", "expert", None),
            P("segment", None, "expert", None),
            P("segment", None, "expert", None),
            P("segment", None),
            P("segment", None, "expert"),
            P("segment", None, "expert"),
            P("segment", "expert", None),
        ),
        out_specs=P("segment", "expert", None),
        check_vma=False,
    )
```

```python
import jax
import jax.numpy as jnp
from jax import lax
from jax.experimental import pallas as pl
from jax.experimental.pallas import tpu as pltpu
from jax.sharding import PartitionSpec as P

GROUP = 4
LANES = 128
CHUNK = 1024
VMEM_LIMIT = 24 * 1024 * 1024


def exchange(value, flip, hop):
    segments, owners = lax.axis_size("segment"), lax.axis_size("expert")
    if flip == 0 and hop % segments == 0:
        return value
    pairs = []
    for seg in range(segments):
        for own in range(owners):
            target = (seg + hop) % segments * owners + (own ^ flip)
            pairs.append((seg * owners + own, target))
    return lax.ppermute(value, ("segment", "expert"), pairs)


def load_kernel(gate_ref, up_ref, down_ref, gate_out, up_out, down_out, sems):
    copies = [
        pltpu.make_async_copy(source, target, sems.at[place])
        for place, (source, target) in enumerate(((gate_ref, gate_out), (up_ref, up_out), (down_ref, down_out)))
    ]
    for copy in copies:
        copy.start()
    for copy in copies:
        copy.wait()


def load(weights):
    return pl.pallas_call(
        load_kernel,
        out_shape=[pltpu.VMEM(w.shape, w.dtype) for w in weights],
        in_specs=[pl.BlockSpec(memory_space=pltpu.HBM)] * 3,
        out_specs=[pl.BlockSpec(memory_space=pltpu.VMEM)] * 3,
        scratch_shapes=[pltpu.SemaphoreType.DMA((3,))],
        compiler_params=pltpu.CompilerParams(vmem_limit_bytes=VMEM_LIMIT),
        cost_estimate=pl.CostEstimate(
            flops=0, bytes_accessed=sum(2 * w.size for w in weights), transcendentals=0
        ),
    )(*[pltpu.with_memory_space_constraint(w, pltpu.HBM) for w in weights])


def mlp_kernel(own_ref, far_ref, gain_ref, gate_ref, up_ref, down_ref, own_out, far_out, rows_ref):
    half = own_ref.shape[0]
    dim = gate_ref.shape[1]
    for part, ref in enumerate((own_ref, far_ref)):
        square = jnp.zeros((half, LANES), jnp.float32)
        for start in range(0, dim, LANES):
            piece = ref[:, start:start + LANES].astype(jnp.float32)
            square += piece * piece
        inv = lax.rsqrt(jnp.sum(square, axis=1, keepdims=True) / dim + 1e-06)
        for start in range(0, dim, CHUNK):
            piece = ref[:, start:start + CHUNK].astype(jnp.float32)
            scaled = piece * inv * gain_ref[:, start:start + CHUNK]
            rows_ref[part * half:(part + 1) * half, start:start + CHUNK] = scaled.astype(jnp.bfloat16)
    gated = jnp.zeros((2 * half, gate_ref.shape[2]), jnp.float32)
    up_part = jnp.zeros((2 * half, gate_ref.shape[2]), jnp.float32)
    for start in range(0, dim, CHUNK):
        rows = rows_ref[:, start:start + CHUNK]
        gated += jnp.dot(rows, gate_ref[0, start:start + CHUNK, :], preferred_element_type=jnp.float32)
        up_part += jnp.dot(rows, up_ref[0, start:start + CHUNK, :], preferred_element_type=jnp.float32)
    inner = (gated / (1.0 + jnp.exp(-gated)) * up_part).astype(jnp.bfloat16)
    for start in range(0, dim, CHUNK):
        terms = jnp.dot(inner, down_ref[0, :, start:start + CHUNK], preferred_element_type=jnp.float32)
        own_out[:, start:start + CHUNK] = terms[:half].astype(jnp.bfloat16)
        far_out[:, start:start + CHUNK] = terms[half:].astype(jnp.bfloat16)


def mlp(own, far, gain, gate, up, down):
    half, dim = own.shape
    vmem = pl.BlockSpec(memory_space=pltpu.VMEM)
    gate, up, down = [pltpu.with_memory_space_constraint(w, pltpu.VMEM) for w in (gate, up, down)]
    return pl.pallas_call(
        mlp_kernel,
        out_shape=[jax.ShapeDtypeStruct((half, dim), jnp.bfloat16)] * 2,
        in_specs=[vmem] * 6,
        out_specs=[vmem] * 2,
        scratch_shapes=[pltpu.VMEM((2 * half, dim), jnp.bfloat16)],
        compiler_params=pltpu.CompilerParams(vmem_limit_bytes=VMEM_LIMIT),
        cost_estimate=pl.CostEstimate(
            flops=12 * half * dim * gate.shape[2], bytes_accessed=6 * dim * gate.shape[2], transcendentals=0
        ),
    )(own, far, gain, gate, up, down)


def on_device(states, routing, route_weight, norm_gain, gate_proj, up_proj, down_proj):
    owners = lax.axis_size("expert")
    experts = owners // GROUP
    row_dev = states.shape[1]
    passes_count = routing.shape[1]
    flips = range(0, owners, 2)
    mine = lax.axis_index("expert") // GROUP
    expert_ids = jnp.arange(experts, dtype=jnp.int32)
    gate, up, down = load((gate_proj, up_proj, down_proj))

    picked = routing[0][..., None] == expert_ids
    dense = jnp.sum(jnp.where(picked, route_weight[0][..., None].astype(jnp.float32), 0.0), axis=2)
    last_dense = exchange(dense[-1].astype(jnp.bfloat16), 0, 1).astype(jnp.float32)

    current = states[0]
    for step_no in range(passes_count):
        last = step_no == passes_count - 1
        hop, out_hop = int(step_no > 0), int(last)
        blocks = [exchange(current, flip, hop) for flip in flips]
        own = jnp.concatenate(blocks, axis=0)
        if step_no == 0:
            own, gate, up, down = lax.optimization_barrier((own, gate, up, down))
        far = exchange(own, 1, 0)
        kept, sent = mlp(own, far, norm_gain, gate, up, down)
        chip = kept.astype(jnp.float32) + exchange(sent, 1, 0).astype(jnp.float32)
        chip = chip.astype(jnp.bfloat16)

        total = exchange(current, 0, hop + out_hop).astype(jnp.float32)
        weights = last_dense if last else dense[step_no]
        for place, flip in enumerate(flips):
            part = exchange(chip[place * row_dev:(place + 1) * row_dev], flip, out_hop).astype(jnp.float32)
            here = expert_ids == (mine ^ (flip // GROUP))
            weight = jnp.sum(jnp.where(here, weights, 0.0), axis=1, keepdims=True)
            total = total + jnp.where(weight > 0.0, weight * part, 0.0)
        current = total.astype(jnp.bfloat16)
    return current[None]


def solution(mesh):
    return jax.shard_map(
        on_device,
        mesh=mesh,
        in_specs=(
            P("segment", "expert", None),
            P("segment", None, "expert", None),
            P("segment", None, "expert", None),
            P("segment", None),
            P("segment", None, "expert"),
            P("segment", None, "expert"),
            P("segment", "expert", None),
        ),
        out_specs=P("segment", "expert", None),
        check_vma=False,
    )
```

```python
import jax
import jax.numpy as jnp
from jax import lax
from jax.experimental import pallas as pl
from jax.experimental.pallas import tpu as pltpu
from jax.sharding import PartitionSpec as P

GROUP = 4
LANES = 128
CHUNK = 1024
VMEM_LIMIT = 24 * 1024 * 1024


def exchange(value, flip, hop):
    segments, owners = lax.axis_size("segment"), lax.axis_size("expert")
    if flip == 0 and hop % segments == 0:
        return value
    pairs = []
    for seg in range(segments):
        for own in range(owners):
            target = (seg + hop) % segments * owners + (own ^ flip)
            pairs.append((seg * owners + own, target))
    return lax.ppermute(value, ("segment", "expert"), pairs)


def mlp_kernel(own_ref, far_ref, gain_ref, gate_hbm, up_hbm, down_hbm, own_out, far_out,
               rows_ref, gate_ref, up_ref, down_ref, sems):
    half, dim = own_ref.shape
    starts = range(0, dim, CHUNK)
    loads = {}
    for place, start in enumerate(starts):
        span = pl.ds(start, CHUNK)
        loads["gate", start] = pltpu.make_async_copy(gate_hbm.at[0, span, :], gate_ref.at[span, :], sems.at[0, place])
        loads["up", start] = pltpu.make_async_copy(up_hbm.at[0, span, :], up_ref.at[span, :], sems.at[1, place])
        loads["gate", start].start()
        loads["up", start].start()
    for place, start in enumerate(starts):
        span = pl.ds(start, CHUNK)
        loads["down", start] = pltpu.make_async_copy(
            down_hbm.at[0, :, span], down_ref.at[:, span], sems.at[2, place])
        loads["down", start].start()
    for part, ref in enumerate((own_ref, far_ref)):
        square = jnp.zeros((half, LANES), jnp.float32)
        for start in range(0, dim, LANES):
            piece = ref[:, start:start + LANES].astype(jnp.float32)
            square += piece * piece
        inv = lax.rsqrt(jnp.sum(square, axis=1, keepdims=True) / dim + 1e-06)
        for start in starts:
            piece = ref[:, start:start + CHUNK].astype(jnp.float32)
            scaled = piece * inv * gain_ref[:, start:start + CHUNK]
            rows_ref[part * half:(part + 1) * half, start:start + CHUNK] = scaled.astype(jnp.bfloat16)
    gated = jnp.zeros((2 * half, gate_ref.shape[1]), jnp.float32)
    up_part = jnp.zeros((2 * half, gate_ref.shape[1]), jnp.float32)
    for start in starts:
        rows = rows_ref[:, start:start + CHUNK]
        loads["gate", start].wait()
        gated += jnp.dot(rows, gate_ref[start:start + CHUNK, :], preferred_element_type=jnp.float32)
        loads["up", start].wait()
        up_part += jnp.dot(rows, up_ref[start:start + CHUNK, :], preferred_element_type=jnp.float32)
    inner = (gated / (1.0 + jnp.exp(-gated)) * up_part).astype(jnp.bfloat16)
    for start in starts:
        loads["down", start].wait()
        terms = jnp.dot(inner, down_ref[:, start:start + CHUNK], preferred_element_type=jnp.float32)
        own_out[:, start:start + CHUNK] = terms[:half].astype(jnp.bfloat16)
        far_out[:, start:start + CHUNK] = terms[half:].astype(jnp.bfloat16)


def mlp(own, far, gain, gate, up, down):
    half, dim = own.shape
    hidden = gate.shape[2]
    vmem = pl.BlockSpec(memory_space=pltpu.VMEM)
    hbm = pl.BlockSpec(memory_space=pltpu.HBM)
    gate, up, down = [pltpu.with_memory_space_constraint(w, pltpu.HBM) for w in (gate, up, down)]
    return pl.pallas_call(
        mlp_kernel,
        out_shape=[jax.ShapeDtypeStruct((half, dim), jnp.bfloat16)] * 2,
        in_specs=[vmem] * 3 + [hbm] * 3,
        out_specs=[vmem] * 2,
        scratch_shapes=[
            pltpu.VMEM((2 * half, dim), jnp.bfloat16),
            pltpu.VMEM((dim, hidden), jnp.bfloat16),
            pltpu.VMEM((dim, hidden), jnp.bfloat16),
            pltpu.VMEM((hidden, dim), jnp.bfloat16),
            pltpu.SemaphoreType.DMA((3, dim // CHUNK)),
        ],
        compiler_params=pltpu.CompilerParams(vmem_limit_bytes=VMEM_LIMIT),
        cost_estimate=pl.CostEstimate(flops=12 * half * dim * hidden, bytes_accessed=6 * dim * hidden, transcendentals=0),
    )(own, far, gain, gate, up, down)


def on_device(states, routing, route_weight, norm_gain, gate_proj, up_proj, down_proj):
    owners = lax.axis_size("expert")
    experts = owners // GROUP
    row_dev, model_dim = states.shape[1:]
    passes_count = routing.shape[1]
    groups = [list(range(core, owners, 2)) for core in range(2)]
    expert_ids = jnp.arange(experts, dtype=jnp.int32)

    picked = routing[0][..., None] == expert_ids
    dense = jnp.sum(jnp.where(picked, route_weight[0][..., None].astype(jnp.float32), 0.0), axis=2)

    current = states[0]
    for step_no in range(passes_count):
        own = lax.all_gather(current, "expert", axis=0, tiled=True, axis_index_groups=groups)
        far = exchange(own, 1, 0)
        kept, sent = mlp(own, far, norm_gain, gate_proj, up_proj, down_proj)
        chip = kept.astype(jnp.float32) + exchange(sent, 1, 0).astype(jnp.float32)
        chip = chip.astype(jnp.bfloat16).reshape(owners // 2, row_dev, model_dim)
        parts = lax.all_to_all(chip, "expert", split_axis=0, concat_axis=0, tiled=True, axis_index_groups=groups)
        total = current.astype(jnp.float32)
        for place in range(owners // 2):
            weight = dense[step_no, :, place * 2 // GROUP, None]
            total = total + jnp.where(weight > 0.0, weight * parts[place].astype(jnp.float32), 0.0)
        current = exchange(total.astype(jnp.bfloat16), 0, 1)
    return current[None]


def solution(mesh):
    return jax.shard_map(
        on_device,
        mesh=mesh,
        in_specs=(
            P("segment", "expert", None),
            P("segment", None, "expert", None),
            P("segment", None, "expert", None),
            P("segment", None),
            P("segment", None, "expert"),
            P("segment", None, "expert"),
            P("segment", "expert", None),
        ),
        out_specs=P("segment", "expert", None),
        check_vma=False,
    )
```

```python
import functools

import jax
import jax.numpy as jnp
from jax import lax
from jax.experimental import pallas as pl
from jax.experimental.pallas import tpu as pltpu
from jax.sharding import PartitionSpec as P

GROUP = 4
LANES = 128
CHUNK = 1024
VMEM_LIMIT = 16 * 1024 * 1024
VMEM = pl.BlockSpec(memory_space=pltpu.VMEM)


def exchange(value, flips, hop):
    segments, owners = lax.axis_size("segment"), lax.axis_size("expert")
    if flips == (0, 0) and hop % segments == 0:
        return value
    pairs = []
    for seg in range(segments):
        for own in range(owners):
            target = (seg + hop) % segments * owners + (own ^ flips[own % 2])
            pairs.append((seg * owners + own, target))
    return lax.ppermute(value, ("segment", "expert"), pairs)


def direct_flips(owners):
    bits = [1 << place for place in range(1, owners.bit_length() - 1)]
    even, odd = bits[1:], bits[:1] + bits[2:]
    flips = []
    for number in range(owners // 4):
        chosen = [place for place in range(len(even)) if number >> place & 1]
        flips.append((sum(even[place] for place in chosen), sum(odd[place] for place in chosen)))
    return flips


BIG = (2, 4)
CORE = (1, 1)


def spans(dim):
    return [slice(start, min(start + CHUNK, dim)) for start in range(0, dim, CHUNK)]


def call(kernel, outs, *args, **more):
    return pl.pallas_call(
        kernel,
        out_shape=[jax.ShapeDtypeStruct(shape, jnp.bfloat16) for shape in outs],
        in_specs=more.pop("in_specs", [VMEM] * len(args)),
        out_specs=[VMEM] * len(outs),
        compiler_params=pltpu.CompilerParams(vmem_limit_bytes=VMEM_LIMIT),
        **more,
    )(*args)


def load_kernel(gate_ref, up_ref, down_ref, gate_out, up_out, down_out, sems):
    copies = [
        pltpu.make_async_copy(source, target, sems.at[place])
        for place, (source, target) in enumerate(((gate_ref, gate_out), (up_ref, up_out), (down_ref, down_out)))
    ]
    for copy in copies:
        copy.start()
    for copy in copies:
        copy.wait()


def load(weights):
    return pl.pallas_call(
        load_kernel,
        out_shape=[pltpu.VMEM(w.shape, w.dtype) for w in weights],
        in_specs=[pl.BlockSpec(memory_space=pltpu.HBM)] * 3,
        out_specs=[VMEM] * 3,
        scratch_shapes=[pltpu.SemaphoreType.DMA((3,))],
        compiler_params=pltpu.CompilerParams(vmem_limit_bytes=VMEM_LIMIT),
        cost_estimate=pl.CostEstimate(
            flops=0, bytes_accessed=sum(2 * w.size for w in weights), transcendentals=0
        ),
    )(*[pltpu.with_memory_space_constraint(w, pltpu.HBM) for w in weights])


def prepare_kernel(experts, states_ref, routing_ref, weight_ref, out_ref):
    rows, dim = states_ref.shape[1:]
    for span in spans(dim):
        out_ref[:, span] = states_ref[0, :, span]
    lane = lax.broadcasted_iota(jnp.int32, (rows, LANES), 1).astype(jnp.float32)
    diagonal = lax.broadcasted_iota(jnp.int32, (rows, rows), 0) == lax.broadcasted_iota(jnp.int32, (rows, rows), 1)

    def upright(line):
        return jnp.sum(jnp.where(diagonal, line.astype(jnp.float32), 0.0), axis=1, keepdims=True)

    total = jnp.zeros((rows, LANES), jnp.float32)
    for step in range(routing_ref.shape[1]):
        for k in range(routing_ref.shape[2]):
            column = upright(routing_ref[0, step, k:k + 1, :]) + step * experts
            total += jnp.where(lane == column, upright(weight_ref[0, step, k:k + 1, :]), 0.0)
    out_ref[:, dim:] = total.astype(jnp.bfloat16)


def join_kernel(*refs):
    *parts, out_ref = refs
    for span in spans(out_ref.shape[1]):
        rows = [part[:, span].astype(jnp.float32) for part in parts]
        out_ref[:, span] = jnp.concatenate(rows, axis=0).astype(jnp.bfloat16)


def add_kernel(*refs):
    *parts, out_ref = refs
    for span in spans(out_ref.shape[1]):
        out_ref[:, span] = sum(part[:, span].astype(jnp.float32) for part in parts).astype(jnp.bfloat16)


def split_kernel(count, *refs):
    parts, outs = refs[:-count], refs[-count:]
    rows = outs[0].shape[0]
    for span in spans(outs[0].shape[1]):
        total = sum(part[:, span].astype(jnp.float32) for part in parts)
        for place, out_ref in enumerate(outs):
            out_ref[:, span] = total[place * rows:(place + 1) * rows].astype(jnp.bfloat16)


def mlp_kernel(step_no, *refs):
    x_refs, refs = refs[:4], refs[4:]
    if step_no > 0:
        tail_ref, refs = refs[0], refs[1:]
    (gain_ref, gate_ref, up_ref, down_ref), outs, refs = refs[:4], refs[4:8], refs[8:]
    rows_ref = refs[-1]
    part = outs[0].shape[0]
    dim, hidden = gate_ref.shape[1:]
    experts = lax.axis_size("expert") // GROUP
    column = step_no * experts + lax.axis_index("expert") // GROUP
    lane = lax.broadcasted_iota(jnp.int32, (part, LANES), 1)
    weights = []
    for place, ref in enumerate(x_refs):
        band = slice(place * part, (place + 1) * part)
        square = jnp.zeros((part, LANES), jnp.float32)
        for start in range(0, dim, LANES):
            piece = ref[:, start:start + LANES].astype(jnp.float32)
            square += piece * piece
        inv = lax.rsqrt(jnp.sum(square, axis=1, keepdims=True) / dim + 1e-06)
        for span in spans(dim):
            scaled = ref[:, span].astype(jnp.float32) * inv * gain_ref[:, span]
            rows_ref[band, span] = scaled.astype(jnp.bfloat16)
        if step_no == 0:
            tail = ref[:, dim:]
            refs[0][band, :] = tail
        else:
            tail = tail_ref[band, :]
        chosen = jnp.where(lane == column, tail.astype(jnp.float32), 0.0)
        weights.append(jnp.sum(chosen, axis=1, keepdims=True))
    gated = jnp.zeros((4 * part, hidden), jnp.float32)
    up_part = jnp.zeros((4 * part, hidden), jnp.float32)
    for span in spans(dim):
        rows = rows_ref[:, span]
        gated += jnp.dot(rows, gate_ref[0, span, :], preferred_element_type=jnp.float32)
        up_part += jnp.dot(rows, up_ref[0, span, :], preferred_element_type=jnp.float32)
    inner = (gated / (1.0 + jnp.exp(-gated)) * up_part).astype(jnp.bfloat16)
    for span in spans(dim):
        terms = jnp.dot(inner, down_ref[0, :, span], preferred_element_type=jnp.float32)
        for place, out_ref in enumerate(outs):
            weight = weights[place]
            mine = terms[place * part:(place + 1) * part]
            out_ref[:, span] = jnp.where(weight > 0.0, weight * mine, 0.0).astype(jnp.bfloat16)


def mlp(step_no, xs, tail, gain, gate, up, down):
    dim, hidden = gate.shape[1:]
    part = xs[0].shape[0]
    gate, up, down = [pltpu.with_memory_space_constraint(w, pltpu.VMEM) for w in (gate, up, down)]
    first = step_no == 0
    args = list(xs) + ([] if first else [tail]) + [gain, gate, up, down]
    result = call(
        functools.partial(mlp_kernel, step_no), [(part, dim)] * 4 + [(4 * part, LANES)] * first, *args,
        scratch_shapes=[pltpu.VMEM((4 * part, dim), jnp.bfloat16)],
        cost_estimate=pl.CostEstimate(
            flops=24 * part * dim * hidden, bytes_accessed=6 * dim * hidden, transcendentals=0
        ),
    )
    return result[:4], result[4] if first else tail


def on_device(states, routing, route_weight, norm_gain, gate_proj, up_proj, down_proj):
    owners = lax.axis_size("expert")
    experts = owners // GROUP
    row_dev, dim = states.shape[1:]
    passes_count = routing.shape[1]
    directs = direct_flips(owners)
    part = len(directs) * row_dev

    current, tail = states[0], None
    gate, up, down = load((gate_proj, up_proj, down_proj))
    (block,) = call(
        functools.partial(prepare_kernel, experts), [(row_dev, dim + LANES)],
        states, jnp.swapaxes(routing, 2, 3), jnp.swapaxes(route_weight, 2, 3),
    )
    for step_no in range(passes_count):
        last = step_no == passes_count - 1
        hop, out_hop = int(step_no > 0), int(last)
        if step_no > 0:
            block = current
        blocks = [exchange(block, flips, hop) for flips in directs]
        if step_no == 0:
            blocks, gate, up, down = lax.optimization_barrier((blocks, gate, up, down))
        (own_0,) = call(join_kernel, [(part, block.shape[1])], *blocks)
        own_1 = exchange(own_0, BIG, 0)
        far_0 = exchange(own_0, CORE, 0)
        far_1 = exchange(own_1, CORE, 0)
        xs = (own_0, own_1, far_0, far_1)
        outs, tail = mlp(step_no, xs, tail, norm_gain, gate, up, down)
        kept_0, kept_1, sent_0, sent_1 = outs

        (half,) = call(add_kernel, [(part, dim)], kept_1, exchange(sent_1, CORE, 0))
        near = exchange(sent_0, CORE, 0)
        pieces = call(
            functools.partial(split_kernel, len(directs)), [(row_dev, dim)] * len(directs),
            kept_0, near, exchange(half, BIG, 0),
        )
        terms = [exchange(piece, flips, out_hop) for piece, flips in zip(pieces, directs)]
        (current,) = call(add_kernel, [(row_dev, dim)], exchange(current, (0, 0), hop + out_hop), *terms)
    return current[None]


def solution(mesh):
    return jax.shard_map(
        on_device,
        mesh=mesh,
        in_specs=(
            P("segment", "expert", None),
            P("segment", None, "expert", None),
            P("segment", None, "expert", None),
            P("segment", None),
            P("segment", None, "expert"),
            P("segment", None, "expert"),
            P("segment", "expert", None),
        ),
        out_specs=P("segment", "expert", None),
        check_vma=False,
    )
```

```python
import functools

import jax
import jax.numpy as jnp
from jax import lax
from jax.experimental import pallas as pl
from jax.experimental.pallas import tpu as pltpu
from jax.sharding import PartitionSpec as P

GROUP = 4
LANES = 128
CHUNK = 1024
VMEM_LIMIT = 16 * 1024 * 1024
VMEM = pl.BlockSpec(memory_space=pltpu.VMEM)


def exchange(value, flips, hop):
    segments, owners = lax.axis_size("segment"), lax.axis_size("expert")
    if flips == (0, 0) and hop % segments == 0:
        return value
    pairs = []
    for seg in range(segments):
        for own in range(owners):
            target = (seg + hop) % segments * owners + (own ^ flips[own % 2])
            pairs.append((seg * owners + own, target))
    return lax.ppermute(value, ("segment", "expert"), pairs)


def upper_flips(owners):
    return [(1 << place,) * 2 for place in range(owners.bit_length() - 2, 2, -1)]


CORE = (1, 1)
NEAR = (4, 2)
BIG = (2, 4)
STAY = (0, 0)


def spans(dim):
    return [slice(start, min(start + CHUNK, dim)) for start in range(0, dim, CHUNK)]


def call(kernel, outs, *args, **more):
    return pl.pallas_call(
        kernel,
        out_shape=[jax.ShapeDtypeStruct(shape, jnp.bfloat16) for shape in outs],
        in_specs=more.pop("in_specs", [VMEM] * len(args)),
        out_specs=[VMEM] * len(outs),
        compiler_params=pltpu.CompilerParams(vmem_limit_bytes=VMEM_LIMIT),
        **more,
    )(*args)


def load_kernel(gate_ref, up_ref, down_ref, gate_out, up_out, down_out, sems):
    copies = [
        pltpu.make_async_copy(source, target, sems.at[place])
        for place, (source, target) in enumerate(((gate_ref, gate_out), (up_ref, up_out), (down_ref, down_out)))
    ]
    for copy in copies:
        copy.start()
    for copy in copies:
        copy.wait()


def load(weights):
    return pl.pallas_call(
        load_kernel,
        out_shape=[pltpu.VMEM(w.shape, w.dtype) for w in weights],
        in_specs=[pl.BlockSpec(memory_space=pltpu.HBM)] * 3,
        out_specs=[VMEM] * 3,
        scratch_shapes=[pltpu.SemaphoreType.DMA((3,))],
        compiler_params=pltpu.CompilerParams(vmem_limit_bytes=VMEM_LIMIT),
        cost_estimate=pl.CostEstimate(
            flops=0, bytes_accessed=sum(2 * w.size for w in weights), transcendentals=0
        ),
    )(*[pltpu.with_memory_space_constraint(w, pltpu.HBM) for w in weights])


def prepare_kernel(experts, states_hbm, routing_hbm, weight_hbm, out_ref, states_ref, routing_ref, weight_ref, sems):
    pairs = ((routing_hbm, routing_ref), (weight_hbm, weight_ref), (states_hbm, states_ref))
    copies = [pltpu.make_async_copy(source, target, sems.at[place]) for place, (source, target) in enumerate(pairs)]
    for copy in copies:
        copy.start()
    for copy in copies:
        copy.wait()
    rows, dim = states_ref.shape[1:]
    for span in spans(dim):
        out_ref[:, span] = states_ref[0, :, span]
    lane = lax.broadcasted_iota(jnp.int32, (rows, LANES), 1).astype(jnp.float32)
    diagonal = lax.broadcasted_iota(jnp.int32, (rows, rows), 0) == lax.broadcasted_iota(jnp.int32, (rows, rows), 1)

    def upright(line):
        return jnp.sum(jnp.where(diagonal, line.astype(jnp.float32), 0.0), axis=1, keepdims=True)

    total = jnp.zeros((rows, LANES), jnp.float32)
    for step in range(routing_ref.shape[1]):
        for k in range(routing_ref.shape[2]):
            column = upright(routing_ref[0, step, k:k + 1, :]) + step * experts
            total += jnp.where(lane == column, upright(weight_ref[0, step, k:k + 1, :]), 0.0)
    out_ref[:, dim:] = total.astype(jnp.bfloat16)


def prepare(experts, states, routing, weight):
    args = [states, jnp.swapaxes(routing, 2, 3), jnp.swapaxes(weight, 2, 3)]
    rows, dim = states.shape[1:]
    (block,) = call(
        functools.partial(prepare_kernel, experts), [(rows, dim + LANES)],
        *[pltpu.with_memory_space_constraint(x, pltpu.HBM) for x in args],
        in_specs=[pl.BlockSpec(memory_space=pltpu.HBM)] * 3,
        scratch_shapes=[pltpu.VMEM(x.shape, x.dtype) for x in args] + [pltpu.SemaphoreType.DMA((3,))],
    )
    return block


def join_kernel(*refs):
    *parts, out_ref = refs
    for span in spans(out_ref.shape[1]):
        rows = [part[:, span].astype(jnp.float32) for part in parts]
        out_ref[:, span] = jnp.concatenate(rows, axis=0).astype(jnp.bfloat16)


def add_kernel(*refs):
    *parts, out_ref = refs
    for span in spans(out_ref.shape[1]):
        out_ref[:, span] = sum(part[:, span].astype(jnp.float32) for part in parts).astype(jnp.bfloat16)


def split_kernel(count, *refs):
    parts, outs = refs[:-count], refs[-count:]
    rows = outs[0].shape[0]
    for span in spans(outs[0].shape[1]):
        total = sum(part[:, span].astype(jnp.float32) for part in parts)
        for place, out_ref in enumerate(outs):
            out_ref[:, span] = total[place * rows:(place + 1) * rows].astype(jnp.bfloat16)


def meet_kernel(rest_ref, near_ref, far_ref, out_ref, own_ref):
    half = own_ref.shape[0]
    for span in spans(out_ref.shape[1]):
        far = far_ref[:, span].astype(jnp.float32)
        total = rest_ref[:, span].astype(jnp.float32) + near_ref[:, span].astype(jnp.float32)
        total = (total + jnp.concatenate([far[half:], far[:half]], axis=0)).astype(jnp.bfloat16)
        out_ref[:, span] = total
        own_ref[:, span] = total[:half]


def mlp_kernel(step_no, *refs):
    x_refs, refs = refs[:8], refs[8:]
    if step_no > 0:
        tail_ref, refs = refs[0], refs[1:]
    (gain_ref, gate_ref, up_ref, down_ref), outs, refs = refs[:4], refs[4:12], refs[12:]
    rows_ref = refs[-1]
    part = outs[0].shape[0]
    dim, hidden = gate_ref.shape[1:]
    experts = lax.axis_size("expert") // GROUP
    column = step_no * experts + lax.axis_index("expert") // GROUP
    lane = lax.broadcasted_iota(jnp.int32, (part, LANES), 1)
    weights = []
    for place, ref in enumerate(x_refs):
        band = slice(place * part, (place + 1) * part)
        square = jnp.zeros((part, LANES), jnp.float32)
        for start in range(0, dim, LANES):
            piece = ref[:, start:start + LANES].astype(jnp.float32)
            square += piece * piece
        inv = lax.rsqrt(jnp.sum(square, axis=1, keepdims=True) / dim + 1e-06)
        for span in spans(dim):
            scaled = ref[:, span].astype(jnp.float32) * inv * gain_ref[:, span]
            rows_ref[band, span] = scaled.astype(jnp.bfloat16)
        if step_no == 0:
            tail = ref[:, dim:]
            refs[0][band, :] = tail
        else:
            tail = tail_ref[band, :]
        chosen = jnp.where(lane == column, tail.astype(jnp.float32), 0.0)
        weights.append(jnp.sum(chosen, axis=1, keepdims=True))
    gated = jnp.zeros((8 * part, hidden), jnp.float32)
    up_part = jnp.zeros((8 * part, hidden), jnp.float32)
    for span in spans(dim):
        rows = rows_ref[:, span]
        gated += jnp.dot(rows, gate_ref[0, span, :], preferred_element_type=jnp.float32)
        up_part += jnp.dot(rows, up_ref[0, span, :], preferred_element_type=jnp.float32)
    inner = (gated / (1.0 + jnp.exp(-gated)) * up_part).astype(jnp.bfloat16)
    for span in spans(dim):
        terms = jnp.dot(inner, down_ref[0, :, span], preferred_element_type=jnp.float32)
        for place, out_ref in enumerate(outs):
            weight = weights[place]
            mine = terms[place * part:(place + 1) * part]
            out_ref[:, span] = jnp.where(weight > 0.0, weight * mine, 0.0).astype(jnp.bfloat16)


def mlp(step_no, xs, tail, gain, gate, up, down):
    dim, hidden = gate.shape[1:]
    part = xs[0].shape[0]
    gate, up, down = [pltpu.with_memory_space_constraint(w, pltpu.VMEM) for w in (gate, up, down)]
    first = step_no == 0
    args = list(xs) + ([] if first else [tail]) + [gain, gate, up, down]
    result = call(
        functools.partial(mlp_kernel, step_no), [(part, dim)] * 8 + [(8 * part, LANES)] * first, *args,
        scratch_shapes=[pltpu.VMEM((8 * part, dim), jnp.bfloat16)],
        cost_estimate=pl.CostEstimate(
            flops=48 * part * dim * hidden, bytes_accessed=6 * dim * hidden, transcendentals=0
        ),
    )
    return result[:8], result[8] if first else tail


def add(*parts):
    rows = parts[0].shape[0]
    dim = parts[-1].shape[1]
    return call(add_kernel, [(rows, dim)], *parts)[0]


def split(*parts):
    rows, dim = parts[0].shape
    return call(functools.partial(split_kernel, 2), [(rows // 2, dim)] * 2, *parts)


def join(*parts):
    return call(join_kernel, [(sum(part.shape[0] for part in parts), parts[0].shape[1])], *parts)[0]


def on_device(states, routing, route_weight, norm_gain, gate_proj, up_proj, down_proj):
    owners = lax.axis_size("expert")
    row_dev, dim = states.shape[1:]
    passes_count = routing.shape[1]
    top, *middle = upper_flips(owners)

    weights = load((gate_proj, up_proj, down_proj))
    block = prepare(owners // GROUP, states, routing, route_weight)
    other = exchange(block, top, 0)
    block, other, *weights = lax.optimization_barrier((block, other, *weights))
    pair, own, tail = join(block, other), states[0], None
    for step_no in range(passes_count):
        rows_a = pair
        for flips in middle:
            rows_a = join(rows_a, exchange(rows_a, flips, 0))
        rows_b = exchange(rows_a, NEAR, 0)
        rows_c = exchange(rows_a, BIG, 0)
        rows_d = exchange(rows_b, BIG, 0)
        mine = [rows_a, rows_b, rows_c, rows_d]
        outs, tail = mlp(step_no, mine + [exchange(rows, CORE, 0) for rows in mine], tail, norm_gain, *weights)

        kept_a, kept_b, kept_c, kept_d = outs[:4]
        far_a, far_b, far_c, far_d = [exchange(rows, CORE, 0) for rows in outs[4:]]
        big_b = exchange(add(kept_d, far_d), BIG, 0)
        big_a = exchange(add(kept_c, far_c), BIG, 0)
        near_a = exchange(add(kept_b, far_b, big_b), NEAR, 0)
        parts = [kept_a, far_a, big_a, near_a]
        for flips in middle[::-1]:
            low, high = split(*parts)
            parts = [low, exchange(high, flips, 0)]
        if step_no < passes_count - 1:
            total = add(*parts)
            rest = exchange(pair, STAY, 1)
            pair, own = call(
                meet_kernel, [(2 * row_dev, dim), (row_dev, dim)], rest, exchange(total, STAY, 1), exchange(total, top, 1)
            )
        else:
            low, high = split(*parts)
            rest = exchange(own, STAY, 1)
            own = add(rest, exchange(low, STAY, 1), exchange(high, top, 1))
    return own[None]


def solution(mesh):
    return jax.shard_map(
        on_device,
        mesh=mesh,
        in_specs=(
            P("segment", "expert", None),
            P("segment", None, "expert", None),
            P("segment", None, "expert", None),
            P("segment", None),
            P("segment", None, "expert"),
            P("segment", None, "expert"),
            P("segment", "expert", None),
        ),
        out_specs=P("segment", "expert", None),
        check_vma=False,
    )
```

```python
import functools

import jax
import jax.numpy as jnp
from jax import lax
from jax.experimental import pallas as pl
from jax.experimental.pallas import tpu as pltpu
from jax.sharding import PartitionSpec as P

GROUP = 4
LANES = 128
CHUNK = 1024
VMEM_LIMIT = 16 * 1024 * 1024
VMEM = pl.BlockSpec(memory_space=pltpu.VMEM)


def exchange(value, flips, hop):
    segments, owners = lax.axis_size("segment"), lax.axis_size("expert")
    if flips == (0, 0) and hop % segments == 0:
        return value
    pairs = []
    for seg in range(segments):
        for own in range(owners):
            target = (seg + hop) % segments * owners + (own ^ flips[own % 2])
            pairs.append((seg * owners + own, target))
    return lax.ppermute(value, ("segment", "expert"), pairs)


def upper_flips(owners):
    return [(1 << place,) * 2 for place in range(owners.bit_length() - 2, 2, -1)]


CORE = (1, 1)
SQUARE = ((4, 2), (2, 4), (6, 6))
STAY = (0, 0)


def spans(dim):
    return [slice(start, min(start + CHUNK, dim)) for start in range(0, dim, CHUNK)]


def call(kernel, outs, *args, **more):
    return pl.pallas_call(
        kernel,
        out_shape=[jax.ShapeDtypeStruct(shape, jnp.bfloat16) for shape in outs],
        in_specs=more.pop("in_specs", [VMEM] * len(args)),
        out_specs=[VMEM] * len(outs),
        compiler_params=pltpu.CompilerParams(vmem_limit_bytes=VMEM_LIMIT),
        **more,
    )(*args)


def load_kernel(gate_ref, up_ref, down_ref, gate_out, up_out, down_out, sems):
    copies = [
        pltpu.make_async_copy(source, target, sems.at[place])
        for place, (source, target) in enumerate(((gate_ref, gate_out), (up_ref, up_out), (down_ref, down_out)))
    ]
    for copy in copies:
        copy.start()
    for copy in copies:
        copy.wait()


def load(weights):
    return pl.pallas_call(
        load_kernel,
        out_shape=[pltpu.VMEM(w.shape, w.dtype) for w in weights],
        in_specs=[pl.BlockSpec(memory_space=pltpu.HBM)] * 3,
        out_specs=[VMEM] * 3,
        scratch_shapes=[pltpu.SemaphoreType.DMA((3,))],
        compiler_params=pltpu.CompilerParams(vmem_limit_bytes=VMEM_LIMIT),
        cost_estimate=pl.CostEstimate(
            flops=0, bytes_accessed=sum(2 * w.size for w in weights), transcendentals=0
        ),
    )(*[pltpu.with_memory_space_constraint(w, pltpu.HBM) for w in weights])


def route_kernel(experts, routing_hbm, weight_hbm, out_ref, routing_ref, weight_ref, sems):
    pairs = ((routing_hbm, routing_ref), (weight_hbm, weight_ref))
    copies = [pltpu.make_async_copy(source, target, sems.at[place]) for place, (source, target) in enumerate(pairs)]
    for copy in copies:
        copy.start()
    for copy in copies:
        copy.wait()
    rows = out_ref.shape[0]
    lane = lax.broadcasted_iota(jnp.int32, (rows, LANES), 1).astype(jnp.float32)
    diagonal = lax.broadcasted_iota(jnp.int32, (rows, rows), 0) == lax.broadcasted_iota(jnp.int32, (rows, rows), 1)

    def upright(line):
        return jnp.sum(jnp.where(diagonal, line.astype(jnp.float32), 0.0), axis=1, keepdims=True)

    total = jnp.zeros((rows, LANES), jnp.float32)
    for step in range(routing_ref.shape[1]):
        for k in range(routing_ref.shape[2]):
            column = upright(routing_ref[0, step, k:k + 1, :]) + step * experts
            total += jnp.where(lane == column, upright(weight_ref[0, step, k:k + 1, :]), 0.0)
    out_ref[...] = total.astype(jnp.bfloat16)


def route(experts, routing, weight):
    args = [jnp.swapaxes(routing, 2, 3), jnp.swapaxes(weight, 2, 3)]
    return call(
        functools.partial(route_kernel, experts), [(routing.shape[2], LANES)],
        *[pltpu.with_memory_space_constraint(x, pltpu.HBM) for x in args],
        in_specs=[pl.BlockSpec(memory_space=pltpu.HBM)] * 2,
        scratch_shapes=[pltpu.VMEM(x.shape, x.dtype) for x in args] + [pltpu.SemaphoreType.DMA((2,))],
    )[0]


def first_kernel(own_ref, far_ref, own_tail_ref, far_tail_ref, out_ref):
    dim = own_ref.shape[1]
    for span in spans(dim):
        rows = [ref[:, span].astype(jnp.float32) for ref in (own_ref, far_ref)]
        out_ref[:, span] = jnp.concatenate(rows, axis=0).astype(jnp.bfloat16)
    tails = [ref[...].astype(jnp.float32) for ref in (own_tail_ref, far_tail_ref)]
    out_ref[:, dim:] = jnp.concatenate(tails, axis=0).astype(jnp.bfloat16)


def join_kernel(*refs):
    *parts, out_ref = refs
    for span in spans(out_ref.shape[1]):
        rows = [part[:, span].astype(jnp.float32) for part in parts]
        out_ref[:, span] = jnp.concatenate(rows, axis=0).astype(jnp.bfloat16)


def add_kernel(*refs):
    *parts, out_ref = refs
    for span in spans(out_ref.shape[1]):
        out_ref[:, span] = sum(part[:, span].astype(jnp.float32) for part in parts).astype(jnp.bfloat16)


def split_kernel(count, *refs):
    parts, outs = refs[:-count], refs[-count:]
    rows = outs[0].shape[0]
    for span in spans(outs[0].shape[1]):
        total = sum(part[:, span].astype(jnp.float32) for part in parts)
        for place, out_ref in enumerate(outs):
            out_ref[:, span] = total[place * rows:(place + 1) * rows].astype(jnp.bfloat16)


def meet_kernel(rest_ref, near_ref, far_ref, out_ref, own_ref):
    half = own_ref.shape[0]
    for span in spans(out_ref.shape[1]):
        far = far_ref[:, span].astype(jnp.float32)
        total = rest_ref[:, span].astype(jnp.float32) + near_ref[:, span].astype(jnp.float32)
        total = (total + jnp.concatenate([far[half:], far[:half]], axis=0)).astype(jnp.bfloat16)
        out_ref[:, span] = total
        own_ref[:, span] = total[:half]


def mlp_kernel(step_no, *refs):
    x_refs, refs = refs[:8], refs[8:]
    if step_no > 0:
        tail_ref, refs = refs[0], refs[1:]
    (gain_ref, gate_ref, up_ref, down_ref), outs, refs = refs[:4], refs[4:12], refs[12:]
    rows_ref = refs[-1]
    part = outs[0].shape[0]
    dim, hidden = gate_ref.shape[1:]
    experts = lax.axis_size("expert") // GROUP
    column = step_no * experts + lax.axis_index("expert") // GROUP
    lane = lax.broadcasted_iota(jnp.int32, (part, LANES), 1)
    weights = []
    for place, ref in enumerate(x_refs):
        band = slice(place * part, (place + 1) * part)
        square = jnp.zeros((part, LANES), jnp.float32)
        for start in range(0, dim, LANES):
            piece = ref[:, start:start + LANES].astype(jnp.float32)
            square += piece * piece
        inv = lax.rsqrt(jnp.sum(square, axis=1, keepdims=True) / dim + 1e-06)
        for span in spans(dim):
            scaled = ref[:, span].astype(jnp.float32) * inv * gain_ref[:, span]
            rows_ref[band, span] = scaled.astype(jnp.bfloat16)
        if step_no == 0:
            tail = ref[:, dim:]
            refs[0][band, :] = tail
        else:
            tail = tail_ref[band, :]
        chosen = jnp.where(lane == column, tail.astype(jnp.float32), 0.0)
        weights.append(jnp.sum(chosen, axis=1, keepdims=True))
    gated = jnp.zeros((8 * part, hidden), jnp.float32)
    up_part = jnp.zeros((8 * part, hidden), jnp.float32)
    for span in spans(dim):
        rows = rows_ref[:, span]
        gated += jnp.dot(rows, gate_ref[0, span, :], preferred_element_type=jnp.float32)
        up_part += jnp.dot(rows, up_ref[0, span, :], preferred_element_type=jnp.float32)
    inner = (gated / (1.0 + jnp.exp(-gated)) * up_part).astype(jnp.bfloat16)
    for span in spans(dim):
        terms = jnp.dot(inner, down_ref[0, :, span], preferred_element_type=jnp.float32)
        for place, out_ref in enumerate(outs):
            weight = weights[place]
            mine = terms[place * part:(place + 1) * part]
            out_ref[:, span] = jnp.where(weight > 0.0, weight * mine, 0.0).astype(jnp.bfloat16)


def mlp(step_no, xs, tail, gain, gate, up, down):
    dim, hidden = gate.shape[1:]
    part = xs[0].shape[0]
    gate, up, down = [pltpu.with_memory_space_constraint(w, pltpu.VMEM) for w in (gate, up, down)]
    first = step_no == 0
    args = list(xs) + ([] if first else [tail]) + [gain, gate, up, down]
    result = call(
        functools.partial(mlp_kernel, step_no), [(part, dim)] * 8 + [(8 * part, LANES)] * first, *args,
        scratch_shapes=[pltpu.VMEM((8 * part, dim), jnp.bfloat16)],
        cost_estimate=pl.CostEstimate(
            flops=48 * part * dim * hidden, bytes_accessed=6 * dim * hidden, transcendentals=0
        ),
    )
    return result[:8], result[8] if first else tail


def add(*parts):
    rows = parts[0].shape[0]
    dim = parts[-1].shape[1]
    return call(add_kernel, [(rows, dim)], *parts)[0]


def split(*parts):
    rows, dim = parts[0].shape
    return call(functools.partial(split_kernel, 2), [(rows // 2, dim)] * 2, *parts)


def join(*parts):
    return call(join_kernel, [(sum(part.shape[0] for part in parts), parts[0].shape[1])], *parts)[0]


def on_device(states, routing, route_weight, norm_gain, gate_proj, up_proj, down_proj):
    owners = lax.axis_size("expert")
    row_dev, dim = states.shape[1:]
    passes_count = routing.shape[1]
    top, *middle = upper_flips(owners)

    weights = load((gate_proj, up_proj, down_proj))
    own, tail = states[0], None
    lanes = route(owners // GROUP, routing, route_weight)
    other, other_lanes = exchange(own, top, 0), exchange(lanes, top, 0)
    other, other_lanes, *weights = lax.optimization_barrier((other, other_lanes, *weights))
    (pair,) = call(first_kernel, [(2 * row_dev, dim + LANES)], own, other, lanes, other_lanes)
    for step_no in range(passes_count):
        rows_a = pair
        for flips in middle:
            rows_a = join(rows_a, exchange(rows_a, flips, 0))
        mine = [rows_a] + [exchange(rows_a, flips, 0) for flips in SQUARE]
        outs, tail = mlp(step_no, mine + [exchange(rows, CORE, 0) for rows in mine], tail, norm_gain, *weights)

        kept, sent = outs[:4], [exchange(rows, CORE, 0) for rows in outs[4:]]
        parts = [kept[0], sent[0]]
        for place in (3, 2, 1):
            parts.append(exchange(add(kept[place], sent[place]), SQUARE[place - 1], 0))
        for flips in middle[::-1]:
            low, high = split(*parts)
            parts = [low, exchange(high, flips, 0)]
        if step_no < passes_count - 1:
            total = add(*parts)
            rest = exchange(pair, STAY, 1)
            pair, own = call(
                meet_kernel, [(2 * row_dev, dim), (row_dev, dim)], rest, exchange(total, STAY, 1), exchange(total, top, 1)
            )
        else:
            low, high = split(*parts)
            rest = exchange(own, STAY, 1)
            own = add(rest, exchange(low, STAY, 1), exchange(high, top, 1))
    return own[None]


def solution(mesh):
    return jax.shard_map(
        on_device,
        mesh=mesh,
        in_specs=(
            P("segment", "expert", None),
            P("segment", None, "expert", None),
            P("segment", None, "expert", None),
            P("segment", None),
            P("segment", None, "expert"),
            P("segment", None, "expert"),
            P("segment", "expert", None),
        ),
        out_specs=P("segment", "expert", None),
        check_vma=False,
    )
```

```python
import functools

import jax
import jax.numpy as jnp
from jax import lax
from jax.experimental import pallas as pl
from jax.experimental.pallas import tpu as pltpu
from jax.sharding import PartitionSpec as P

GROUP = 4
LANES = 128
CHUNK = 1024
VMEM_LIMIT = 16 * 1024 * 1024
VMEM = pl.BlockSpec(memory_space=pltpu.VMEM)


def exchange(value, flips, hop):
    segments, owners = lax.axis_size("segment"), lax.axis_size("expert")
    if flips == (0, 0) and hop % segments == 0:
        return value
    pairs = []
    for seg in range(segments):
        for own in range(owners):
            target = (seg + hop) % segments * owners + (own ^ flips[own % 2])
            pairs.append((seg * owners + own, target))
    return lax.ppermute(value, ("segment", "expert"), pairs)


def upper_flips(owners):
    return [(1 << place,) * 2 for place in range(owners.bit_length() - 2, 2, -1)]


CORE = (1, 1)
SQUARE = ((6, 6), (2, 4), (4, 2))
STAY = (0, 0)


def spans(dim):
    return [slice(start, min(start + CHUNK, dim)) for start in range(0, dim, CHUNK)]


def call(kernel, outs, *args, **more):
    return pl.pallas_call(
        kernel,
        out_shape=[jax.ShapeDtypeStruct(shape, jnp.bfloat16) for shape in outs],
        in_specs=more.pop("in_specs", [VMEM] * len(args)),
        out_specs=[VMEM] * len(outs),
        compiler_params=pltpu.CompilerParams(vmem_limit_bytes=VMEM_LIMIT),
        **more,
    )(*args)


def load_kernel(gate_ref, up_ref, down_ref, gate_out, up_out, down_out, sems):
    copies = [
        pltpu.make_async_copy(source, target, sems.at[place])
        for place, (source, target) in enumerate(((gate_ref, gate_out), (up_ref, up_out), (down_ref, down_out)))
    ]
    for copy in copies:
        copy.start()
    for copy in copies:
        copy.wait()


def load(weights):
    return pl.pallas_call(
        load_kernel,
        out_shape=[pltpu.VMEM(w.shape, w.dtype) for w in weights],
        in_specs=[pl.BlockSpec(memory_space=pltpu.HBM)] * 3,
        out_specs=[VMEM] * 3,
        scratch_shapes=[pltpu.SemaphoreType.DMA((3,))],
        compiler_params=pltpu.CompilerParams(vmem_limit_bytes=VMEM_LIMIT),
        cost_estimate=pl.CostEstimate(
            flops=0, bytes_accessed=sum(2 * w.size for w in weights), transcendentals=0
        ),
    )(*[pltpu.with_memory_space_constraint(w, pltpu.HBM) for w in weights])


def route_kernel(experts, routing_hbm, weight_hbm, out_ref, routing_ref, weight_ref, sems):
    pairs = ((routing_hbm, routing_ref), (weight_hbm, weight_ref))
    copies = [pltpu.make_async_copy(source, target, sems.at[place]) for place, (source, target) in enumerate(pairs)]
    for copy in copies:
        copy.start()
    for copy in copies:
        copy.wait()
    rows = out_ref.shape[0]
    lane = lax.broadcasted_iota(jnp.int32, (rows, LANES), 1).astype(jnp.float32)
    diagonal = lax.broadcasted_iota(jnp.int32, (rows, rows), 0) == lax.broadcasted_iota(jnp.int32, (rows, rows), 1)

    def upright(line):
        return jnp.sum(jnp.where(diagonal, line.astype(jnp.float32), 0.0), axis=1, keepdims=True)

    total = jnp.zeros((rows, LANES), jnp.float32)
    for step in range(routing_ref.shape[1]):
        for k in range(routing_ref.shape[2]):
            column = upright(routing_ref[0, step, k:k + 1, :]) + step * experts
            total += jnp.where(lane == column, upright(weight_ref[0, step, k:k + 1, :]), 0.0)
    out_ref[...] = total.astype(jnp.bfloat16)


def route(experts, routing, weight):
    args = [jnp.swapaxes(routing, 2, 3), jnp.swapaxes(weight, 2, 3)]
    return call(
        functools.partial(route_kernel, experts), [(routing.shape[2], LANES)],
        *[pltpu.with_memory_space_constraint(x, pltpu.HBM) for x in args],
        in_specs=[pl.BlockSpec(memory_space=pltpu.HBM)] * 2,
        scratch_shapes=[pltpu.VMEM(x.shape, x.dtype) for x in args] + [pltpu.SemaphoreType.DMA((2,))],
    )[0]


def first_kernel(own_ref, far_ref, own_tail_ref, far_tail_ref, out_ref):
    dim = own_ref.shape[1]
    for span in spans(dim):
        rows = [ref[:, span].astype(jnp.float32) for ref in (own_ref, far_ref)]
        out_ref[:, span] = jnp.concatenate(rows, axis=0).astype(jnp.bfloat16)
    tails = [ref[...].astype(jnp.float32) for ref in (own_tail_ref, far_tail_ref)]
    out_ref[:, dim:] = jnp.concatenate(tails, axis=0).astype(jnp.bfloat16)


def join_kernel(*refs):
    *parts, out_ref = refs
    for span in spans(out_ref.shape[1]):
        rows = [part[:, span].astype(jnp.float32) for part in parts]
        out_ref[:, span] = jnp.concatenate(rows, axis=0).astype(jnp.bfloat16)


def add_kernel(*refs):
    *parts, out_ref = refs
    for span in spans(out_ref.shape[1]):
        out_ref[:, span] = sum(part[:, span].astype(jnp.float32) for part in parts).astype(jnp.bfloat16)


def split_kernel(count, *refs):
    parts, outs = refs[:-count], refs[-count:]
    rows = outs[0].shape[0]
    for span in spans(outs[0].shape[1]):
        total = sum(part[:, span].astype(jnp.float32) for part in parts)
        for place, out_ref in enumerate(outs):
            out_ref[:, span] = total[place * rows:(place + 1) * rows].astype(jnp.bfloat16)


def meet_kernel(rest_ref, far_ref, near_ref, out_ref, own_ref):
    half = own_ref.shape[0]
    for span in spans(out_ref.shape[1]):
        far = far_ref[:, span].astype(jnp.float32)
        total = rest_ref[:, span].astype(jnp.float32) + near_ref[:, span].astype(jnp.float32)
        total = (total + jnp.concatenate([far[half:], far[:half]], axis=0)).astype(jnp.bfloat16)
        out_ref[:, span] = total
        own_ref[:, span] = total[:half]


def mlp_kernel(step_no, count, *refs):
    x_refs, refs = refs[:count], refs[count:]
    if step_no > 0:
        tail_ref, refs = refs[0], refs[1:]
    (gain_ref, gate_ref, up_ref, down_ref), outs, refs = refs[:4], refs[4:4 + count], refs[4 + count:]
    rows_ref = refs[-1]
    part = outs[0].shape[0]
    dim, hidden = gate_ref.shape[1:]
    experts = lax.axis_size("expert") // GROUP
    column = step_no * experts + lax.axis_index("expert") // GROUP
    lane = lax.broadcasted_iota(jnp.int32, (part, LANES), 1)
    weights = []
    for place, ref in enumerate(x_refs):
        band = slice(place * part, (place + 1) * part)
        square = jnp.zeros((part, LANES), jnp.float32)
        for start in range(0, dim, LANES):
            piece = ref[:, start:start + LANES].astype(jnp.float32)
            square += piece * piece
        inv = lax.rsqrt(jnp.sum(square, axis=1, keepdims=True) / dim + 1e-06)
        for span in spans(dim):
            scaled = ref[:, span].astype(jnp.float32) * inv * gain_ref[:, span]
            rows_ref[band, span] = scaled.astype(jnp.bfloat16)
        if step_no == 0:
            tail = ref[:, dim:]
            refs[0][band, :] = tail
        else:
            tail = tail_ref[band, :]
        chosen = jnp.where(lane == column, tail.astype(jnp.float32), 0.0)
        weights.append(jnp.sum(chosen, axis=1, keepdims=True))
    gated = jnp.zeros((count * part, hidden), jnp.float32)
    up_part = jnp.zeros((count * part, hidden), jnp.float32)
    for span in spans(dim):
        rows = rows_ref[:, span]
        gated += jnp.dot(rows, gate_ref[0, span, :], preferred_element_type=jnp.float32)
        up_part += jnp.dot(rows, up_ref[0, span, :], preferred_element_type=jnp.float32)
    inner = (gated / (1.0 + jnp.exp(-gated)) * up_part).astype(jnp.bfloat16)
    for span in spans(dim):
        terms = jnp.dot(inner, down_ref[0, :, span], preferred_element_type=jnp.float32)
        for place, out_ref in enumerate(outs):
            weight = weights[place]
            mine = terms[place * part:(place + 1) * part]
            out_ref[:, span] = jnp.where(weight > 0.0, weight * mine, 0.0).astype(jnp.bfloat16)


def mlp(step_no, xs, tail, gain, gate, up, down):
    dim, hidden = gate.shape[1:]
    part, count = xs[0].shape[0], len(xs)
    gate, up, down = [pltpu.with_memory_space_constraint(w, pltpu.VMEM) for w in (gate, up, down)]
    first = step_no == 0
    args = list(xs) + ([] if first else [tail]) + [gain, gate, up, down]
    result = call(
        functools.partial(mlp_kernel, step_no, count), [(part, dim)] * count + [(count * part, LANES)] * first, *args,
        scratch_shapes=[pltpu.VMEM((count * part, dim), jnp.bfloat16)],
        cost_estimate=pl.CostEstimate(
            flops=6 * count * part * dim * hidden, bytes_accessed=6 * dim * hidden, transcendentals=0
        ),
    )
    return result[:count], result[count] if first else tail


def add(*parts):
    rows = parts[0].shape[0]
    dim = parts[-1].shape[1]
    return call(add_kernel, [(rows, dim)], *parts)[0]


def split(*parts):
    rows, dim = parts[0].shape
    return call(functools.partial(split_kernel, 2), [(rows // 2, dim)] * 2, *parts)


def join(*parts):
    return call(join_kernel, [(sum(part.shape[0] for part in parts), parts[0].shape[1])], *parts)[0]


def on_device(states, routing, route_weight, norm_gain, gate_proj, up_proj, down_proj):
    owners = lax.axis_size("expert")
    row_dev, dim = states.shape[1:]
    passes_count = routing.shape[1]
    top, *middle = upper_flips(owners)

    weights = load((gate_proj, up_proj, down_proj))
    own, tail, tail_a = states[0], None, None
    lanes = route(owners // GROUP, routing, route_weight)
    other, other_lanes = exchange(own, top, 0), exchange(lanes, top, 0)
    other, other_lanes, *weights = lax.optimization_barrier((other, other_lanes, *weights))
    (pair,) = call(first_kernel, [(2 * row_dev, dim + LANES)], own, other, lanes, other_lanes)
    for step_no in range(passes_count):
        rows_a = pair
        for flips in middle:
            rows_a = join(rows_a, exchange(rows_a, flips, 0))
        (kept_a, sent_a), tail_a = mlp(
            step_no, [rows_a, exchange(rows_a, CORE, 0)], tail_a, norm_gain, *weights
        )
        mine = [exchange(rows_a, flips, 0) for flips in SQUARE]
        mine[2], kept_a, sent_a = lax.optimization_barrier((mine[2], kept_a, sent_a))
        outs, tail = mlp(step_no, mine + [exchange(rows, CORE, 0) for rows in mine], tail, norm_gain, *weights)

        parts = [kept_a, exchange(sent_a, CORE, 0)]
        for place in range(len(SQUARE))[::-1]:
            chip = add(outs[place], exchange(outs[place + len(SQUARE)], CORE, 0))
            parts.append(exchange(chip, SQUARE[place], 0))
        for flips in middle[::-1]:
            low, high = split(*parts)
            parts = [low, exchange(high, flips, 0)]
        if step_no < passes_count - 1:
            total = add(*parts)
            rest = exchange(pair, STAY, 1)
            pair, own = call(
                meet_kernel, [(2 * row_dev, dim), (row_dev, dim)], rest, exchange(total, top, 1), exchange(total, STAY, 1)
            )
        else:
            low, high = split(*parts)
            rest = exchange(own, STAY, 1)
            far = exchange(high, top, 1)
            own = add(rest, far, exchange(low, STAY, 1))
    return own[None]


def solution(mesh):
    return jax.shard_map(
        on_device,
        mesh=mesh,
        in_specs=(
            P("segment", "expert", None),
            P("segment", None, "expert", None),
            P("segment", None, "expert", None),
            P("segment", None),
            P("segment", None, "expert"),
            P("segment", None, "expert"),
            P("segment", "expert", None),
        ),
        out_specs=P("segment", "expert", None),
        check_vma=False,
    )
```

```python
import functools

import jax
import jax.numpy as jnp
from jax import lax
from jax.experimental import pallas as pl
from jax.experimental.pallas import tpu as pltpu
from jax.sharding import PartitionSpec as P

GROUP = 4
LANES = 128
CHUNK = 896
HALVES = 2
VMEM_LIMIT = 16 * 1024 * 1024
VMEM = pl.BlockSpec(memory_space=pltpu.VMEM)


def exchange(value, flips, hop):
    segments, owners = lax.axis_size("segment"), lax.axis_size("expert")
    if flips == (0, 0) and hop % segments == 0:
        return value
    pairs = []
    for seg in range(segments):
        for own in range(owners):
            target = (seg + hop) % segments * owners + (own ^ flips[own % 2])
            pairs.append((seg * owners + own, target))
    return lax.ppermute(value, ("segment", "expert"), pairs)


def upper_flips(owners):
    return [(1 << place,) * 2 for place in range(owners.bit_length() - 2, 2, -1)]


CORE = (1, 1)
SQUARE = ((4, 2), (2, 4), (6, 6))
STAY = (0, 0)


def spans(dim):
    return [slice(start, min(start + CHUNK, dim)) for start in range(0, dim, CHUNK)]


def call(kernel, outs, *args, **more):
    return pl.pallas_call(
        kernel,
        out_shape=[jax.ShapeDtypeStruct(shape, jnp.bfloat16) for shape in outs],
        in_specs=more.pop("in_specs", [VMEM] * len(args)),
        out_specs=[VMEM] * len(outs),
        compiler_params=pltpu.CompilerParams(vmem_limit_bytes=VMEM_LIMIT),
        **more,
    )(*args)


def load_kernel(gate_ref, up_ref, down_ref, gate_out, up_out, down_out, sems):
    copies = [
        pltpu.make_async_copy(source, target, sems.at[place])
        for place, (source, target) in enumerate(((gate_ref, gate_out), (up_ref, up_out), (down_ref, down_out)))
    ]
    for copy in copies:
        copy.start()
    for copy in copies:
        copy.wait()


def load(weights):
    return pl.pallas_call(
        load_kernel,
        out_shape=[pltpu.VMEM(w.shape, w.dtype) for w in weights],
        in_specs=[pl.BlockSpec(memory_space=pltpu.HBM)] * 3,
        out_specs=[VMEM] * 3,
        scratch_shapes=[pltpu.SemaphoreType.DMA((3,))],
        compiler_params=pltpu.CompilerParams(vmem_limit_bytes=VMEM_LIMIT),
        cost_estimate=pl.CostEstimate(
            flops=0, bytes_accessed=sum(2 * w.size for w in weights), transcendentals=0
        ),
    )(*[pltpu.with_memory_space_constraint(w, pltpu.HBM) for w in weights])


def route_kernel(experts, routing_hbm, weight_hbm, out_ref, routing_ref, weight_ref, sems):
    pairs = ((routing_hbm, routing_ref), (weight_hbm, weight_ref))
    copies = [pltpu.make_async_copy(source, target, sems.at[place]) for place, (source, target) in enumerate(pairs)]
    for copy in copies:
        copy.start()
    for copy in copies:
        copy.wait()
    rows = out_ref.shape[0]
    lane = lax.broadcasted_iota(jnp.int32, (rows, LANES), 1).astype(jnp.float32)
    diagonal = lax.broadcasted_iota(jnp.int32, (rows, rows), 0) == lax.broadcasted_iota(jnp.int32, (rows, rows), 1)

    def upright(line):
        return jnp.sum(jnp.where(diagonal, line.astype(jnp.float32), 0.0), axis=1, keepdims=True)

    total = jnp.zeros((rows, LANES), jnp.float32)
    for step in range(routing_ref.shape[1]):
        for k in range(routing_ref.shape[2]):
            column = upright(routing_ref[0, step, k:k + 1, :]) + step * experts
            total += jnp.where(lane == column, upright(weight_ref[0, step, k:k + 1, :]), 0.0)
    out_ref[...] = total.astype(jnp.bfloat16)


def route(experts, routing, weight):
    args = [jnp.swapaxes(routing, 2, 3), jnp.swapaxes(weight, 2, 3)]
    return call(
        functools.partial(route_kernel, experts), [(routing.shape[2], LANES)],
        *[pltpu.with_memory_space_constraint(x, pltpu.HBM) for x in args],
        in_specs=[pl.BlockSpec(memory_space=pltpu.HBM)] * 2,
        scratch_shapes=[pltpu.VMEM(x.shape, x.dtype) for x in args] + [pltpu.SemaphoreType.DMA((2,))],
    )[0]


def first_kernel(own_ref, far_ref, own_tail_ref, far_tail_ref, out_ref):
    dim = own_ref.shape[1]
    for span in spans(dim):
        rows = [ref[:, span].astype(jnp.float32) for ref in (own_ref, far_ref)]
        out_ref[:, span] = jnp.concatenate(rows, axis=0).astype(jnp.bfloat16)
    tails = [ref[...].astype(jnp.float32) for ref in (own_tail_ref, far_tail_ref)]
    out_ref[:, dim:] = jnp.concatenate(tails, axis=0).astype(jnp.bfloat16)


def join_kernel(*refs):
    *parts, out_ref = refs
    for span in spans(out_ref.shape[1]):
        rows = [part[:, span].astype(jnp.float32) for part in parts]
        out_ref[:, span] = jnp.concatenate(rows, axis=0).astype(jnp.bfloat16)


def add_kernel(*refs):
    *parts, out_ref = refs
    for span in spans(out_ref.shape[1]):
        out_ref[:, span] = sum(part[:, span].astype(jnp.float32) for part in parts).astype(jnp.bfloat16)


def split_kernel(count, *refs):
    parts, outs = refs[:-count], refs[-count:]
    rows = outs[0].shape[0]
    for span in spans(outs[0].shape[1]):
        total = sum(part[:, span].astype(jnp.float32) for part in parts)
        for place, out_ref in enumerate(outs):
            out_ref[:, span] = total[place * rows:(place + 1) * rows].astype(jnp.bfloat16)


def meet_kernel(offset, rest_ref, near_ref, far_ref, out_ref, own_ref):
    half = own_ref.shape[0]
    for span in spans(out_ref.shape[1]):
        far = far_ref[:, span].astype(jnp.float32)
        rest = rest_ref[:, offset + span.start:offset + span.stop].astype(jnp.float32)
        total = rest + near_ref[:, span].astype(jnp.float32)
        total = (total + jnp.concatenate([far[half:], far[:half]], axis=0)).astype(jnp.bfloat16)
        out_ref[:, span] = total
        own_ref[:, span] = total[:half]


def widen_kernel(*refs):
    *parts, out_ref = refs
    start = 0
    for part in parts:
        out_ref[:, start:start + part.shape[1]] = part[...]
        start += part.shape[1]


def mlp_kernel(step_no, count, cuts_in, cuts_out, *refs):
    x_refs, refs = refs[:count * cuts_in], refs[count * cuts_in:]
    if step_no > 0:
        tail_ref, refs = refs[0], refs[1:]
    (gain_ref, gate_ref, up_ref, down_ref), outs, refs = refs[:4], refs[4:4 + count * cuts_out], refs[4 + count * cuts_out:]
    rows_ref = refs[-1]
    part = outs[0].shape[0]
    dim, hidden = gate_ref.shape[1:]
    width_in, width_out = dim // cuts_in, dim // cuts_out
    experts = lax.axis_size("expert") // GROUP
    column = step_no * experts + lax.axis_index("expert") // GROUP
    lane = lax.broadcasted_iota(jnp.int32, (part, LANES), 1)
    weights = []
    for place in range(count):
        band = slice(place * part, (place + 1) * part)
        cuts = x_refs[place::count]
        square = jnp.zeros((part, LANES), jnp.float32)
        for ref in cuts:
            for start in range(0, width_in, LANES):
                piece = ref[:, start:start + LANES].astype(jnp.float32)
                square += piece * piece
        inv = lax.rsqrt(jnp.sum(square, axis=1, keepdims=True) / dim + 1e-06)
        for number, ref in enumerate(cuts):
            for span in spans(width_in):
                there = slice(number * width_in + span.start, number * width_in + span.stop)
                scaled = ref[:, span].astype(jnp.float32) * inv * gain_ref[:, there]
                rows_ref[band, there] = scaled.astype(jnp.bfloat16)
        if step_no == 0:
            tail = cuts[-1][:, width_in:]
            refs[0][band, :] = tail
        else:
            tail = tail_ref[band, :]
        chosen = jnp.where(lane == column, tail.astype(jnp.float32), 0.0)
        weights.append(jnp.sum(chosen, axis=1, keepdims=True))
    gated = jnp.zeros((count * part, hidden), jnp.float32)
    up_part = jnp.zeros((count * part, hidden), jnp.float32)
    for span in spans(dim):
        rows = rows_ref[:, span]
        gated += jnp.dot(rows, gate_ref[0, span, :], preferred_element_type=jnp.float32)
        up_part += jnp.dot(rows, up_ref[0, span, :], preferred_element_type=jnp.float32)
    inner = (gated / (1.0 + jnp.exp(-gated)) * up_part).astype(jnp.bfloat16)
    for span in spans(dim):
        terms = jnp.dot(inner, down_ref[0, :, span], preferred_element_type=jnp.float32)
        cut = span.start // width_out
        there = slice(span.start - cut * width_out, span.stop - cut * width_out)
        for place in range(count):
            weight = weights[place]
            mine = terms[place * part:(place + 1) * part]
            chosen = jnp.where(weight > 0.0, weight * mine, 0.0)
            outs[cut * count + place][:, there] = chosen.astype(jnp.bfloat16)


def mlp(step_no, cuts, cuts_out, tail, gain, gate, up, down):
    dim, hidden = gate.shape[1:]
    part, count = cuts[0][0].shape[0], len(cuts[0])
    gate, up, down = [pltpu.with_memory_space_constraint(w, pltpu.VMEM) for w in (gate, up, down)]
    first = step_no == 0
    xs = [piece for cut in cuts for piece in cut]
    args = xs + ([] if first else [tail]) + [gain, gate, up, down]
    result = call(
        functools.partial(mlp_kernel, step_no, count, len(cuts), cuts_out),
        [(part, dim // cuts_out)] * (count * cuts_out) + [(count * part, LANES)] * first, *args,
        scratch_shapes=[pltpu.VMEM((count * part, dim), jnp.bfloat16)],
        cost_estimate=pl.CostEstimate(
            flops=6 * count * part * dim * hidden, bytes_accessed=6 * dim * hidden, transcendentals=0
        ),
    )
    outs = [result[number * count:(number + 1) * count] for number in range(cuts_out)]
    return outs, result[-1] if first else tail


def add(*parts):
    rows = parts[0].shape[0]
    dim = parts[-1].shape[1]
    return call(add_kernel, [(rows, dim)], *parts)[0]


def split(*parts):
    rows, dim = parts[0].shape
    return call(functools.partial(split_kernel, 2), [(rows // 2, dim)] * 2, *parts)


def join(*parts):
    return call(join_kernel, [(sum(part.shape[0] for part in parts), parts[0].shape[1])], *parts)[0]


def on_device(states, routing, route_weight, norm_gain, gate_proj, up_proj, down_proj):
    owners = lax.axis_size("expert")
    row_dev, dim = states.shape[1:]
    passes_count = routing.shape[1]
    top, *middle = upper_flips(owners)

    weights = load((gate_proj, up_proj, down_proj))
    own, tail = states[0], None
    lanes = route(owners // GROUP, routing, route_weight)
    other, other_lanes = exchange(own, top, 0), exchange(lanes, top, 0)
    other, other_lanes, *weights = lax.optimization_barrier((other, other_lanes, *weights))
    (pair,) = call(first_kernel, [(2 * row_dev, dim + LANES)], own, other, lanes, other_lanes)
    pairs = [pair]
    for step_no in range(passes_count):
        last = step_no == passes_count - 1
        cuts_out = 1 if last else HALVES
        cuts = []
        for rows in pairs:
            for flips in middle:
                rows = join(rows, exchange(rows, flips, 0))
            mine = [rows] + [exchange(rows, flips, 0) for flips in SQUARE]
            cuts.append(mine + [exchange(rows, CORE, 0) for rows in mine])
        outs, tail = mlp(step_no, cuts, cuts_out, tail, norm_gain, *weights)

        sums = []
        for cut in outs:
            kept, sent = cut[:4], [exchange(rows, CORE, 0) for rows in cut[4:]]
            parts = [kept[0], sent[0]]
            for place in (3, 2, 1):
                parts.append(exchange(add(kept[place], sent[place]), SQUARE[place - 1], 0))
            for flips in middle[::-1]:
                low, high = split(*parts)
                parts = [low, exchange(high, flips, 0)]
            sums.append(parts)
        if not last:
            rests = [exchange(rows, STAY, 1) for rows in pairs]
            pairs, owns = [], []
            width = dim // cuts_out
            for number, parts in enumerate(sums):
                total = add(*parts)
                rest, offset = (rests[0], number * width) if len(rests) == 1 else (rests[number], 0)
                rows, own = call(
                    functools.partial(meet_kernel, offset), [(2 * row_dev, width), (row_dev, width)],
                    rest, exchange(total, STAY, 1), exchange(total, top, 1),
                )
                pairs.append(rows)
                owns.append(own)
            (own,) = call(widen_kernel, [(row_dev, dim)], *owns)
        else:
            low, high = split(*sums[0])
            rest = exchange(own, STAY, 1)
            own = add(rest, exchange(high, top, 1), exchange(low, STAY, 1))
    return own[None]


def solution(mesh):
    return jax.shard_map(
        on_device,
        mesh=mesh,
        in_specs=(
            P("segment", "expert", None),
            P("segment", None, "expert", None),
            P("segment", None, "expert", None),
            P("segment", None),
            P("segment", None, "expert"),
            P("segment", None, "expert"),
            P("segment", "expert", None),
        ),
        out_specs=P("segment", "expert", None),
        check_vma=False,
    )
```

```python
import functools

import jax
import jax.numpy as jnp
from jax import lax
from jax.experimental import pallas as pl
from jax.experimental.pallas import tpu as pltpu
from jax.sharding import PartitionSpec as P

GROUP = 4
LANES = 128
CHUNK = 1024
VMEM_LIMIT = 16 * 1024 * 1024
VMEM = pl.BlockSpec(memory_space=pltpu.VMEM)


def exchange(value, flips, hop):
    segments, owners = lax.axis_size("segment"), lax.axis_size("expert")
    if flips == (0, 0) and hop % segments == 0:
        return value
    pairs = []
    for seg in range(segments):
        for own in range(owners):
            target = (seg + hop) % segments * owners + (own ^ flips[own % 2])
            pairs.append((seg * owners + own, target))
    return lax.ppermute(value, ("segment", "expert"), pairs)


def upper_flips(owners):
    return [(1 << place,) * 2 for place in range(owners.bit_length() - 2, 2, -1)]


CORE = (1, 1)
SQUARE = ((4, 2), (2, 4), (6, 6))
STAY = (0, 0)


def spans(dim):
    return [slice(start, min(start + CHUNK, dim)) for start in range(0, dim, CHUNK)]


def call(kernel, outs, *args, **more):
    return pl.pallas_call(
        kernel,
        out_shape=[jax.ShapeDtypeStruct(shape, jnp.bfloat16) for shape in outs],
        in_specs=more.pop("in_specs", [VMEM] * len(args)),
        out_specs=[VMEM] * len(outs),
        compiler_params=pltpu.CompilerParams(vmem_limit_bytes=VMEM_LIMIT),
        **more,
    )(*args)


def load_kernel(gate_ref, up_ref, down_ref, gate_out, up_out, down_out, sems):
    copies = [
        pltpu.make_async_copy(source, target, sems.at[place])
        for place, (source, target) in enumerate(((gate_ref, gate_out), (up_ref, up_out), (down_ref, down_out)))
    ]
    for copy in copies:
        copy.start()
    for copy in copies:
        copy.wait()


def load(weights):
    return pl.pallas_call(
        load_kernel,
        out_shape=[pltpu.VMEM(w.shape, w.dtype) for w in weights],
        in_specs=[pl.BlockSpec(memory_space=pltpu.HBM)] * 3,
        out_specs=[VMEM] * 3,
        scratch_shapes=[pltpu.SemaphoreType.DMA((3,))],
        compiler_params=pltpu.CompilerParams(vmem_limit_bytes=VMEM_LIMIT),
        cost_estimate=pl.CostEstimate(
            flops=0, bytes_accessed=sum(2 * w.size for w in weights), transcendentals=0
        ),
    )(*[pltpu.with_memory_space_constraint(w, pltpu.HBM) for w in weights])


def prepare_kernel(experts, states_hbm, routing_hbm, weight_hbm, out_ref, states_ref, routing_ref, weight_ref, sems):
    pairs = ((routing_hbm, routing_ref), (weight_hbm, weight_ref), (states_hbm, states_ref))
    copies = [pltpu.make_async_copy(source, target, sems.at[place]) for place, (source, target) in enumerate(pairs)]
    for copy in copies:
        copy.start()
    for copy in copies:
        copy.wait()
    rows, dim = states_ref.shape[1:]
    for span in spans(dim):
        out_ref[:, span] = states_ref[0, :, span]
    lane = lax.broadcasted_iota(jnp.int32, (rows, LANES), 1).astype(jnp.float32)
    diagonal = lax.broadcasted_iota(jnp.int32, (rows, rows), 0) == lax.broadcasted_iota(jnp.int32, (rows, rows), 1)

    def upright(line):
        return jnp.sum(jnp.where(diagonal, line.astype(jnp.float32), 0.0), axis=1, keepdims=True)

    total = jnp.zeros((rows, LANES), jnp.float32)
    for step in range(routing_ref.shape[1]):
        for k in range(routing_ref.shape[2]):
            column = upright(routing_ref[0, step, k:k + 1, :]) + step * experts
            total += jnp.where(lane == column, upright(weight_ref[0, step, k:k + 1, :]), 0.0)
    out_ref[:, dim:] = total.astype(jnp.bfloat16)


def prepare(experts, states, routing, weight):
    args = [states, jnp.swapaxes(routing, 2, 3), jnp.swapaxes(weight, 2, 3)]
    rows, dim = states.shape[1:]
    (block,) = call(
        functools.partial(prepare_kernel, experts), [(rows, dim + LANES)],
        *[pltpu.with_memory_space_constraint(x, pltpu.HBM) for x in args],
        in_specs=[pl.BlockSpec(memory_space=pltpu.HBM)] * 3,
        scratch_shapes=[pltpu.VMEM(x.shape, x.dtype) for x in args] + [pltpu.SemaphoreType.DMA((3,))],
    )
    return block


def join_kernel(*refs):
    *parts, out_ref = refs
    for span in spans(out_ref.shape[1]):
        rows = [part[:, span].astype(jnp.float32) for part in parts]
        out_ref[:, span] = jnp.concatenate(rows, axis=0).astype(jnp.bfloat16)


def add_kernel(*refs):
    *parts, out_ref = refs
    for span in spans(out_ref.shape[1]):
        out_ref[:, span] = sum(part[:, span].astype(jnp.float32) for part in parts).astype(jnp.bfloat16)


def split_kernel(count, *refs):
    parts, outs = refs[:-count], refs[-count:]
    rows = outs[0].shape[0]
    for span in spans(outs[0].shape[1]):
        total = sum(part[:, span].astype(jnp.float32) for part in parts)
        for place, out_ref in enumerate(outs):
            out_ref[:, span] = total[place * rows:(place + 1) * rows].astype(jnp.bfloat16)


def normalise(raw_ref, gain_ref, out_ref):
    rows, dim = raw_ref.shape
    square = jnp.zeros((rows, LANES), jnp.float32)
    for start in range(0, dim, LANES):
        piece = raw_ref[:, start:start + LANES].astype(jnp.float32)
        square += piece * piece
    inv = lax.rsqrt(jnp.sum(square, axis=1, keepdims=True) / dim + 1e-06)
    for span in spans(dim):
        scaled = raw_ref[:, span].astype(jnp.float32) * inv * gain_ref[:, span]
        out_ref[:, span] = scaled.astype(jnp.bfloat16)


def first_kernel(own_ref, far_ref, gain_ref, out_ref, raw_ref):
    dim = raw_ref.shape[1]
    for span in spans(dim):
        rows = [ref[:, span].astype(jnp.float32) for ref in (own_ref, far_ref)]
        raw_ref[:, span] = jnp.concatenate(rows, axis=0).astype(jnp.bfloat16)
    tails = [ref[:, dim:].astype(jnp.float32) for ref in (own_ref, far_ref)]
    out_ref[:, dim:] = jnp.concatenate(tails, axis=0).astype(jnp.bfloat16)
    normalise(raw_ref, gain_ref, out_ref)


def meet_kernel(rest_ref, near_ref, far_ref, gain_ref, out_ref, raw_ref, own_ref):
    half = own_ref.shape[0]
    for span in spans(out_ref.shape[1]):
        far = far_ref[:, span].astype(jnp.float32)
        total = rest_ref[:, span].astype(jnp.float32) + near_ref[:, span].astype(jnp.float32)
        total = (total + jnp.concatenate([far[half:], far[:half]], axis=0)).astype(jnp.bfloat16)
        raw_ref[:, span] = total
        own_ref[:, span] = total[:half]
    normalise(raw_ref, gain_ref, out_ref)


def mlp_kernel(step_no, *refs):
    x_refs, refs = refs[:8], refs[8:]
    if step_no > 0:
        tail_ref, refs = refs[0], refs[1:]
    (gate_ref, up_ref, down_ref), outs, refs = refs[:3], refs[3:11], refs[11:]
    part = outs[0].shape[0]
    dim, hidden = gate_ref.shape[1:]
    experts = lax.axis_size("expert") // GROUP
    column = step_no * experts + lax.axis_index("expert") // GROUP
    lane = lax.broadcasted_iota(jnp.int32, (part, LANES), 1)
    weights = []
    for place, ref in enumerate(x_refs):
        band = slice(place * part, (place + 1) * part)
        if step_no == 0:
            tail = ref[:, dim:]
            refs[0][band, :] = tail
        else:
            tail = tail_ref[band, :]
        chosen = jnp.where(lane == column, tail.astype(jnp.float32), 0.0)
        weights.append(jnp.sum(chosen, axis=1, keepdims=True))
    gated = jnp.zeros((8 * part, hidden), jnp.float32)
    up_part = jnp.zeros((8 * part, hidden), jnp.float32)
    for span in spans(dim):
        rows = jnp.concatenate([ref[:, span].astype(jnp.float32) for ref in x_refs], axis=0).astype(jnp.bfloat16)
        gated += jnp.dot(rows, gate_ref[0, span, :], preferred_element_type=jnp.float32)
        up_part += jnp.dot(rows, up_ref[0, span, :], preferred_element_type=jnp.float32)
    inner = (gated / (1.0 + jnp.exp(-gated)) * up_part).astype(jnp.bfloat16)
    for span in spans(dim):
        terms = jnp.dot(inner, down_ref[0, :, span], preferred_element_type=jnp.float32)
        for place, out_ref in enumerate(outs):
            weight = weights[place]
            mine = terms[place * part:(place + 1) * part]
            out_ref[:, span] = jnp.where(weight > 0.0, weight * mine, 0.0).astype(jnp.bfloat16)


def mlp(step_no, xs, tail, gate, up, down):
    dim, hidden = gate.shape[1:]
    part = xs[0].shape[0]
    gate, up, down = [pltpu.with_memory_space_constraint(w, pltpu.VMEM) for w in (gate, up, down)]
    first = step_no == 0
    args = list(xs) + ([] if first else [tail]) + [gate, up, down]
    result = call(
        functools.partial(mlp_kernel, step_no), [(part, dim)] * 8 + [(8 * part, LANES)] * first, *args,
        cost_estimate=pl.CostEstimate(
            flops=48 * part * dim * hidden, bytes_accessed=6 * dim * hidden, transcendentals=0
        ),
    )
    return result[:8], result[8] if first else tail


def add(*parts):
    rows = parts[0].shape[0]
    dim = parts[-1].shape[1]
    return call(add_kernel, [(rows, dim)], *parts)[0]


def split(*parts):
    rows, dim = parts[0].shape
    return call(functools.partial(split_kernel, 2), [(rows // 2, dim)] * 2, *parts)


def join(*parts):
    return call(join_kernel, [(sum(part.shape[0] for part in parts), parts[0].shape[1])], *parts)[0]


def on_device(states, routing, route_weight, norm_gain, gate_proj, up_proj, down_proj):
    owners = lax.axis_size("expert")
    row_dev, dim = states.shape[1:]
    passes_count = routing.shape[1]
    top, *middle = upper_flips(owners)

    weights = load((gate_proj, up_proj, down_proj))
    block = prepare(owners // GROUP, states, routing, route_weight)
    other = exchange(block, top, 0)
    block, other, *weights = lax.optimization_barrier((block, other, *weights))
    pair, raw = call(first_kernel, [(2 * row_dev, dim + LANES), (2 * row_dev, dim)], block, other, norm_gain)
    own, tail = states[0], None
    for step_no in range(passes_count):
        rows_a = pair
        for flips in middle:
            rows_a = join(rows_a, exchange(rows_a, flips, 0))
        mine = [rows_a] + [exchange(rows_a, flips, 0) for flips in SQUARE]
        outs, tail = mlp(step_no, mine + [exchange(rows, CORE, 0) for rows in mine], tail, *weights)

        kept, sent = outs[:4], [exchange(rows, CORE, 0) for rows in outs[4:]]
        parts = [kept[0], sent[0]]
        for place in (3, 2, 1):
            parts.append(exchange(add(kept[place], sent[place]), SQUARE[place - 1], 0))
        for flips in middle[::-1]:
            low, high = split(*parts)
            parts = [low, exchange(high, flips, 0)]
        if step_no < passes_count - 1:
            total = add(*parts)
            rest = exchange(raw, STAY, 1)
            pair, raw, own = call(
                meet_kernel, [(2 * row_dev, dim), (2 * row_dev, dim), (row_dev, dim)],
                rest, exchange(total, STAY, 1), exchange(total, top, 1), norm_gain,
            )
        else:
            low, high = split(*parts)
            rest = exchange(own, STAY, 1)
            own = add(rest, exchange(high, top, 1), exchange(low, STAY, 1))
    return own[None]


def solution(mesh):
    return jax.shard_map(
        on_device,
        mesh=mesh,
        in_specs=(
            P("segment", "expert", None),
            P("segment", None, "expert", None),
            P("segment", None, "expert", None),
            P("segment", None),
            P("segment", None, "expert"),
            P("segment", None, "expert"),
            P("segment", "expert", None),
        ),
        out_specs=P("segment", "expert", None),
        check_vma=False,
    )
```

```python
import functools

import jax
import jax.numpy as jnp
from jax import lax
from jax.experimental import pallas as pl
from jax.experimental.pallas import tpu as pltpu
from jax.sharding import PartitionSpec as P

GROUP = 4
LANES = 128
CHUNK = 1024
VMEM_LIMIT = 16 * 1024 * 1024
VMEM = pl.BlockSpec(memory_space=pltpu.VMEM)


def exchange(value, flips, hop):
    segments, owners = lax.axis_size("segment"), lax.axis_size("expert")
    if flips == (0, 0) and hop % segments == 0:
        return value
    pairs = []
    for seg in range(segments):
        for own in range(owners):
            target = (seg + hop) % segments * owners + (own ^ flips[own % 2])
            pairs.append((seg * owners + own, target))
    return lax.ppermute(value, ("segment", "expert"), pairs)


def upper_flips(owners):
    return [(1 << place,) * 2 for place in range(owners.bit_length() - 2, 2, -1)]


CORE = (1, 1)
SQUARE = ((4, 2), (2, 4), (6, 6))
STAY = (0, 0)


def spans(dim):
    return [slice(start, min(start + CHUNK, dim)) for start in range(0, dim, CHUNK)]


def call(kernel, outs, *args, **more):
    return pl.pallas_call(
        kernel,
        out_shape=[jax.ShapeDtypeStruct(shape, jnp.bfloat16) for shape in outs],
        in_specs=more.pop("in_specs", [VMEM] * len(args)),
        out_specs=[VMEM] * len(outs),
        compiler_params=pltpu.CompilerParams(vmem_limit_bytes=VMEM_LIMIT),
        **more,
    )(*args)


def load_kernel(count, *refs):
    sems = refs[-1]
    copies = [pltpu.make_async_copy(refs[place], refs[count + place], sems.at[place]) for place in range(count)]
    for copy in copies:
        copy.start()
    for copy in copies:
        copy.wait()


def load(*weights):
    count = len(weights)
    return pl.pallas_call(
        functools.partial(load_kernel, count),
        out_shape=[pltpu.VMEM(w.shape, w.dtype) for w in weights],
        in_specs=[pl.BlockSpec(memory_space=pltpu.HBM)] * count,
        out_specs=[VMEM] * count,
        scratch_shapes=[pltpu.SemaphoreType.DMA((count,))],
        compiler_params=pltpu.CompilerParams(vmem_limit_bytes=VMEM_LIMIT),
        cost_estimate=pl.CostEstimate(
            flops=0, bytes_accessed=sum(2 * w.size for w in weights), transcendentals=0
        ),
    )(*[pltpu.with_memory_space_constraint(w, pltpu.HBM) for w in weights])


def normalise(raw_ref, gain_ref, out_ref):
    rows, dim = raw_ref.shape[0], gain_ref.shape[1]
    square = jnp.zeros((rows, LANES), jnp.float32)
    for start in range(0, dim, LANES):
        piece = raw_ref[:, start:start + LANES].astype(jnp.float32)
        square += piece * piece
    inv = lax.rsqrt(jnp.sum(square, axis=1, keepdims=True) / dim + 1e-06)
    for span in spans(dim):
        scaled = raw_ref[:, span].astype(jnp.float32) * inv * gain_ref[:, span]
        out_ref[:, span] = scaled.astype(jnp.bfloat16)


def prepare_kernel(experts, states_hbm, routing_hbm, weight_hbm, gain_hbm, raw_ref, out_ref, gain_ref,
                   states_ref, routing_ref, weight_ref, sems):
    pairs = ((routing_hbm, routing_ref), (weight_hbm, weight_ref), (states_hbm, states_ref), (gain_hbm, gain_ref))
    copies = [pltpu.make_async_copy(source, target, sems.at[place]) for place, (source, target) in enumerate(pairs)]
    for copy in copies:
        copy.start()
    for copy in copies:
        copy.wait()
    rows, dim = states_ref.shape[1:]
    for span in spans(dim):
        raw_ref[:, span] = states_ref[0, :, span]
    lane = lax.broadcasted_iota(jnp.int32, (rows, LANES), 1).astype(jnp.float32)
    diagonal = lax.broadcasted_iota(jnp.int32, (rows, rows), 0) == lax.broadcasted_iota(jnp.int32, (rows, rows), 1)

    def upright(line):
        return jnp.sum(jnp.where(diagonal, line.astype(jnp.float32), 0.0), axis=1, keepdims=True)

    total = jnp.zeros((rows, LANES), jnp.float32)
    for step in range(routing_ref.shape[1]):
        for k in range(routing_ref.shape[2]):
            column = upright(routing_ref[0, step, k:k + 1, :]) + step * experts
            total += jnp.where(lane == column, upright(weight_ref[0, step, k:k + 1, :]), 0.0)
    raw_ref[:, dim:] = total.astype(jnp.bfloat16)
    out_ref[:, dim:] = total.astype(jnp.bfloat16)
    normalise(raw_ref, gain_ref, out_ref)


def prepare(experts, states, routing, weight, gain):
    args = [states, jnp.swapaxes(routing, 2, 3), jnp.swapaxes(weight, 2, 3), gain]
    rows, dim = states.shape[1:]
    block = jax.ShapeDtypeStruct((rows, dim + LANES), jnp.bfloat16)
    return pl.pallas_call(
        functools.partial(prepare_kernel, experts),
        out_shape=[block, block, pltpu.VMEM(gain.shape, gain.dtype)],
        in_specs=[pl.BlockSpec(memory_space=pltpu.HBM)] * 4,
        out_specs=[VMEM] * 3,
        scratch_shapes=[pltpu.VMEM(x.shape, x.dtype) for x in args[:3]] + [pltpu.SemaphoreType.DMA((4,))],
        compiler_params=pltpu.CompilerParams(vmem_limit_bytes=VMEM_LIMIT),
    )(*[pltpu.with_memory_space_constraint(x, pltpu.HBM) for x in args])


def join_kernel(*refs):
    *parts, out_ref = refs
    for span in spans(out_ref.shape[1]):
        rows = [part[:, span].astype(jnp.float32) for part in parts]
        out_ref[:, span] = jnp.concatenate(rows, axis=0).astype(jnp.bfloat16)


def add_kernel(*refs):
    *parts, out_ref = refs
    for span in spans(out_ref.shape[1]):
        out_ref[:, span] = sum(part[:, span].astype(jnp.float32) for part in parts).astype(jnp.bfloat16)


def split_kernel(count, *refs):
    parts, outs = refs[:-count], refs[-count:]
    rows = outs[0].shape[0]
    for span in spans(outs[0].shape[1]):
        total = sum(part[:, span].astype(jnp.float32) for part in parts)
        for place, out_ref in enumerate(outs):
            out_ref[:, span] = total[place * rows:(place + 1) * rows].astype(jnp.bfloat16)


def second_kernel(own_ref, far_ref, gain_ref, out_ref, raw_ref):
    dim = raw_ref.shape[1]
    for span in spans(dim):
        rows = [ref[:, span].astype(jnp.float32) for ref in (own_ref, far_ref)]
        raw_ref[:, span] = jnp.concatenate(rows, axis=0).astype(jnp.bfloat16)
    out_ref[:, dim:] = far_ref[:, dim:]
    normalise(far_ref, gain_ref, out_ref)


def meet_kernel(rest_ref, near_ref, far_ref, gain_ref, out_ref, raw_ref, own_ref):
    half = own_ref.shape[0]
    for span in spans(out_ref.shape[1]):
        far = far_ref[:, span].astype(jnp.float32)
        total = rest_ref[:, span].astype(jnp.float32) + near_ref[:, span].astype(jnp.float32)
        total = (total + jnp.concatenate([far[half:], far[:half]], axis=0)).astype(jnp.bfloat16)
        raw_ref[:, span] = total
        own_ref[:, span] = total[:half]
    normalise(raw_ref, gain_ref, out_ref)


def mlp_kernel(step_no, count, order, *refs):
    x_refs, refs = refs[:count], refs[count:]
    if step_no > 0:
        tail_ref, refs = refs[0], refs[1:]
    (gate_ref, up_ref, down_ref), outs, refs = refs[:3], refs[3:11], refs[11:]
    part = outs[0].shape[0]
    dim, hidden = gate_ref.shape[1:]
    experts = lax.axis_size("expert") // GROUP
    column = step_no * experts + lax.axis_index("expert") // GROUP
    def stack(span):
        values = [ref[:, span].astype(jnp.float32) for ref in x_refs]
        return jnp.concatenate([values[place][start:stop] for place, start, stop in order], axis=0)

    if step_no == 0:
        tails = stack(slice(dim, dim + LANES))
        refs[0][...] = tails.astype(jnp.bfloat16)
    else:
        tails = tail_ref[...].astype(jnp.float32)
    lane = lax.broadcasted_iota(jnp.int32, tails.shape, 1)
    weights = jnp.sum(jnp.where(lane == column, tails, 0.0), axis=1, keepdims=True)
    gated = jnp.zeros((8 * part, hidden), jnp.float32)
    up_part = jnp.zeros((8 * part, hidden), jnp.float32)
    for span in spans(dim):
        rows = stack(span).astype(jnp.bfloat16)
        gated += jnp.dot(rows, gate_ref[0, span, :], preferred_element_type=jnp.float32)
        up_part += jnp.dot(rows, up_ref[0, span, :], preferred_element_type=jnp.float32)
    inner = (gated / (1.0 + jnp.exp(-gated)) * up_part).astype(jnp.bfloat16)
    for span in spans(dim):
        terms = jnp.dot(inner, down_ref[0, :, span], preferred_element_type=jnp.float32)
        chosen = jnp.where(weights > 0.0, weights * terms, 0.0)
        for place, out_ref in enumerate(outs):
            out_ref[:, span] = chosen[place * part:(place + 1) * part].astype(jnp.bfloat16)


def mlp(step_no, xs, order, tail, gate, up, down):
    dim, hidden = gate.shape[1:]
    part = sum(x.shape[0] for x in xs) // 8
    gate, up, down = [pltpu.with_memory_space_constraint(w, pltpu.VMEM) for w in (gate, up, down)]
    first = step_no == 0
    args = list(xs) + ([] if first else [tail]) + [gate, up, down]
    result = call(
        functools.partial(mlp_kernel, step_no, len(xs), order), [(part, dim)] * 8 + [(8 * part, LANES)] * first, *args,
        cost_estimate=pl.CostEstimate(
            flops=48 * part * dim * hidden, bytes_accessed=6 * dim * hidden, transcendentals=0
        ),
    )
    return result[:8], result[8] if first else tail


def add(*parts):
    rows = parts[0].shape[0]
    dim = parts[-1].shape[1]
    return call(add_kernel, [(rows, dim)], *parts)[0]


def split(*parts):
    rows, dim = parts[0].shape
    return call(functools.partial(split_kernel, 2), [(rows // 2, dim)] * 2, *parts)


def join(*parts):
    return call(join_kernel, [(sum(part.shape[0] for part in parts), parts[0].shape[1])], *parts)[0]


def square(rows):
    return [rows] + [exchange(rows, flips, 0) for flips in SQUARE]


def both_cores(mine):
    xs = mine + [exchange(rows, CORE, 0) for rows in mine]
    return xs, [(place, 0, rows.shape[0]) for place, rows in enumerate(xs)]


def on_device(states, routing, route_weight, norm_gain, gate_proj, up_proj, down_proj):
    owners = lax.axis_size("expert")
    row_dev, dim = states.shape[1:]
    passes_count = routing.shape[1]
    top, *middle = upper_flips(owners)

    raw, pair, gain = prepare(owners // GROUP, states, routing, route_weight, norm_gain)
    gain = pltpu.with_memory_space_constraint(gain, pltpu.VMEM)
    other = exchange(raw, top, 0)
    (gate,) = load(gate_proj)
    firsts = square(pair)
    other, gate, firsts = lax.optimization_barrier((other, gate, firsts))
    pair, raw = call(second_kernel, [pair.shape, (2 * row_dev, dim)], raw, other, gain)
    pair, up_hbm, down_hbm = lax.optimization_barrier((pair, up_proj, down_proj))
    up, down = load(up_hbm, down_hbm)
    seconds = square(pair)
    seconds[3], up, down = lax.optimization_barrier((seconds[3], up, down))
    weights = (gate, up, down)
    if middle:
        rows_a = join(firsts[0], seconds[0])
        for flips in middle:
            rows_a = join(rows_a, exchange(rows_a, flips, 0))
        xs, order = both_cores(square(rows_a))
    else:
        far = exchange(join(*firsts), CORE, 0)
        xs = firsts + seconds + [far] + [exchange(rows, CORE, 0) for rows in seconds]
        order = [(place + late, 0, row_dev) for place in range(4) for late in (0, 4)]
        for place in range(4):
            order += [(8, place * row_dev, (place + 1) * row_dev), (9 + place, 0, row_dev)]
    own, tail = states[0], None
    for step_no in range(passes_count):
        outs, tail = mlp(step_no, xs, order, tail, *weights)

        kept, sent = outs[:4], [exchange(rows, CORE, 0) for rows in outs[4:]]
        parts = [kept[0], sent[0]]
        for place in (3, 2, 1):
            parts.append(exchange(add(kept[place], sent[place]), SQUARE[place - 1], 0))
        for flips in middle[::-1]:
            low, high = split(*parts)
            parts = [low, exchange(high, flips, 0)]
        if step_no < passes_count - 1:
            total = add(*parts)
            rest = exchange(raw, STAY, 1)
            pair, raw, own = call(
                meet_kernel, [(2 * row_dev, dim), (2 * row_dev, dim), (row_dev, dim)],
                rest, exchange(total, STAY, 1), exchange(total, top, 1), gain,
            )
            for flips in middle:
                pair = join(pair, exchange(pair, flips, 0))
            xs, order = both_cores(square(pair))
        else:
            low, high = split(*parts)
            rest = exchange(own, STAY, 1)
            own = add(rest, exchange(high, top, 1), exchange(low, STAY, 1))
    return own[None]


def solution(mesh):
    return jax.shard_map(
        on_device,
        mesh=mesh,
        in_specs=(
            P("segment", "expert", None),
            P("segment", None, "expert", None),
            P("segment", None, "expert", None),
            P("segment", None),
            P("segment", None, "expert"),
            P("segment", None, "expert"),
            P("segment", "expert", None),
        ),
        out_specs=P("segment", "expert", None),
        check_vma=False,
    )
```

```python
import functools

import jax
import jax.numpy as jnp
from jax import lax
from jax.experimental import pallas as pl
from jax.experimental.pallas import tpu as pltpu
from jax.sharding import PartitionSpec as P

GROUP = 4
LANES = 128
CHUNK = 1024
VMEM_LIMIT = 16 * 1024 * 1024
VMEM = pl.BlockSpec(memory_space=pltpu.VMEM)


def exchange(value, flips, hop):
    segments, owners = lax.axis_size("segment"), lax.axis_size("expert")
    if flips == (0, 0) and hop % segments == 0:
        return value
    pairs = []
    for seg in range(segments):
        for own in range(owners):
            target = (seg + hop) % segments * owners + (own ^ flips[own % 2])
            pairs.append((seg * owners + own, target))
    return lax.ppermute(value, ("segment", "expert"), pairs)


def upper_flips(owners):
    return [(1 << place,) * 2 for place in range(owners.bit_length() - 2, 2, -1)]


CORE = (1, 1)
SQUARE = ((4, 2), (2, 4), (6, 6))
STAY = (0, 0)


def spans(dim):
    return [slice(start, min(start + CHUNK, dim)) for start in range(0, dim, CHUNK)]


def call(kernel, outs, *args, **more):
    return pl.pallas_call(
        kernel,
        out_shape=[jax.ShapeDtypeStruct(shape, jnp.bfloat16) for shape in outs],
        in_specs=more.pop("in_specs", [VMEM] * len(args)),
        out_specs=[VMEM] * len(outs),
        compiler_params=pltpu.CompilerParams(vmem_limit_bytes=VMEM_LIMIT),
        **more,
    )(*args)


def load_kernel(count, *refs):
    sems = refs[-1]
    copies = [pltpu.make_async_copy(refs[place], refs[count + place], sems.at[place]) for place in range(count)]
    for copy in copies:
        copy.start()
    for copy in copies:
        copy.wait()


def load(*weights):
    count = len(weights)
    return pl.pallas_call(
        functools.partial(load_kernel, count),
        out_shape=[pltpu.VMEM(w.shape, w.dtype) for w in weights],
        in_specs=[pl.BlockSpec(memory_space=pltpu.HBM)] * count,
        out_specs=[VMEM] * count,
        scratch_shapes=[pltpu.SemaphoreType.DMA((count,))],
        compiler_params=pltpu.CompilerParams(vmem_limit_bytes=VMEM_LIMIT),
        cost_estimate=pl.CostEstimate(
            flops=0, bytes_accessed=sum(2 * w.size for w in weights), transcendentals=0
        ),
    )(*[pltpu.with_memory_space_constraint(w, pltpu.HBM) for w in weights])


def prepare_kernel(experts, states_hbm, routing_hbm, weight_hbm, out_ref, states_ref, routing_ref, weight_ref, sems):
    pairs = ((routing_hbm, routing_ref), (weight_hbm, weight_ref), (states_hbm, states_ref))
    copies = [pltpu.make_async_copy(source, target, sems.at[place]) for place, (source, target) in enumerate(pairs)]
    for copy in copies:
        copy.start()
    for copy in copies:
        copy.wait()
    rows, dim = states_ref.shape[1:]
    for span in spans(dim):
        out_ref[:, span] = states_ref[0, :, span]
    lane = lax.broadcasted_iota(jnp.int32, (rows, LANES), 1).astype(jnp.float32)
    diagonal = lax.broadcasted_iota(jnp.int32, (rows, rows), 0) == lax.broadcasted_iota(jnp.int32, (rows, rows), 1)

    def upright(line):
        return jnp.sum(jnp.where(diagonal, line.astype(jnp.float32), 0.0), axis=1, keepdims=True)

    total = jnp.zeros((rows, LANES), jnp.float32)
    for step in range(routing_ref.shape[1]):
        for k in range(routing_ref.shape[2]):
            column = upright(routing_ref[0, step, k:k + 1, :]) + step * experts
            total += jnp.where(lane == column, upright(weight_ref[0, step, k:k + 1, :]), 0.0)
    out_ref[:, dim:] = total.astype(jnp.bfloat16)


def prepare(experts, states, routing, weight):
    args = [states, jnp.swapaxes(routing, 2, 3), jnp.swapaxes(weight, 2, 3)]
    rows, dim = states.shape[1:]
    (block,) = call(
        functools.partial(prepare_kernel, experts), [(rows, dim + LANES)],
        *[pltpu.with_memory_space_constraint(x, pltpu.HBM) for x in args],
        in_specs=[pl.BlockSpec(memory_space=pltpu.HBM)] * 3,
        scratch_shapes=[pltpu.VMEM(x.shape, x.dtype) for x in args] + [pltpu.SemaphoreType.DMA((3,))],
    )
    return block


def join_kernel(*refs):
    *parts, out_ref = refs
    for span in spans(out_ref.shape[1]):
        rows = [part[:, span].astype(jnp.float32) for part in parts]
        out_ref[:, span] = jnp.concatenate(rows, axis=0).astype(jnp.bfloat16)


def add_kernel(*refs):
    *parts, out_ref = refs
    for span in spans(out_ref.shape[1]):
        out_ref[:, span] = sum(part[:, span].astype(jnp.float32) for part in parts).astype(jnp.bfloat16)


def split_kernel(count, *refs):
    parts, outs = refs[:-count], refs[-count:]
    rows = outs[0].shape[0]
    for span in spans(outs[0].shape[1]):
        total = sum(part[:, span].astype(jnp.float32) for part in parts)
        for place, out_ref in enumerate(outs):
            out_ref[:, span] = total[place * rows:(place + 1) * rows].astype(jnp.bfloat16)


def normalise(raw_ref, gain_ref, out_ref):
    rows, dim = raw_ref.shape
    square = jnp.zeros((rows, LANES), jnp.float32)
    for start in range(0, dim, LANES):
        piece = raw_ref[:, start:start + LANES].astype(jnp.float32)
        square += piece * piece
    inv = lax.rsqrt(jnp.sum(square, axis=1, keepdims=True) / dim + 1e-06)
    for span in spans(dim):
        scaled = raw_ref[:, span].astype(jnp.float32) * inv * gain_ref[:, span]
        out_ref[:, span] = scaled.astype(jnp.bfloat16)


def first_kernel(own_ref, far_ref, gain_ref, out_ref, raw_ref):
    dim = raw_ref.shape[1]
    for span in spans(dim):
        rows = [ref[:, span].astype(jnp.float32) for ref in (own_ref, far_ref)]
        raw_ref[:, span] = jnp.concatenate(rows, axis=0).astype(jnp.bfloat16)
    tails = [ref[:, dim:].astype(jnp.float32) for ref in (own_ref, far_ref)]
    out_ref[:, dim:] = jnp.concatenate(tails, axis=0).astype(jnp.bfloat16)
    normalise(raw_ref, gain_ref, out_ref)


def meet_kernel(rest_ref, near_ref, far_ref, gain_ref, out_ref, own_ref, raw_ref):
    half = own_ref.shape[0]
    for span in spans(out_ref.shape[1]):
        far = far_ref[:, span].astype(jnp.float32)
        total = rest_ref[:, span].astype(jnp.float32) + near_ref[:, span].astype(jnp.float32)
        total = (total + jnp.concatenate([far[half:], far[:half]], axis=0)).astype(jnp.bfloat16)
        raw_ref[:, span] = total
        own_ref[:, span] = total[:half]
    normalise(raw_ref, gain_ref, out_ref)


def mlp_kernel(step_no, *refs):
    x_refs, refs = refs[:8], refs[8:]
    if step_no > 0:
        tail_ref, refs = refs[0], refs[1:]
    (gate_ref, up_ref, down_ref), outs, refs = refs[:3], refs[3:11], refs[11:]
    part = outs[0].shape[0]
    dim, hidden = gate_ref.shape[1:]
    experts = lax.axis_size("expert") // GROUP
    column = step_no * experts + lax.axis_index("expert") // GROUP
    lane = lax.broadcasted_iota(jnp.int32, (part, LANES), 1)
    weights = []
    for place, ref in enumerate(x_refs):
        band = slice(place * part, (place + 1) * part)
        if step_no == 0:
            tail = ref[:, dim:]
            refs[0][band, :] = tail
        else:
            tail = tail_ref[band, :]
        chosen = jnp.where(lane == column, tail.astype(jnp.float32), 0.0)
        weights.append(jnp.sum(chosen, axis=1, keepdims=True))
    gated = jnp.zeros((8 * part, hidden), jnp.float32)
    up_part = jnp.zeros((8 * part, hidden), jnp.float32)
    for span in spans(dim):
        rows = jnp.concatenate([ref[:, span] for ref in x_refs], axis=0)
        gated += jnp.dot(rows, gate_ref[0, span, :], preferred_element_type=jnp.float32)
        up_part += jnp.dot(rows, up_ref[0, span, :], preferred_element_type=jnp.float32)
    inner = (gated / (1.0 + jnp.exp(-gated)) * up_part).astype(jnp.bfloat16)
    for span in spans(dim):
        terms = jnp.dot(inner, down_ref[0, :, span], preferred_element_type=jnp.float32)
        for place, out_ref in enumerate(outs):
            weight = weights[place]
            mine = terms[place * part:(place + 1) * part]
            out_ref[:, span] = jnp.where(weight > 0.0, weight * mine, 0.0).astype(jnp.bfloat16)


def mlp(step_no, xs, tail, gate, up, down):
    dim, hidden = gate.shape[1:]
    part = xs[0].shape[0]
    gate, up, down = [pltpu.with_memory_space_constraint(w, pltpu.VMEM) for w in (gate, up, down)]
    first = step_no == 0
    args = list(xs) + ([] if first else [tail]) + [gate, up, down]
    result = call(
        functools.partial(mlp_kernel, step_no), [(part, dim)] * 8 + [(8 * part, LANES)] * first, *args,
        cost_estimate=pl.CostEstimate(
            flops=48 * part * dim * hidden, bytes_accessed=6 * dim * hidden, transcendentals=0
        ),
    )
    return result[:8], result[8] if first else tail


def add(*parts):
    rows = parts[0].shape[0]
    dim = parts[-1].shape[1]
    return call(add_kernel, [(rows, dim)], *parts)[0]


def split(*parts):
    rows, dim = parts[0].shape
    return call(functools.partial(split_kernel, 2), [(rows // 2, dim)] * 2, *parts)


def join(*parts):
    return call(join_kernel, [(sum(part.shape[0] for part in parts), parts[0].shape[1])], *parts)[0]


def on_device(states, routing, route_weight, norm_gain, gate_proj, up_proj, down_proj):
    owners = lax.axis_size("expert")
    row_dev, dim = states.shape[1:]
    passes_count = routing.shape[1]
    top, *middle = upper_flips(owners)

    gate, up = load(gate_proj, up_proj)
    block = prepare(owners // GROUP, states, routing, route_weight)
    other = exchange(block, top, 0)
    other, gate, up = lax.optimization_barrier((other, gate, up))
    pair, raw = call(first_kernel, [(2 * row_dev, dim + LANES), (2 * row_dev, dim)], block, other, norm_gain)
    pair, down_hbm = lax.optimization_barrier((pair, down_proj))
    (down,) = load(down_hbm)
    own, tail = states[0], None
    for step_no in range(passes_count):
        rows_a = pair
        for flips in middle:
            rows_a = join(rows_a, exchange(rows_a, flips, 0))
        mine = [rows_a] + [exchange(rows_a, flips, 0) for flips in SQUARE]
        near = rows_a
        if step_no == 0:
            near, down = lax.optimization_barrier((near, down))
        fars = [exchange(rows, CORE, 0) for rows in [near] + mine[1:]]
        outs, tail = mlp(step_no, mine + fars, tail, gate, up, down)

        kept, sent = outs[:4], [exchange(rows, CORE, 0) for rows in outs[4:]]
        parts = [kept[0], sent[0]]
        for place in (3, 2, 1):
            parts.append(exchange(add(kept[place], sent[place]), SQUARE[place - 1], 0))
        for flips in middle[::-1]:
            low, high = split(*parts)
            parts = [low, exchange(high, flips, 0)]
        if step_no < passes_count - 1:
            total = add(*parts)
            rest = exchange(raw, STAY, 1)
            more = step_no < passes_count - 2
            pair, own, *raws = call(
                meet_kernel, [(2 * row_dev, dim), (row_dev, dim)] + [(2 * row_dev, dim)] * more,
                rest, exchange(total, STAY, 1), exchange(total, top, 1), norm_gain,
                scratch_shapes=[] if more else [pltpu.VMEM((2 * row_dev, dim), jnp.bfloat16)],
            )
            raw = raws[0] if more else None
        else:
            low, high = split(*parts)
            rest = exchange(own, STAY, 1)
            own = add(rest, exchange(high, top, 1), exchange(low, STAY, 1))
    return own[None]


def solution(mesh):
    return jax.shard_map(
        on_device,
        mesh=mesh,
        in_specs=(
            P("segment", "expert", None),
            P("segment", None, "expert", None),
            P("segment", None, "expert", None),
            P("segment", None),
            P("segment", None, "expert"),
            P("segment", None, "expert"),
            P("segment", "expert", None),
        ),
        out_specs=P("segment", "expert", None),
        check_vma=False,
    )
```

```python
import functools

import jax
import jax.numpy as jnp
from jax import lax
from jax.experimental import pallas as pl
from jax.experimental.pallas import tpu as pltpu
from jax.sharding import PartitionSpec as P

GROUP = 4
LANES = 128
CHUNK = 1024
VMEM_LIMIT = 16 * 1024 * 1024
VMEM = pl.BlockSpec(memory_space=pltpu.VMEM)


def exchange(value, flips, hop):
    segments, owners = lax.axis_size("segment"), lax.axis_size("expert")
    if flips == (0, 0) and hop % segments == 0:
        return value
    pairs = []
    for seg in range(segments):
        for own in range(owners):
            target = (seg + hop) % segments * owners + (own ^ flips[own % 2])
            pairs.append((seg * owners + own, target))
    return lax.ppermute(value, ("segment", "expert"), pairs)


def upper_flips(owners):
    return [(1 << place,) * 2 for place in range(owners.bit_length() - 2, 2, -1)]


CORE = (1, 1)
SQUARE = ((4, 2), (2, 4), (6, 6))
STAY = (0, 0)


def spans(dim):
    return [slice(start, min(start + CHUNK, dim)) for start in range(0, dim, CHUNK)]


def call(kernel, outs, *args, **more):
    return pl.pallas_call(
        kernel,
        out_shape=[jax.ShapeDtypeStruct(shape, jnp.bfloat16) for shape in outs],
        in_specs=more.pop("in_specs", [VMEM] * len(args)),
        out_specs=[VMEM] * len(outs),
        compiler_params=pltpu.CompilerParams(vmem_limit_bytes=VMEM_LIMIT),
        **more,
    )(*args)


def load_kernel(count, *refs):
    sems = refs[-1]
    copies = [pltpu.make_async_copy(refs[place], refs[count + place], sems.at[place]) for place in range(count)]
    for copy in copies:
        copy.start()
    for copy in copies:
        copy.wait()


def load(*weights):
    count = len(weights)
    return pl.pallas_call(
        functools.partial(load_kernel, count),
        out_shape=[pltpu.VMEM(w.shape, w.dtype) for w in weights],
        in_specs=[pl.BlockSpec(memory_space=pltpu.HBM)] * count,
        out_specs=[VMEM] * count,
        scratch_shapes=[pltpu.SemaphoreType.DMA((count,))],
        compiler_params=pltpu.CompilerParams(vmem_limit_bytes=VMEM_LIMIT),
        cost_estimate=pl.CostEstimate(
            flops=0, bytes_accessed=sum(2 * w.size for w in weights), transcendentals=0
        ),
    )(*[pltpu.with_memory_space_constraint(w, pltpu.HBM) for w in weights])


def route_kernel(experts, routing_hbm, weight_hbm, out_ref, routing_ref, weight_ref, sems):
    pairs = ((routing_hbm, routing_ref), (weight_hbm, weight_ref))
    copies = [pltpu.make_async_copy(source, target, sems.at[place]) for place, (source, target) in enumerate(pairs)]
    for copy in copies:
        copy.start()
    for copy in copies:
        copy.wait()
    rows = out_ref.shape[0]
    lane = lax.broadcasted_iota(jnp.int32, (rows, LANES), 1).astype(jnp.float32)
    diagonal = lax.broadcasted_iota(jnp.int32, (rows, rows), 0) == lax.broadcasted_iota(jnp.int32, (rows, rows), 1)

    def upright(line):
        return jnp.sum(jnp.where(diagonal, line.astype(jnp.float32), 0.0), axis=1, keepdims=True)

    total = jnp.zeros((rows, LANES), jnp.float32)
    for step in range(routing_ref.shape[1]):
        for k in range(routing_ref.shape[2]):
            column = upright(routing_ref[0, step, k:k + 1, :]) + step * experts
            total += jnp.where(lane == column, upright(weight_ref[0, step, k:k + 1, :]), 0.0)
    out_ref[...] = total.astype(jnp.bfloat16)


def route(experts, routing, weight):
    args = [jnp.swapaxes(routing, 2, 3), jnp.swapaxes(weight, 2, 3)]
    return call(
        functools.partial(route_kernel, experts), [(routing.shape[2], LANES)],
        *[pltpu.with_memory_space_constraint(x, pltpu.HBM) for x in args],
        in_specs=[pl.BlockSpec(memory_space=pltpu.HBM)] * 2,
        scratch_shapes=[pltpu.VMEM(x.shape, x.dtype) for x in args] + [pltpu.SemaphoreType.DMA((2,))],
    )[0]


def join_kernel(*refs):
    *parts, out_ref = refs
    for span in spans(out_ref.shape[1]):
        rows = [part[:, span].astype(jnp.float32) for part in parts]
        out_ref[:, span] = jnp.concatenate(rows, axis=0).astype(jnp.bfloat16)


def add_kernel(*refs):
    *parts, out_ref = refs
    for span in spans(out_ref.shape[1]):
        out_ref[:, span] = sum(part[:, span].astype(jnp.float32) for part in parts).astype(jnp.bfloat16)


def split_kernel(count, *refs):
    parts, outs = refs[:-count], refs[-count:]
    rows = outs[0].shape[0]
    for span in spans(outs[0].shape[1]):
        total = sum(part[:, span].astype(jnp.float32) for part in parts)
        for place, out_ref in enumerate(outs):
            out_ref[:, span] = total[place * rows:(place + 1) * rows].astype(jnp.bfloat16)


def normalise(raw_ref, gain_ref, out_ref):
    rows, dim = raw_ref.shape
    square = jnp.zeros((rows, LANES), jnp.float32)
    for start in range(0, dim, LANES):
        piece = raw_ref[:, start:start + LANES].astype(jnp.float32)
        square += piece * piece
    inv = lax.rsqrt(jnp.sum(square, axis=1, keepdims=True) / dim + 1e-06)
    for span in spans(dim):
        scaled = raw_ref[:, span].astype(jnp.float32) * inv * gain_ref[:, span]
        out_ref[:, span] = scaled.astype(jnp.bfloat16)


def first_kernel(own_ref, far_ref, own_tail_ref, far_tail_ref, gain_ref, out_ref, raw_ref):
    dim = raw_ref.shape[1]
    for span in spans(dim):
        rows = [ref[:, span].astype(jnp.float32) for ref in (own_ref, far_ref)]
        raw_ref[:, span] = jnp.concatenate(rows, axis=0).astype(jnp.bfloat16)
    tails = [ref[...].astype(jnp.float32) for ref in (own_tail_ref, far_tail_ref)]
    out_ref[:, dim:] = jnp.concatenate(tails, axis=0).astype(jnp.bfloat16)
    normalise(raw_ref, gain_ref, out_ref)


def meet_kernel(rest_ref, near_ref, far_ref, gain_ref, out_ref, own_ref, raw_ref):
    half = own_ref.shape[0]
    for span in spans(out_ref.shape[1]):
        far = far_ref[:, span].astype(jnp.float32)
        total = rest_ref[:, span].astype(jnp.float32) + near_ref[:, span].astype(jnp.float32)
        total = (total + jnp.concatenate([far[half:], far[:half]], axis=0)).astype(jnp.bfloat16)
        raw_ref[:, span] = total
        own_ref[:, span] = total[:half]
    normalise(raw_ref, gain_ref, out_ref)


def mlp_kernel(step_no, *refs):
    x_refs, refs = refs[:8], refs[8:]
    if step_no > 0:
        tail_ref, refs = refs[0], refs[1:]
    (gate_ref, up_ref, down_ref), outs, refs = refs[:3], refs[3:11], refs[11:]
    part = outs[0].shape[0]
    dim, hidden = gate_ref.shape[1:]
    experts = lax.axis_size("expert") // GROUP
    column = step_no * experts + lax.axis_index("expert") // GROUP
    lane = lax.broadcasted_iota(jnp.int32, (part, LANES), 1)
    weights = []
    for place, ref in enumerate(x_refs):
        band = slice(place * part, (place + 1) * part)
        if step_no == 0:
            tail = ref[:, dim:]
            refs[0][band, :] = tail
        else:
            tail = tail_ref[band, :]
        chosen = jnp.where(lane == column, tail.astype(jnp.float32), 0.0)
        weights.append(jnp.sum(chosen, axis=1, keepdims=True))
    gated = jnp.zeros((8 * part, hidden), jnp.float32)
    up_part = jnp.zeros((8 * part, hidden), jnp.float32)
    for span in spans(dim):
        rows = jnp.concatenate([ref[:, span] for ref in x_refs], axis=0)
        gated += jnp.dot(rows, gate_ref[0, span, :], preferred_element_type=jnp.float32)
        up_part += jnp.dot(rows, up_ref[0, span, :], preferred_element_type=jnp.float32)
    inner = (gated / (1.0 + jnp.exp(-gated)) * up_part).astype(jnp.bfloat16)
    for span in spans(dim):
        terms = jnp.dot(inner, down_ref[0, :, span], preferred_element_type=jnp.float32)
        for place, out_ref in enumerate(outs):
            weight = weights[place]
            mine = terms[place * part:(place + 1) * part]
            out_ref[:, span] = jnp.where(weight > 0.0, weight * mine, 0.0).astype(jnp.bfloat16)


def mlp(step_no, xs, tail, gate, up, down):
    dim, hidden = gate.shape[1:]
    part = xs[0].shape[0]
    gate, up, down = [pltpu.with_memory_space_constraint(w, pltpu.VMEM) for w in (gate, up, down)]
    first = step_no == 0
    args = list(xs) + ([] if first else [tail]) + [gate, up, down]
    result = call(
        functools.partial(mlp_kernel, step_no), [(part, dim)] * 8 + [(8 * part, LANES)] * first, *args,
        cost_estimate=pl.CostEstimate(
            flops=48 * part * dim * hidden, bytes_accessed=6 * dim * hidden, transcendentals=0
        ),
    )
    return result[:8], result[8] if first else tail


def add(*parts):
    rows = parts[0].shape[0]
    dim = parts[-1].shape[1]
    return call(add_kernel, [(rows, dim)], *parts)[0]


def split(*parts):
    rows, dim = parts[0].shape
    return call(functools.partial(split_kernel, 2), [(rows // 2, dim)] * 2, *parts)


def join(*parts):
    return call(join_kernel, [(sum(part.shape[0] for part in parts), parts[0].shape[1])], *parts)[0]


def on_device(states, routing, route_weight, norm_gain, gate_proj, up_proj, down_proj):
    owners = lax.axis_size("expert")
    row_dev, dim = states.shape[1:]
    passes_count = routing.shape[1]
    top, *middle = upper_flips(owners)

    own, tail = states[0], None
    other = exchange(own, top, 0)
    lanes = route(owners // GROUP, routing, route_weight)
    other_lanes = exchange(lanes, top, 0)
    (gate,) = load(gate_proj)
    other, other_lanes, gate = lax.optimization_barrier((other, other_lanes, gate))
    pair, raw = call(
        first_kernel, [(2 * row_dev, dim + LANES), (2 * row_dev, dim)], own, other, lanes, other_lanes, norm_gain
    )
    pair, up_hbm, down_hbm = lax.optimization_barrier((pair, up_proj, down_proj))
    up, down = load(up_hbm, down_hbm)
    for step_no in range(passes_count):
        rows_a = pair
        for flips in middle:
            rows_a = join(rows_a, exchange(rows_a, flips, 0))
        mine = [rows_a] + [exchange(rows_a, flips, 0) for flips in SQUARE]
        near = rows_a
        if step_no == 0:
            near, up, down = lax.optimization_barrier((near, up, down))
        fars = [exchange(rows, CORE, 0) for rows in [near] + mine[1:]]
        outs, tail = mlp(step_no, mine + fars, tail, gate, up, down)

        kept, sent = outs[:4], [exchange(rows, CORE, 0) for rows in outs[4:]]
        parts = [kept[0], sent[0]]
        for place in (3, 2, 1):
            parts.append(exchange(add(kept[place], sent[place]), SQUARE[place - 1], 0))
        for flips in middle[::-1]:
            low, high = split(*parts)
            parts = [low, exchange(high, flips, 0)]
        if step_no < passes_count - 1:
            total = add(*parts)
            rest = exchange(raw, STAY, 1)
            more = step_no < passes_count - 2
            pair, own, *raws = call(
                meet_kernel, [(2 * row_dev, dim), (row_dev, dim)] + [(2 * row_dev, dim)] * more,
                rest, exchange(total, STAY, 1), exchange(total, top, 1), norm_gain,
                scratch_shapes=[] if more else [pltpu.VMEM((2 * row_dev, dim), jnp.bfloat16)],
            )
            raw = raws[0] if more else None
        else:
            low, high = split(*parts)
            rest = exchange(own, STAY, 1)
            own = add(rest, exchange(high, top, 1), exchange(low, STAY, 1))
    return own[None]


def solution(mesh):
    return jax.shard_map(
        on_device,
        mesh=mesh,
        in_specs=(
            P("segment", "expert", None),
            P("segment", None, "expert", None),
            P("segment", None, "expert", None),
            P("segment", None),
            P("segment", None, "expert"),
            P("segment", None, "expert"),
            P("segment", "expert", None),
        ),
        out_specs=P("segment", "expert", None),
        check_vma=False,
    )
```

```python
import functools

import jax
import jax.numpy as jnp
from jax import lax
from jax.experimental import pallas as pl
from jax.experimental.pallas import tpu as pltpu
from jax.sharding import PartitionSpec as P

GROUP = 4
LANES = 128
CHUNK = 1024
VMEM_LIMIT = 16 * 1024 * 1024
VMEM = pl.BlockSpec(memory_space=pltpu.VMEM)


def exchange(value, flips, hop):
    segments, owners = lax.axis_size("segment"), lax.axis_size("expert")
    if flips == (0, 0) and hop % segments == 0:
        return value
    pairs = []
    for seg in range(segments):
        for own in range(owners):
            target = (seg + hop) % segments * owners + (own ^ flips[own % 2])
            pairs.append((seg * owners + own, target))
    return lax.ppermute(value, ("segment", "expert"), pairs)


def upper_flips(owners):
    return [(1 << place,) * 2 for place in range(owners.bit_length() - 2, 2, -1)]


CORE = (1, 1)
SQUARE = ((4, 2), (2, 4), (6, 6))
STAY = (0, 0)


def spans(dim):
    return [slice(start, min(start + CHUNK, dim)) for start in range(0, dim, CHUNK)]


def call(kernel, outs, *args, **more):
    return pl.pallas_call(
        kernel,
        out_shape=[jax.ShapeDtypeStruct(shape, jnp.bfloat16) for shape in outs],
        in_specs=more.pop("in_specs", [VMEM] * len(args)),
        out_specs=[VMEM] * len(outs),
        compiler_params=pltpu.CompilerParams(vmem_limit_bytes=VMEM_LIMIT),
        **more,
    )(*args)


def load_kernel(count, *refs):
    out_ref, sems = refs[count:]
    copies, start = [], 0
    for place, ref in enumerate(refs[:count]):
        columns = pl.ds(start, ref.shape[2])
        copies.append(pltpu.make_async_copy(ref, out_ref.at[:, :, columns], sems.at[place]))
        start += ref.shape[2]
    for copy in copies:
        copy.start()
    for copy in copies:
        copy.wait()


def load(*weights):
    count = len(weights)
    columns = sum(w.shape[2] for w in weights)
    return pl.pallas_call(
        functools.partial(load_kernel, count),
        out_shape=pltpu.VMEM(weights[0].shape[:2] + (columns,), weights[0].dtype),
        in_specs=[pl.BlockSpec(memory_space=pltpu.HBM)] * count,
        out_specs=VMEM,
        scratch_shapes=[pltpu.SemaphoreType.DMA((count,))],
        compiler_params=pltpu.CompilerParams(vmem_limit_bytes=VMEM_LIMIT),
        cost_estimate=pl.CostEstimate(
            flops=0, bytes_accessed=sum(2 * w.size for w in weights), transcendentals=0
        ),
    )(*[pltpu.with_memory_space_constraint(w, pltpu.HBM) for w in weights])


def prepare_kernel(experts, states_hbm, routing_hbm, weight_hbm, out_ref, states_ref, routing_ref, weight_ref, sems):
    pairs = ((routing_hbm, routing_ref), (weight_hbm, weight_ref), (states_hbm, states_ref))
    copies = [pltpu.make_async_copy(source, target, sems.at[place]) for place, (source, target) in enumerate(pairs)]
    for copy in copies:
        copy.start()
    for copy in copies:
        copy.wait()
    rows, dim = states_ref.shape[1:]
    for span in spans(dim):
        out_ref[:, span] = states_ref[0, :, span]
    lane = lax.broadcasted_iota(jnp.int32, (rows, LANES), 1).astype(jnp.float32)
    diagonal = lax.broadcasted_iota(jnp.int32, (rows, rows), 0) == lax.broadcasted_iota(jnp.int32, (rows, rows), 1)

    def upright(line):
        return jnp.sum(jnp.where(diagonal, line.astype(jnp.float32), 0.0), axis=1, keepdims=True)

    total = jnp.zeros((rows, LANES), jnp.float32)
    for step in range(routing_ref.shape[1]):
        for k in range(routing_ref.shape[2]):
            column = upright(routing_ref[0, step, k:k + 1, :]) + step * experts
            total += jnp.where(lane == column, upright(weight_ref[0, step, k:k + 1, :]), 0.0)
    out_ref[:, dim:] = total.astype(jnp.bfloat16)


def prepare(experts, states, routing, weight):
    args = [states, jnp.swapaxes(routing, 2, 3), jnp.swapaxes(weight, 2, 3)]
    rows, dim = states.shape[1:]
    (block,) = call(
        functools.partial(prepare_kernel, experts), [(rows, dim + LANES)],
        *[pltpu.with_memory_space_constraint(x, pltpu.HBM) for x in args],
        in_specs=[pl.BlockSpec(memory_space=pltpu.HBM)] * 3,
        scratch_shapes=[pltpu.VMEM(x.shape, x.dtype) for x in args] + [pltpu.SemaphoreType.DMA((3,))],
    )
    return block


def join_kernel(*refs):
    *parts, out_ref = refs
    for span in spans(out_ref.shape[1]):
        rows = [part[:, span].astype(jnp.float32) for part in parts]
        out_ref[:, span] = jnp.concatenate(rows, axis=0).astype(jnp.bfloat16)


def add_kernel(*refs):
    *parts, out_ref = refs
    for span in spans(out_ref.shape[1]):
        out_ref[:, span] = sum(part[:, span].astype(jnp.float32) for part in parts).astype(jnp.bfloat16)


def split_kernel(count, *refs):
    parts, outs = refs[:-count], refs[-count:]
    rows = outs[0].shape[0]
    for span in spans(outs[0].shape[1]):
        total = sum(part[:, span].astype(jnp.float32) for part in parts)
        for place, out_ref in enumerate(outs):
            out_ref[:, span] = total[place * rows:(place + 1) * rows].astype(jnp.bfloat16)


def normalise(raw_ref, gain_ref, out_ref):
    rows, dim = raw_ref.shape
    square = jnp.zeros((rows, LANES), jnp.float32)
    for start in range(0, dim, LANES):
        piece = raw_ref[:, start:start + LANES].astype(jnp.float32)
        square += piece * piece
    inv = lax.rsqrt(jnp.sum(square, axis=1, keepdims=True) / dim + 1e-06)
    for span in spans(dim):
        scaled = raw_ref[:, span].astype(jnp.float32) * inv * gain_ref[:, span]
        out_ref[:, span] = scaled.astype(jnp.bfloat16)


def first_kernel(own_ref, far_ref, gain_ref, out_ref, raw_ref):
    dim = raw_ref.shape[1]
    for span in spans(dim):
        rows = [ref[:, span].astype(jnp.float32) for ref in (own_ref, far_ref)]
        raw_ref[:, span] = jnp.concatenate(rows, axis=0).astype(jnp.bfloat16)
    tails = [ref[:, dim:].astype(jnp.float32) for ref in (own_ref, far_ref)]
    out_ref[:, dim:] = jnp.concatenate(tails, axis=0).astype(jnp.bfloat16)
    normalise(raw_ref, gain_ref, out_ref)


def meet_kernel(rest_ref, near_ref, far_ref, gain_ref, out_ref, own_ref, raw_ref):
    half = own_ref.shape[0]
    for span in spans(out_ref.shape[1]):
        far = far_ref[:, span].astype(jnp.float32)
        total = rest_ref[:, span].astype(jnp.float32) + near_ref[:, span].astype(jnp.float32)
        total = (total + jnp.concatenate([far[half:], far[:half]], axis=0)).astype(jnp.bfloat16)
        raw_ref[:, span] = total
        own_ref[:, span] = total[:half]
    normalise(raw_ref, gain_ref, out_ref)


def mlp_kernel(step_no, *refs):
    x_refs, refs = refs[:8], refs[8:]
    if step_no > 0:
        tail_ref, refs = refs[0], refs[1:]
    (wide_ref, down_ref), outs, refs = refs[:2], refs[2:10], refs[10:]
    part = outs[0].shape[0]
    hidden, dim = down_ref.shape[1:]
    experts = lax.axis_size("expert") // GROUP
    column = step_no * experts + lax.axis_index("expert") // GROUP
    lane = lax.broadcasted_iota(jnp.int32, (part, LANES), 1)
    weights = []
    for place, ref in enumerate(x_refs):
        band = slice(place * part, (place + 1) * part)
        if step_no == 0:
            tail = ref[:, dim:]
            refs[0][band, :] = tail
        else:
            tail = tail_ref[band, :]
        chosen = jnp.where(lane == column, tail.astype(jnp.float32), 0.0)
        weights.append(jnp.sum(chosen, axis=1, keepdims=True))
    both = jnp.zeros((8 * part, 2 * hidden), jnp.float32)
    for span in spans(dim):
        rows = jnp.concatenate([ref[:, span] for ref in x_refs], axis=0)
        both += jnp.dot(rows, wide_ref[0, span, :], preferred_element_type=jnp.float32)
    gated, up_part = both[:, :hidden], both[:, hidden:]
    inner = (gated / (1.0 + jnp.exp(-gated)) * up_part).astype(jnp.bfloat16)
    for span in spans(dim):
        terms = jnp.dot(inner, down_ref[0, :, span], preferred_element_type=jnp.float32)
        for place, out_ref in enumerate(outs):
            weight = weights[place]
            mine = terms[place * part:(place + 1) * part]
            out_ref[:, span] = jnp.where(weight > 0.0, weight * mine, 0.0).astype(jnp.bfloat16)


def mlp(step_no, xs, tail, wide, down):
    hidden, dim = down.shape[1:]
    part = xs[0].shape[0]
    wide, down = [pltpu.with_memory_space_constraint(w, pltpu.VMEM) for w in (wide, down)]
    first = step_no == 0
    args = list(xs) + ([] if first else [tail]) + [wide, down]
    result = call(
        functools.partial(mlp_kernel, step_no), [(part, dim)] * 8 + [(8 * part, LANES)] * first, *args,
        cost_estimate=pl.CostEstimate(
            flops=48 * part * dim * hidden, bytes_accessed=6 * dim * hidden, transcendentals=0
        ),
    )
    return result[:8], result[8] if first else tail


def add(*parts):
    rows = parts[0].shape[0]
    dim = parts[-1].shape[1]
    return call(add_kernel, [(rows, dim)], *parts)[0]


def split(*parts):
    rows, dim = parts[0].shape
    return call(functools.partial(split_kernel, 2), [(rows // 2, dim)] * 2, *parts)


def join(*parts):
    return call(join_kernel, [(sum(part.shape[0] for part in parts), parts[0].shape[1])], *parts)[0]


def on_device(states, routing, route_weight, norm_gain, gate_proj, up_proj, down_proj):
    owners = lax.axis_size("expert")
    row_dev, dim = states.shape[1:]
    passes_count = routing.shape[1]
    top, *middle = upper_flips(owners)

    wide = load(gate_proj, up_proj)
    block = prepare(owners // GROUP, states, routing, route_weight)
    other = exchange(block, top, 0)
    other, wide = lax.optimization_barrier((other, wide))
    pair, raw = call(first_kernel, [(2 * row_dev, dim + LANES), (2 * row_dev, dim)], block, other, norm_gain)
    pair, down_hbm = lax.optimization_barrier((pair, down_proj))
    down = load(down_hbm)
    own, tail = states[0], None
    for step_no in range(passes_count):
        rows_a = pair
        for flips in middle:
            rows_a = join(rows_a, exchange(rows_a, flips, 0))
        mine = [rows_a] + [exchange(rows_a, flips, 0) for flips in SQUARE]
        near = rows_a
        if step_no == 0:
            near, down = lax.optimization_barrier((near, down))
        fars = [exchange(rows, CORE, 0) for rows in [near] + mine[1:]]
        outs, tail = mlp(step_no, mine + fars, tail, wide, down)

        kept, sent = outs[:4], [exchange(rows, CORE, 0) for rows in outs[4:]]
        parts = [kept[0], sent[0]]
        for place in (3, 2, 1):
            parts.append(exchange(add(kept[place], sent[place]), SQUARE[place - 1], 0))
        for flips in middle[::-1]:
            low, high = split(*parts)
            parts = [low, exchange(high, flips, 0)]
        if step_no < passes_count - 1:
            total = add(*parts)
            rest = exchange(raw, STAY, 1)
            more = step_no < passes_count - 2
            pair, own, *raws = call(
                meet_kernel, [(2 * row_dev, dim), (row_dev, dim)] + [(2 * row_dev, dim)] * more,
                rest, exchange(total, STAY, 1), exchange(total, top, 1), norm_gain,
                scratch_shapes=[] if more else [pltpu.VMEM((2 * row_dev, dim), jnp.bfloat16)],
            )
            raw = raws[0] if more else None
        else:
            low, high = split(*parts)
            rest = exchange(own, STAY, 1)
            own = add(rest, exchange(high, top, 1), exchange(low, STAY, 1))
    return own[None]


def solution(mesh):
    return jax.shard_map(
        on_device,
        mesh=mesh,
        in_specs=(
            P("segment", "expert", None),
            P("segment", None, "expert", None),
            P("segment", None, "expert", None),
            P("segment", None),
            P("segment", None, "expert"),
            P("segment", None, "expert"),
            P("segment", "expert", None),
        ),
        out_specs=P("segment", "expert", None),
        check_vma=False,
    )
```

```python
import functools

import jax
import jax.numpy as jnp
from jax import lax
from jax.experimental import pallas as pl
from jax.experimental.pallas import tpu as pltpu
from jax.sharding import PartitionSpec as P

GROUP = 4
LANES = 128
CHUNK = 1024
VMEM_LIMIT = 16 * 1024 * 1024
VMEM = pl.BlockSpec(memory_space=pltpu.VMEM)


def exchange(value, flips, hop):
    segments, owners = lax.axis_size("segment"), lax.axis_size("expert")
    if flips == (0, 0) and hop % segments == 0:
        return value
    pairs = []
    for seg in range(segments):
        for own in range(owners):
            target = (seg + hop) % segments * owners + (own ^ flips[own % 2])
            pairs.append((seg * owners + own, target))
    return lax.ppermute(value, ("segment", "expert"), pairs)


def upper_flips(owners):
    return [(1 << place,) * 2 for place in range(owners.bit_length() - 2, 2, -1)]


CORE = (1, 1)
SQUARE = ((2, 2), (4, 4), (6, 6))
STAY = (0, 0)


def spans(dim):
    return [slice(start, min(start + CHUNK, dim)) for start in range(0, dim, CHUNK)]


def call(kernel, outs, *args, **more):
    return pl.pallas_call(
        kernel,
        out_shape=[jax.ShapeDtypeStruct(shape, jnp.bfloat16) for shape in outs],
        in_specs=more.pop("in_specs", [VMEM] * len(args)),
        out_specs=[VMEM] * len(outs),
        compiler_params=pltpu.CompilerParams(vmem_limit_bytes=VMEM_LIMIT),
        **more,
    )(*args)


def load_kernel(count, *refs):
    sems = refs[-1]
    copies = [pltpu.make_async_copy(refs[place], refs[count + place], sems.at[place]) for place in range(count)]
    for copy in copies:
        copy.start()
    for copy in copies:
        copy.wait()


def load(*weights):
    count = len(weights)
    return pl.pallas_call(
        functools.partial(load_kernel, count),
        out_shape=[pltpu.VMEM(w.shape, w.dtype) for w in weights],
        in_specs=[pl.BlockSpec(memory_space=pltpu.HBM)] * count,
        out_specs=[VMEM] * count,
        scratch_shapes=[pltpu.SemaphoreType.DMA((count,))],
        compiler_params=pltpu.CompilerParams(vmem_limit_bytes=VMEM_LIMIT),
        cost_estimate=pl.CostEstimate(
            flops=0, bytes_accessed=sum(2 * w.size for w in weights), transcendentals=0
        ),
    )(*[pltpu.with_memory_space_constraint(w, pltpu.HBM) for w in weights])


def prepare_kernel(experts, states_hbm, routing_hbm, weight_hbm, out_ref, states_ref, routing_ref, weight_ref, sems):
    pairs = ((routing_hbm, routing_ref), (weight_hbm, weight_ref), (states_hbm, states_ref))
    copies = [pltpu.make_async_copy(source, target, sems.at[place]) for place, (source, target) in enumerate(pairs)]
    for copy in copies:
        copy.start()
    for copy in copies:
        copy.wait()
    rows, dim = states_ref.shape[1:]
    for span in spans(dim):
        out_ref[:, span] = states_ref[0, :, span]
    lane = lax.broadcasted_iota(jnp.int32, (rows, LANES), 1).astype(jnp.float32)
    diagonal = lax.broadcasted_iota(jnp.int32, (rows, rows), 0) == lax.broadcasted_iota(jnp.int32, (rows, rows), 1)

    def upright(line):
        return jnp.sum(jnp.where(diagonal, line.astype(jnp.float32), 0.0), axis=1, keepdims=True)

    total = jnp.zeros((rows, LANES), jnp.float32)
    for step in range(routing_ref.shape[1]):
        for k in range(routing_ref.shape[2]):
            column = upright(routing_ref[0, step, k:k + 1, :]) + step * experts
            total += jnp.where(lane == column, upright(weight_ref[0, step, k:k + 1, :]), 0.0)
    out_ref[:, dim:] = total.astype(jnp.bfloat16)


def prepare(experts, states, routing, weight):
    args = [states, jnp.swapaxes(routing, 2, 3), jnp.swapaxes(weight, 2, 3)]
    rows, dim = states.shape[1:]
    (block,) = call(
        functools.partial(prepare_kernel, experts), [(rows, dim + LANES)],
        *[pltpu.with_memory_space_constraint(x, pltpu.HBM) for x in args],
        in_specs=[pl.BlockSpec(memory_space=pltpu.HBM)] * 3,
        scratch_shapes=[pltpu.VMEM(x.shape, x.dtype) for x in args] + [pltpu.SemaphoreType.DMA((3,))],
    )
    return block


def join_kernel(*refs):
    *parts, out_ref = refs
    for span in spans(out_ref.shape[1]):
        rows = [part[:, span].astype(jnp.float32) for part in parts]
        out_ref[:, span] = jnp.concatenate(rows, axis=0).astype(jnp.bfloat16)


def add_kernel(*refs):
    *parts, out_ref = refs
    for span in spans(out_ref.shape[1]):
        out_ref[:, span] = sum(part[:, span].astype(jnp.float32) for part in parts).astype(jnp.bfloat16)


def split_kernel(count, *refs):
    parts, outs = refs[:-count], refs[-count:]
    rows = outs[0].shape[0]
    for span in spans(outs[0].shape[1]):
        total = sum(part[:, span].astype(jnp.float32) for part in parts)
        for place, out_ref in enumerate(outs):
            out_ref[:, span] = total[place * rows:(place + 1) * rows].astype(jnp.bfloat16)


def normalise(raw_ref, gain_ref, out_ref):
    rows, dim = raw_ref.shape
    square = jnp.zeros((rows, LANES), jnp.float32)
    for start in range(0, dim, LANES):
        piece = raw_ref[:, start:start + LANES].astype(jnp.float32)
        square += piece * piece
    inv = lax.rsqrt(jnp.sum(square, axis=1, keepdims=True) / dim + 1e-06)
    for span in spans(dim):
        scaled = raw_ref[:, span].astype(jnp.float32) * inv * gain_ref[:, span]
        out_ref[:, span] = scaled.astype(jnp.bfloat16)


def first_kernel(own_ref, far_ref, gain_ref, out_ref, raw_ref):
    dim = raw_ref.shape[1]
    for span in spans(dim):
        rows = [ref[:, span].astype(jnp.float32) for ref in (own_ref, far_ref)]
        raw_ref[:, span] = jnp.concatenate(rows, axis=0).astype(jnp.bfloat16)
    tails = [ref[:, dim:].astype(jnp.float32) for ref in (own_ref, far_ref)]
    out_ref[:, dim:] = jnp.concatenate(tails, axis=0).astype(jnp.bfloat16)
    normalise(raw_ref, gain_ref, out_ref)


def meet_kernel(rest_ref, near_ref, far_ref, gain_ref, out_ref, own_ref, raw_ref):
    half = own_ref.shape[0]
    for span in spans(out_ref.shape[1]):
        far = far_ref[:, span].astype(jnp.float32)
        total = rest_ref[:, span].astype(jnp.float32) + near_ref[:, span].astype(jnp.float32)
        total = (total + jnp.concatenate([far[half:], far[:half]], axis=0)).astype(jnp.bfloat16)
        raw_ref[:, span] = total
        own_ref[:, span] = total[:half]
    normalise(raw_ref, gain_ref, out_ref)


def mlp_kernel(step_no, *refs):
    x_refs, refs = refs[:8], refs[8:]
    if step_no > 0:
        tail_ref, refs = refs[0], refs[1:]
    (gate_ref, up_ref, down_ref), outs, refs = refs[:3], refs[3:11], refs[11:]
    part = outs[0].shape[0]
    dim, hidden = gate_ref.shape[1:]
    experts = lax.axis_size("expert") // GROUP
    column = step_no * experts + lax.axis_index("expert") // GROUP
    lane = lax.broadcasted_iota(jnp.int32, (part, LANES), 1)
    weights = []
    for place, ref in enumerate(x_refs):
        band = slice(place * part, (place + 1) * part)
        if step_no == 0:
            tail = ref[:, dim:]
            refs[0][band, :] = tail
        else:
            tail = tail_ref[band, :]
        chosen = jnp.where(lane == column, tail.astype(jnp.float32), 0.0)
        weights.append(jnp.sum(chosen, axis=1, keepdims=True))
    gated = jnp.zeros((8 * part, hidden), jnp.float32)
    up_part = jnp.zeros((8 * part, hidden), jnp.float32)
    for span in spans(dim):
        rows = jnp.concatenate([ref[:, span] for ref in x_refs], axis=0)
        gated += jnp.dot(rows, gate_ref[0, span, :], preferred_element_type=jnp.float32)
        up_part += jnp.dot(rows, up_ref[0, span, :], preferred_element_type=jnp.float32)
    inner = (gated / (1.0 + jnp.exp(-gated)) * up_part).astype(jnp.bfloat16)
    for span in spans(dim):
        terms = jnp.dot(inner, down_ref[0, :, span], preferred_element_type=jnp.float32)
        for place, out_ref in enumerate(outs):
            weight = weights[place]
            mine = terms[place * part:(place + 1) * part]
            out_ref[:, span] = jnp.where(weight > 0.0, weight * mine, 0.0).astype(jnp.bfloat16)


def mlp(step_no, xs, tail, gate, up, down):
    dim, hidden = gate.shape[1:]
    part = xs[0].shape[0]
    gate, up, down = [pltpu.with_memory_space_constraint(w, pltpu.VMEM) for w in (gate, up, down)]
    first = step_no == 0
    args = list(xs) + ([] if first else [tail]) + [gate, up, down]
    result = call(
        functools.partial(mlp_kernel, step_no), [(part, dim)] * 8 + [(8 * part, LANES)] * first, *args,
        cost_estimate=pl.CostEstimate(
            flops=48 * part * dim * hidden, bytes_accessed=6 * dim * hidden, transcendentals=0
        ),
    )
    return result[:8], result[8] if first else tail


def add(*parts):
    rows = parts[0].shape[0]
    dim = parts[-1].shape[1]
    return call(add_kernel, [(rows, dim)], *parts)[0]


def split(*parts):
    rows, dim = parts[0].shape
    return call(functools.partial(split_kernel, 2), [(rows // 2, dim)] * 2, *parts)


def join(*parts):
    return call(join_kernel, [(sum(part.shape[0] for part in parts), parts[0].shape[1])], *parts)[0]


def on_device(states, routing, route_weight, norm_gain, gate_proj, up_proj, down_proj):
    owners = lax.axis_size("expert")
    row_dev, dim = states.shape[1:]
    passes_count = routing.shape[1]
    top, *middle = upper_flips(owners)

    gate, up = load(gate_proj, up_proj)
    block = prepare(owners // GROUP, states, routing, route_weight)
    other = exchange(block, top, 0)
    other, gate, up = lax.optimization_barrier((other, gate, up))
    pair, raw = call(first_kernel, [(2 * row_dev, dim + LANES), (2 * row_dev, dim)], block, other, norm_gain)
    pair, down_hbm = lax.optimization_barrier((pair, down_proj))
    (down,) = load(down_hbm)
    own, tail = states[0], None
    for step_no in range(passes_count):
        rows_a = pair
        for flips in middle:
            rows_a = join(rows_a, exchange(rows_a, flips, 0))
        mine = [rows_a] + [exchange(rows_a, flips, 0) for flips in SQUARE]
        near = rows_a
        if step_no == 0:
            near, down = lax.optimization_barrier((near, down))
        fars = [exchange(rows, CORE, 0) for rows in [near] + mine[1:]]
        outs, tail = mlp(step_no, mine + fars, tail, gate, up, down)

        kept, sent = outs[:4], [exchange(rows, CORE, 0) for rows in outs[4:]]
        parts = [kept[0], sent[0]]
        for place in (3, 2, 1):
            parts.append(exchange(add(kept[place], sent[place]), SQUARE[place - 1], 0))
        for flips in middle[::-1]:
            low, high = split(*parts)
            parts = [low, exchange(high, flips, 0)]
        if step_no < passes_count - 1:
            total = add(*parts)
            rest = exchange(raw, STAY, 1)
            more = step_no < passes_count - 2
            pair, own, *raws = call(
                meet_kernel, [(2 * row_dev, dim), (row_dev, dim)] + [(2 * row_dev, dim)] * more,
                rest, exchange(total, STAY, 1), exchange(total, top, 1), norm_gain,
                scratch_shapes=[] if more else [pltpu.VMEM((2 * row_dev, dim), jnp.bfloat16)],
            )
            raw = raws[0] if more else None
        else:
            low, high = split(*parts)
            rest = exchange(own, STAY, 1)
            own = add(rest, exchange(high, top, 1), exchange(low, STAY, 1))
    return own[None]


def solution(mesh):
    return jax.shard_map(
        on_device,
        mesh=mesh,
        in_specs=(
            P("segment", "expert", None),
            P("segment", None, "expert", None),
            P("segment", None, "expert", None),
            P("segment", None),
            P("segment", None, "expert"),
            P("segment", None, "expert"),
            P("segment", "expert", None),
        ),
        out_specs=P("segment", "expert", None),
        check_vma=False,
    )
```

```python
import functools

import jax
import jax.numpy as jnp
from jax import lax
from jax.experimental import pallas as pl
from jax.experimental.pallas import tpu as pltpu
from jax.sharding import PartitionSpec as P

GROUP = 4
LANES = 128
CHUNK = 1024
VMEM_LIMIT = 16 * 1024 * 1024
VMEM = pl.BlockSpec(memory_space=pltpu.VMEM)


def exchange(value, flips, hop):
    segments, owners = lax.axis_size("segment"), lax.axis_size("expert")
    if flips == (0, 0) and hop % segments == 0:
        return value
    pairs = []
    for seg in range(segments):
        for own in range(owners):
            target = (seg + hop) % segments * owners + (own ^ flips[own % 2])
            pairs.append((seg * owners + own, target))
    return lax.ppermute(value, ("segment", "expert"), pairs)


def upper_flips(owners):
    return [(1 << place,) * 2 for place in range(owners.bit_length() - 2, 2, -1)]


CORE = (1, 1)
SQUARE = ((4, 4), (2, 2), (6, 6))
STAY = (0, 0)


def spans(dim):
    return [slice(start, min(start + CHUNK, dim)) for start in range(0, dim, CHUNK)]


def call(kernel, outs, *args, **more):
    return pl.pallas_call(
        kernel,
        out_shape=[jax.ShapeDtypeStruct(shape, jnp.bfloat16) for shape in outs],
        in_specs=more.pop("in_specs", [VMEM] * len(args)),
        out_specs=[VMEM] * len(outs),
        compiler_params=pltpu.CompilerParams(vmem_limit_bytes=VMEM_LIMIT),
        **more,
    )(*args)


def load_kernel(count, *refs):
    sems = refs[-1]
    copies = [pltpu.make_async_copy(refs[place], refs[count + place], sems.at[place]) for place in range(count)]
    for copy in copies:
        copy.start()
    for copy in copies:
        copy.wait()


def load(*weights):
    count = len(weights)
    return pl.pallas_call(
        functools.partial(load_kernel, count),
        out_shape=[pltpu.VMEM(w.shape, w.dtype) for w in weights],
        in_specs=[pl.BlockSpec(memory_space=pltpu.HBM)] * count,
        out_specs=[VMEM] * count,
        scratch_shapes=[pltpu.SemaphoreType.DMA((count,))],
        compiler_params=pltpu.CompilerParams(vmem_limit_bytes=VMEM_LIMIT),
        cost_estimate=pl.CostEstimate(
            flops=0, bytes_accessed=sum(2 * w.size for w in weights), transcendentals=0
        ),
    )(*[pltpu.with_memory_space_constraint(w, pltpu.HBM) for w in weights])


def prepare_kernel(experts, states_hbm, routing_hbm, weight_hbm, out_ref, states_ref, routing_ref, weight_ref, sems):
    pairs = ((routing_hbm, routing_ref), (weight_hbm, weight_ref), (states_hbm, states_ref))
    copies = [pltpu.make_async_copy(source, target, sems.at[place]) for place, (source, target) in enumerate(pairs)]
    for copy in copies:
        copy.start()
    for copy in copies:
        copy.wait()
    rows, dim = states_ref.shape[1:]
    for span in spans(dim):
        out_ref[:, span] = states_ref[0, :, span]
    lane = lax.broadcasted_iota(jnp.int32, (rows, LANES), 1).astype(jnp.float32)
    diagonal = lax.broadcasted_iota(jnp.int32, (rows, rows), 0) == lax.broadcasted_iota(jnp.int32, (rows, rows), 1)

    def upright(line):
        return jnp.sum(jnp.where(diagonal, line.astype(jnp.float32), 0.0), axis=1, keepdims=True)

    total = jnp.zeros((rows, LANES), jnp.float32)
    for step in range(routing_ref.shape[1]):
        for k in range(routing_ref.shape[2]):
            column = upright(routing_ref[0, step, k:k + 1, :]) + step * experts
            total += jnp.where(lane == column, upright(weight_ref[0, step, k:k + 1, :]), 0.0)
    out_ref[:, dim:] = total.astype(jnp.bfloat16)


def prepare(experts, states, routing, weight):
    args = [states, jnp.swapaxes(routing, 2, 3), jnp.swapaxes(weight, 2, 3)]
    rows, dim = states.shape[1:]
    (block,) = call(
        functools.partial(prepare_kernel, experts), [(rows, dim + LANES)],
        *[pltpu.with_memory_space_constraint(x, pltpu.HBM) for x in args],
        in_specs=[pl.BlockSpec(memory_space=pltpu.HBM)] * 3,
        scratch_shapes=[pltpu.VMEM(x.shape, x.dtype) for x in args] + [pltpu.SemaphoreType.DMA((3,))],
    )
    return block


def join_kernel(*refs):
    *parts, out_ref = refs
    for span in spans(out_ref.shape[1]):
        rows = [part[:, span].astype(jnp.float32) for part in parts]
        out_ref[:, span] = jnp.concatenate(rows, axis=0).astype(jnp.bfloat16)


def add_kernel(*refs):
    *parts, out_ref = refs
    for span in spans(out_ref.shape[1]):
        out_ref[:, span] = sum(part[:, span].astype(jnp.float32) for part in parts).astype(jnp.bfloat16)


def split_kernel(count, *refs):
    parts, outs = refs[:-count], refs[-count:]
    rows = outs[0].shape[0]
    for span in spans(outs[0].shape[1]):
        total = sum(part[:, span].astype(jnp.float32) for part in parts)
        for place, out_ref in enumerate(outs):
            out_ref[:, span] = total[place * rows:(place + 1) * rows].astype(jnp.bfloat16)


def normalise(raw_ref, gain_ref, out_ref):
    rows, dim = raw_ref.shape
    square = jnp.zeros((rows, LANES), jnp.float32)
    for start in range(0, dim, LANES):
        piece = raw_ref[:, start:start + LANES].astype(jnp.float32)
        square += piece * piece
    inv = lax.rsqrt(jnp.sum(square, axis=1, keepdims=True) / dim + 1e-06)
    for span in spans(dim):
        scaled = raw_ref[:, span].astype(jnp.float32) * inv * gain_ref[:, span]
        out_ref[:, span] = scaled.astype(jnp.bfloat16)


def first_kernel(own_ref, far_ref, gain_ref, out_ref, raw_ref):
    dim = raw_ref.shape[1]
    for span in spans(dim):
        rows = [ref[:, span].astype(jnp.float32) for ref in (own_ref, far_ref)]
        raw_ref[:, span] = jnp.concatenate(rows, axis=0).astype(jnp.bfloat16)
    tails = [ref[:, dim:].astype(jnp.float32) for ref in (own_ref, far_ref)]
    out_ref[:, dim:] = jnp.concatenate(tails, axis=0).astype(jnp.bfloat16)
    normalise(raw_ref, gain_ref, out_ref)


def meet_kernel(rest_ref, near_ref, far_ref, gain_ref, out_ref, own_ref, raw_ref):
    half = own_ref.shape[0]
    for span in spans(out_ref.shape[1]):
        far = far_ref[:, span].astype(jnp.float32)
        total = rest_ref[:, span].astype(jnp.float32) + near_ref[:, span].astype(jnp.float32)
        total = (total + jnp.concatenate([far[half:], far[:half]], axis=0)).astype(jnp.bfloat16)
        raw_ref[:, span] = total
        own_ref[:, span] = total[:half]
    normalise(raw_ref, gain_ref, out_ref)


def mlp_kernel(step_no, *refs):
    x_refs, refs = refs[:8], refs[8:]
    if step_no > 0:
        tail_ref, refs = refs[0], refs[1:]
    (gate_ref, up_ref, down_ref), outs, refs = refs[:3], refs[3:11], refs[11:]
    part = outs[0].shape[0]
    dim, hidden = gate_ref.shape[1:]
    experts = lax.axis_size("expert") // GROUP
    column = step_no * experts + lax.axis_index("expert") // GROUP
    lane = lax.broadcasted_iota(jnp.int32, (part, LANES), 1)
    weights = []
    for place, ref in enumerate(x_refs):
        band = slice(place * part, (place + 1) * part)
        if step_no == 0:
            tail = ref[:, dim:]
            refs[0][band, :] = tail
        else:
            tail = tail_ref[band, :]
        chosen = jnp.where(lane == column, tail.astype(jnp.float32), 0.0)
        weights.append(jnp.sum(chosen, axis=1, keepdims=True))
    gated = jnp.zeros((8 * part, hidden), jnp.float32)
    up_part = jnp.zeros((8 * part, hidden), jnp.float32)
    for span in spans(dim):
        rows = jnp.concatenate([ref[:, span] for ref in x_refs], axis=0)
        gated += jnp.dot(rows, gate_ref[0, span, :], preferred_element_type=jnp.float32)
        up_part += jnp.dot(rows, up_ref[0, span, :], preferred_element_type=jnp.float32)
    inner = (gated / (1.0 + jnp.exp(-gated)) * up_part).astype(jnp.bfloat16)
    for span in spans(dim):
        terms = jnp.dot(inner, down_ref[0, :, span], preferred_element_type=jnp.float32)
        for place, out_ref in enumerate(outs):
            weight = weights[place]
            mine = terms[place * part:(place + 1) * part]
            out_ref[:, span] = jnp.where(weight > 0.0, weight * mine, 0.0).astype(jnp.bfloat16)


def mlp(step_no, xs, tail, gate, up, down):
    dim, hidden = gate.shape[1:]
    part = xs[0].shape[0]
    gate, up, down = [pltpu.with_memory_space_constraint(w, pltpu.VMEM) for w in (gate, up, down)]
    first = step_no == 0
    args = list(xs) + ([] if first else [tail]) + [gate, up, down]
    result = call(
        functools.partial(mlp_kernel, step_no), [(part, dim)] * 8 + [(8 * part, LANES)] * first, *args,
        cost_estimate=pl.CostEstimate(
            flops=48 * part * dim * hidden, bytes_accessed=6 * dim * hidden, transcendentals=0
        ),
    )
    return result[:8], result[8] if first else tail


def add(*parts):
    rows = parts[0].shape[0]
    dim = parts[-1].shape[1]
    return call(add_kernel, [(rows, dim)], *parts)[0]


def split(*parts):
    rows, dim = parts[0].shape
    return call(functools.partial(split_kernel, 2), [(rows // 2, dim)] * 2, *parts)


def join(*parts):
    return call(join_kernel, [(sum(part.shape[0] for part in parts), parts[0].shape[1])], *parts)[0]


def on_device(states, routing, route_weight, norm_gain, gate_proj, up_proj, down_proj):
    owners = lax.axis_size("expert")
    row_dev, dim = states.shape[1:]
    passes_count = routing.shape[1]
    top, *middle = upper_flips(owners)

    gate, up = load(gate_proj, up_proj)
    block = prepare(owners // GROUP, states, routing, route_weight)
    other = exchange(block, top, 0)
    other, gate, up = lax.optimization_barrier((other, gate, up))
    pair, raw = call(first_kernel, [(2 * row_dev, dim + LANES), (2 * row_dev, dim)], block, other, norm_gain)
    pair, down_hbm = lax.optimization_barrier((pair, down_proj))
    (down,) = load(down_hbm)
    own, tail = states[0], None
    for step_no in range(passes_count):
        rows_a = pair
        for flips in middle:
            rows_a = join(rows_a, exchange(rows_a, flips, 0))
        mine = [rows_a] + [exchange(rows_a, flips, 0) for flips in SQUARE]
        near = rows_a
        if step_no == 0:
            near, down = lax.optimization_barrier((near, down))
        fars = [exchange(rows, CORE, 0) for rows in [near] + mine[1:]]
        outs, tail = mlp(step_no, mine + fars, tail, gate, up, down)

        kept, sent = outs[:4], [exchange(rows, CORE, 0) for rows in outs[4:]]
        parts = [kept[0], sent[0]]
        for place in (3, 2, 1):
            parts.append(exchange(add(kept[place], sent[place]), SQUARE[place - 1], 0))
        for flips in middle[::-1]:
            low, high = split(*parts)
            parts = [low, exchange(high, flips, 0)]
        if step_no < passes_count - 1:
            total = add(*parts)
            rest = exchange(raw, STAY, 1)
            more = step_no < passes_count - 2
            pair, own, *raws = call(
                meet_kernel, [(2 * row_dev, dim), (row_dev, dim)] + [(2 * row_dev, dim)] * more,
                rest, exchange(total, STAY, 1), exchange(total, top, 1), norm_gain,
                scratch_shapes=[] if more else [pltpu.VMEM((2 * row_dev, dim), jnp.bfloat16)],
            )
            raw = raws[0] if more else None
        else:
            low, high = split(*parts)
            rest = exchange(own, STAY, 1)
            own = add(rest, exchange(high, top, 1), exchange(low, STAY, 1))
    return own[None]


def solution(mesh):
    return jax.shard_map(
        on_device,
        mesh=mesh,
        in_specs=(
            P("segment", "expert", None),
            P("segment", None, "expert", None),
            P("segment", None, "expert", None),
            P("segment", None),
            P("segment", None, "expert"),
            P("segment", None, "expert"),
            P("segment", "expert", None),
        ),
        out_specs=P("segment", "expert", None),
        check_vma=False,
    )
```

```python
import functools

import jax
import jax.numpy as jnp
from jax import lax
from jax.experimental import pallas as pl
from jax.experimental.pallas import tpu as pltpu
from jax.sharding import PartitionSpec as P

GROUP = 4
LANES = 128
CHUNK = 1024
VMEM_LIMIT = 16 * 1024 * 1024
VMEM = pl.BlockSpec(memory_space=pltpu.VMEM)


def exchange(value, flips, hop):
    segments, owners = lax.axis_size("segment"), lax.axis_size("expert")
    if flips == (0, 0) and hop % segments == 0:
        return value
    pairs = []
    for seg in range(segments):
        for own in range(owners):
            target = (seg + hop) % segments * owners + (own ^ flips[own % 2])
            pairs.append((seg * owners + own, target))
    return lax.ppermute(value, ("segment", "expert"), pairs)


def upper_flips(owners):
    return [(1 << place,) * 2 for place in range(owners.bit_length() - 2, 2, -1)]


CORE = (1, 1)
SQUARE = ((4, 4), (6, 6), (2, 2))
STAY = (0, 0)


def spans(dim):
    return [slice(start, min(start + CHUNK, dim)) for start in range(0, dim, CHUNK)]


def call(kernel, outs, *args, **more):
    return pl.pallas_call(
        kernel,
        out_shape=[jax.ShapeDtypeStruct(shape, jnp.bfloat16) for shape in outs],
        in_specs=more.pop("in_specs", [VMEM] * len(args)),
        out_specs=[VMEM] * len(outs),
        compiler_params=pltpu.CompilerParams(vmem_limit_bytes=VMEM_LIMIT),
        **more,
    )(*args)


def load_kernel(count, *refs):
    sems = refs[-1]
    copies = [pltpu.make_async_copy(refs[place], refs[count + place], sems.at[place]) for place in range(count)]
    for copy in copies:
        copy.start()
    for copy in copies:
        copy.wait()


def load(*weights):
    count = len(weights)
    return pl.pallas_call(
        functools.partial(load_kernel, count),
        out_shape=[pltpu.VMEM(w.shape, w.dtype) for w in weights],
        in_specs=[pl.BlockSpec(memory_space=pltpu.HBM)] * count,
        out_specs=[VMEM] * count,
        scratch_shapes=[pltpu.SemaphoreType.DMA((count,))],
        compiler_params=pltpu.CompilerParams(vmem_limit_bytes=VMEM_LIMIT),
        cost_estimate=pl.CostEstimate(
            flops=0, bytes_accessed=sum(2 * w.size for w in weights), transcendentals=0
        ),
    )(*[pltpu.with_memory_space_constraint(w, pltpu.HBM) for w in weights])


def prepare_kernel(experts, states_hbm, routing_hbm, weight_hbm, out_ref, states_ref, routing_ref, weight_ref, sems):
    pairs = ((routing_hbm, routing_ref), (weight_hbm, weight_ref), (states_hbm, states_ref))
    copies = [pltpu.make_async_copy(source, target, sems.at[place]) for place, (source, target) in enumerate(pairs)]
    for copy in copies:
        copy.start()
    for copy in copies:
        copy.wait()
    rows, dim = states_ref.shape[1:]
    for span in spans(dim):
        out_ref[:, span] = states_ref[0, :, span]
    lane = lax.broadcasted_iota(jnp.int32, (rows, LANES), 1).astype(jnp.float32)
    diagonal = lax.broadcasted_iota(jnp.int32, (rows, rows), 0) == lax.broadcasted_iota(jnp.int32, (rows, rows), 1)

    def upright(line):
        return jnp.sum(jnp.where(diagonal, line.astype(jnp.float32), 0.0), axis=1, keepdims=True)

    total = jnp.zeros((rows, LANES), jnp.float32)
    for step in range(routing_ref.shape[1]):
        for k in range(routing_ref.shape[2]):
            column = upright(routing_ref[0, step, k:k + 1, :]) + step * experts
            total += jnp.where(lane == column, upright(weight_ref[0, step, k:k + 1, :]), 0.0)
    out_ref[:, dim:] = total.astype(jnp.bfloat16)


def prepare(experts, states, routing, weight):
    args = [states, jnp.swapaxes(routing, 2, 3), jnp.swapaxes(weight, 2, 3)]
    rows, dim = states.shape[1:]
    (block,) = call(
        functools.partial(prepare_kernel, experts), [(rows, dim + LANES)],
        *[pltpu.with_memory_space_constraint(x, pltpu.HBM) for x in args],
        in_specs=[pl.BlockSpec(memory_space=pltpu.HBM)] * 3,
        scratch_shapes=[pltpu.VMEM(x.shape, x.dtype) for x in args] + [pltpu.SemaphoreType.DMA((3,))],
    )
    return block


def join_kernel(*refs):
    *parts, out_ref = refs
    for span in spans(out_ref.shape[1]):
        rows = [part[:, span].astype(jnp.float32) for part in parts]
        out_ref[:, span] = jnp.concatenate(rows, axis=0).astype(jnp.bfloat16)


def add_kernel(*refs):
    *parts, out_ref = refs
    for span in spans(out_ref.shape[1]):
        out_ref[:, span] = sum(part[:, span].astype(jnp.float32) for part in parts).astype(jnp.bfloat16)


def split_kernel(count, *refs):
    parts, outs = refs[:-count], refs[-count:]
    rows = outs[0].shape[0]
    for span in spans(outs[0].shape[1]):
        total = sum(part[:, span].astype(jnp.float32) for part in parts)
        for place, out_ref in enumerate(outs):
            out_ref[:, span] = total[place * rows:(place + 1) * rows].astype(jnp.bfloat16)


def normalise(raw_ref, gain_ref, out_ref):
    rows, dim = raw_ref.shape
    square = jnp.zeros((rows, LANES), jnp.float32)
    for start in range(0, dim, LANES):
        piece = raw_ref[:, start:start + LANES].astype(jnp.float32)
        square += piece * piece
    inv = lax.rsqrt(jnp.sum(square, axis=1, keepdims=True) / dim + 1e-06)
    for span in spans(dim):
        scaled = raw_ref[:, span].astype(jnp.float32) * inv * gain_ref[:, span]
        out_ref[:, span] = scaled.astype(jnp.bfloat16)


def first_kernel(own_ref, far_ref, gain_ref, out_ref, raw_ref):
    dim = raw_ref.shape[1]
    for span in spans(dim):
        rows = [ref[:, span].astype(jnp.float32) for ref in (own_ref, far_ref)]
        raw_ref[:, span] = jnp.concatenate(rows, axis=0).astype(jnp.bfloat16)
    tails = [ref[:, dim:].astype(jnp.float32) for ref in (own_ref, far_ref)]
    out_ref[:, dim:] = jnp.concatenate(tails, axis=0).astype(jnp.bfloat16)
    normalise(raw_ref, gain_ref, out_ref)


def meet_kernel(rest_ref, near_ref, far_ref, gain_ref, out_ref, own_ref, raw_ref):
    half = own_ref.shape[0]
    for span in spans(out_ref.shape[1]):
        far = far_ref[:, span].astype(jnp.float32)
        total = rest_ref[:, span].astype(jnp.float32) + near_ref[:, span].astype(jnp.float32)
        total = (total + jnp.concatenate([far[half:], far[:half]], axis=0)).astype(jnp.bfloat16)
        raw_ref[:, span] = total
        own_ref[:, span] = total[:half]
    normalise(raw_ref, gain_ref, out_ref)


def mlp_kernel(step_no, *refs):
    x_refs, refs = refs[:8], refs[8:]
    if step_no > 0:
        tail_ref, refs = refs[0], refs[1:]
    (gate_ref, up_ref, down_ref), outs, refs = refs[:3], refs[3:11], refs[11:]
    part = outs[0].shape[0]
    dim, hidden = gate_ref.shape[1:]
    experts = lax.axis_size("expert") // GROUP
    column = step_no * experts + lax.axis_index("expert") // GROUP
    lane = lax.broadcasted_iota(jnp.int32, (part, LANES), 1)
    weights = []
    for place, ref in enumerate(x_refs):
        band = slice(place * part, (place + 1) * part)
        if step_no == 0:
            tail = ref[:, dim:]
            refs[0][band, :] = tail
        else:
            tail = tail_ref[band, :]
        chosen = jnp.where(lane == column, tail.astype(jnp.float32), 0.0)
        weights.append(jnp.sum(chosen, axis=1, keepdims=True))
    gated = jnp.zeros((8 * part, hidden), jnp.float32)
    up_part = jnp.zeros((8 * part, hidden), jnp.float32)
    for span in spans(dim):
        rows = jnp.concatenate([ref[:, span] for ref in x_refs], axis=0)
        gated += jnp.dot(rows, gate_ref[0, span, :], preferred_element_type=jnp.float32)
        up_part += jnp.dot(rows, up_ref[0, span, :], preferred_element_type=jnp.float32)
    inner = (gated / (1.0 + jnp.exp(-gated)) * up_part).astype(jnp.bfloat16)
    for span in spans(dim):
        terms = jnp.dot(inner, down_ref[0, :, span], preferred_element_type=jnp.float32)
        for place, out_ref in enumerate(outs):
            weight = weights[place]
            mine = terms[place * part:(place + 1) * part]
            out_ref[:, span] = jnp.where(weight > 0.0, weight * mine, 0.0).astype(jnp.bfloat16)


def mlp(step_no, xs, tail, gate, up, down):
    dim, hidden = gate.shape[1:]
    part = xs[0].shape[0]
    gate, up, down = [pltpu.with_memory_space_constraint(w, pltpu.VMEM) for w in (gate, up, down)]
    first = step_no == 0
    args = list(xs) + ([] if first else [tail]) + [gate, up, down]
    result = call(
        functools.partial(mlp_kernel, step_no), [(part, dim)] * 8 + [(8 * part, LANES)] * first, *args,
        cost_estimate=pl.CostEstimate(
            flops=48 * part * dim * hidden, bytes_accessed=6 * dim * hidden, transcendentals=0
        ),
    )
    return result[:8], result[8] if first else tail


def add(*parts):
    rows = parts[0].shape[0]
    dim = parts[-1].shape[1]
    return call(add_kernel, [(rows, dim)], *parts)[0]


def split(*parts):
    rows, dim = parts[0].shape
    return call(functools.partial(split_kernel, 2), [(rows // 2, dim)] * 2, *parts)


def join(*parts):
    return call(join_kernel, [(sum(part.shape[0] for part in parts), parts[0].shape[1])], *parts)[0]


def on_device(states, routing, route_weight, norm_gain, gate_proj, up_proj, down_proj):
    owners = lax.axis_size("expert")
    row_dev, dim = states.shape[1:]
    passes_count = routing.shape[1]
    top, *middle = upper_flips(owners)

    gate, up = load(gate_proj, up_proj)
    block = prepare(owners // GROUP, states, routing, route_weight)
    other = exchange(block, top, 0)
    other, gate, up = lax.optimization_barrier((other, gate, up))
    pair, raw = call(first_kernel, [(2 * row_dev, dim + LANES), (2 * row_dev, dim)], block, other, norm_gain)
    pair, down_hbm = lax.optimization_barrier((pair, down_proj))
    (down,) = load(down_hbm)
    own, tail = states[0], None
    for step_no in range(passes_count):
        rows_a = pair
        for flips in middle:
            rows_a = join(rows_a, exchange(rows_a, flips, 0))
        mine = [rows_a] + [exchange(rows_a, flips, 0) for flips in SQUARE]
        near = rows_a
        if step_no == 0:
            near, down = lax.optimization_barrier((near, down))
        fars = [exchange(rows, CORE, 0) for rows in [near] + mine[1:]]
        outs, tail = mlp(step_no, mine + fars, tail, gate, up, down)

        kept, sent = outs[:4], [exchange(rows, CORE, 0) for rows in outs[4:]]
        parts = [kept[0], sent[0]]
        for place in (1, 2, 3):
            parts.append(exchange(add(kept[place], sent[place]), SQUARE[place - 1], 0))
        for flips in middle[::-1]:
            low, high = split(*parts)
            parts = [low, exchange(high, flips, 0)]
        if step_no < passes_count - 1:
            total = add(*parts)
            rest = exchange(raw, STAY, 1)
            more = step_no < passes_count - 2
            pair, own, *raws = call(
                meet_kernel, [(2 * row_dev, dim), (row_dev, dim)] + [(2 * row_dev, dim)] * more,
                rest, exchange(total, STAY, 1), exchange(total, top, 1), norm_gain,
                scratch_shapes=[] if more else [pltpu.VMEM((2 * row_dev, dim), jnp.bfloat16)],
            )
            raw = raws[0] if more else None
        else:
            low, high = split(*parts)
            rest = exchange(own, STAY, 1)
            own = add(rest, exchange(high, top, 1), exchange(low, STAY, 1))
    return own[None]


def solution(mesh):
    return jax.shard_map(
        on_device,
        mesh=mesh,
        in_specs=(
            P("segment", "expert", None),
            P("segment", None, "expert", None),
            P("segment", None, "expert", None),
            P("segment", None),
            P("segment", None, "expert"),
            P("segment", None, "expert"),
            P("segment", "expert", None),
        ),
        out_specs=P("segment", "expert", None),
        check_vma=False,
    )
```

```python
import functools

import jax
import jax.numpy as jnp
from jax import lax
from jax.experimental import pallas as pl
from jax.experimental.pallas import tpu as pltpu
from jax.sharding import PartitionSpec as P

GROUP = 4
LANES = 128
CHUNK = 1024
VMEM_LIMIT = 16 * 1024 * 1024
VMEM = pl.BlockSpec(memory_space=pltpu.VMEM)


def exchange(value, flips, hop):
    segments, owners = lax.axis_size("segment"), lax.axis_size("expert")
    if flips == (0, 0) and hop % segments == 0:
        return value
    pairs = []
    for seg in range(segments):
        for own in range(owners):
            target = (seg + hop) % segments * owners + (own ^ flips[own % 2])
            pairs.append((seg * owners + own, target))
    return lax.ppermute(value, ("segment", "expert"), pairs)


def upper_flips(owners):
    return [(1 << place,) * 2 for place in range(owners.bit_length() - 2, 2, -1)]


CORE = (1, 1)
SQUARE = ((4, 4), (2, 2), (6, 6))
STAY = (0, 0)


def spans(dim):
    return [slice(start, min(start + CHUNK, dim)) for start in range(0, dim, CHUNK)]


def call(kernel, outs, *args, **more):
    return pl.pallas_call(
        kernel,
        out_shape=[jax.ShapeDtypeStruct(shape, jnp.bfloat16) for shape in outs],
        in_specs=more.pop("in_specs", [VMEM] * len(args)),
        out_specs=[VMEM] * len(outs),
        compiler_params=pltpu.CompilerParams(vmem_limit_bytes=VMEM_LIMIT),
        **more,
    )(*args)


def load_kernel(count, *refs):
    sems = refs[-1]
    copies = [pltpu.make_async_copy(refs[place], refs[count + place], sems.at[place]) for place in range(count)]
    for copy in copies:
        copy.start()
    for copy in copies:
        copy.wait()


def load(*weights):
    count = len(weights)
    return pl.pallas_call(
        functools.partial(load_kernel, count),
        out_shape=[pltpu.VMEM(w.shape, w.dtype) for w in weights],
        in_specs=[pl.BlockSpec(memory_space=pltpu.HBM)] * count,
        out_specs=[VMEM] * count,
        scratch_shapes=[pltpu.SemaphoreType.DMA((count,))],
        compiler_params=pltpu.CompilerParams(vmem_limit_bytes=VMEM_LIMIT),
        cost_estimate=pl.CostEstimate(
            flops=0, bytes_accessed=sum(2 * w.size for w in weights), transcendentals=0
        ),
    )(*[pltpu.with_memory_space_constraint(w, pltpu.HBM) for w in weights])


def prepare_kernel(experts, states_hbm, routing_hbm, weight_hbm, out_ref, states_ref, routing_ref, weight_ref, sems):
    pairs = ((routing_hbm, routing_ref), (weight_hbm, weight_ref), (states_hbm, states_ref))
    copies = [pltpu.make_async_copy(source, target, sems.at[place]) for place, (source, target) in enumerate(pairs)]
    for copy in copies:
        copy.start()
    for copy in copies:
        copy.wait()
    rows, dim = states_ref.shape[1:]
    for span in spans(dim):
        out_ref[:, span] = states_ref[0, :, span]
    lane = lax.broadcasted_iota(jnp.int32, (rows, LANES), 1).astype(jnp.float32)
    diagonal = lax.broadcasted_iota(jnp.int32, (rows, rows), 0) == lax.broadcasted_iota(jnp.int32, (rows, rows), 1)

    def upright(line):
        return jnp.sum(jnp.where(diagonal, line.astype(jnp.float32), 0.0), axis=1, keepdims=True)

    total = jnp.zeros((rows, LANES), jnp.float32)
    for step in range(routing_ref.shape[1]):
        for k in range(routing_ref.shape[2]):
            column = upright(routing_ref[0, step, k:k + 1, :]) + step * experts
            total += jnp.where(lane == column, upright(weight_ref[0, step, k:k + 1, :]), 0.0)
    out_ref[:, dim:] = total.astype(jnp.bfloat16)


def prepare(experts, states, routing, weight):
    args = [states, jnp.swapaxes(routing, 2, 3), jnp.swapaxes(weight, 2, 3)]
    rows, dim = states.shape[1:]
    (block,) = call(
        functools.partial(prepare_kernel, experts), [(rows, dim + LANES)],
        *[pltpu.with_memory_space_constraint(x, pltpu.HBM) for x in args],
        in_specs=[pl.BlockSpec(memory_space=pltpu.HBM)] * 3,
        scratch_shapes=[pltpu.VMEM(x.shape, x.dtype) for x in args] + [pltpu.SemaphoreType.DMA((3,))],
    )
    return block


def join_kernel(*refs):
    *parts, out_ref = refs
    for span in spans(out_ref.shape[1]):
        rows = [part[:, span].astype(jnp.float32) for part in parts]
        out_ref[:, span] = jnp.concatenate(rows, axis=0).astype(jnp.bfloat16)


def add_kernel(*refs):
    *parts, out_ref = refs
    for span in spans(out_ref.shape[1]):
        out_ref[:, span] = sum(part[:, span].astype(jnp.float32) for part in parts).astype(jnp.bfloat16)


def split_kernel(count, *refs):
    parts, outs = refs[:-count], refs[-count:]
    rows = outs[0].shape[0]
    for span in spans(outs[0].shape[1]):
        total = sum(part[:, span].astype(jnp.float32) for part in parts)
        for place, out_ref in enumerate(outs):
            out_ref[:, span] = total[place * rows:(place + 1) * rows].astype(jnp.bfloat16)


def normalise(raw_ref, gain_ref, out_ref):
    rows, dim = raw_ref.shape
    square = jnp.zeros((rows, LANES), jnp.float32)
    for start in range(0, dim, LANES):
        piece = raw_ref[:, start:start + LANES].astype(jnp.float32)
        square += piece * piece
    inv = lax.rsqrt(jnp.sum(square, axis=1, keepdims=True) / dim + 1e-06)
    for span in spans(dim):
        scaled = raw_ref[:, span].astype(jnp.float32) * inv * gain_ref[:, span]
        out_ref[:, span] = scaled.astype(jnp.bfloat16)


def first_kernel(own_ref, far_ref, gain_ref, out_ref, raw_ref):
    dim = raw_ref.shape[1]
    for span in spans(dim):
        rows = [ref[:, span].astype(jnp.float32) for ref in (own_ref, far_ref)]
        raw_ref[:, span] = jnp.concatenate(rows, axis=0).astype(jnp.bfloat16)
    tails = [ref[:, dim:].astype(jnp.float32) for ref in (own_ref, far_ref)]
    out_ref[:, dim:] = jnp.concatenate(tails, axis=0).astype(jnp.bfloat16)
    normalise(raw_ref, gain_ref, out_ref)


def meet_kernel(rest_ref, near_ref, far_ref, gain_ref, out_ref, own_ref, raw_ref):
    half = own_ref.shape[0]
    for span in spans(out_ref.shape[1]):
        far = far_ref[:, span].astype(jnp.float32)
        total = rest_ref[:, span].astype(jnp.float32) + near_ref[:, span].astype(jnp.float32)
        total = (total + jnp.concatenate([far[half:], far[:half]], axis=0)).astype(jnp.bfloat16)
        raw_ref[:, span] = total
        own_ref[:, span] = total[:half]
    normalise(raw_ref, gain_ref, out_ref)


def mlp_kernel(step_no, *refs):
    x_refs, refs = refs[:8], refs[8:]
    if step_no > 0:
        tail_ref, refs = refs[0], refs[1:]
    (gate_ref, up_ref, down_ref), outs, refs = refs[:3], refs[3:11], refs[11:]
    part = outs[0].shape[0]
    dim, hidden = gate_ref.shape[1:]
    experts = lax.axis_size("expert") // GROUP
    column = step_no * experts + lax.axis_index("expert") // GROUP
    lane = lax.broadcasted_iota(jnp.int32, (part, LANES), 1)
    weights = []
    for place, ref in enumerate(x_refs):
        band = slice(place * part, (place + 1) * part)
        if step_no == 0:
            tail = ref[:, dim:]
            refs[0][band, :] = tail
        else:
            tail = tail_ref[band, :]
        chosen = jnp.where(lane == column, tail.astype(jnp.float32), 0.0)
        weights.append(jnp.sum(chosen, axis=1, keepdims=True))
    gated = jnp.zeros((8 * part, hidden), jnp.float32)
    up_part = jnp.zeros((8 * part, hidden), jnp.float32)
    for span in spans(dim):
        rows = jnp.concatenate([ref[:, span] for ref in x_refs], axis=0)
        gated += jnp.dot(rows, gate_ref[0, span, :], preferred_element_type=jnp.float32)
        up_part += jnp.dot(rows, up_ref[0, span, :], preferred_element_type=jnp.float32)
    inner = (gated / (1.0 + jnp.exp(-gated)) * up_part).astype(jnp.bfloat16)
    for span in spans(dim):
        terms = jnp.dot(inner, down_ref[0, :, span], preferred_element_type=jnp.float32)
        for place, out_ref in enumerate(outs):
            weight = weights[place]
            mine = terms[place * part:(place + 1) * part]
            out_ref[:, span] = jnp.where(weight > 0.0, weight * mine, 0.0).astype(jnp.bfloat16)


def mlp(step_no, xs, tail, gate, up, down):
    dim, hidden = gate.shape[1:]
    part = xs[0].shape[0]
    gate, up, down = [pltpu.with_memory_space_constraint(w, pltpu.VMEM) for w in (gate, up, down)]
    first = step_no == 0
    args = list(xs) + ([] if first else [tail]) + [gate, up, down]
    result = call(
        functools.partial(mlp_kernel, step_no), [(part, dim)] * 8 + [(8 * part, LANES)] * first, *args,
        cost_estimate=pl.CostEstimate(
            flops=48 * part * dim * hidden, bytes_accessed=6 * dim * hidden, transcendentals=0
        ),
    )
    return result[:8], result[8] if first else tail


def add(*parts):
    rows = parts[0].shape[0]
    dim = parts[-1].shape[1]
    return call(add_kernel, [(rows, dim)], *parts)[0]


def split(*parts):
    rows, dim = parts[0].shape
    return call(functools.partial(split_kernel, 2), [(rows // 2, dim)] * 2, *parts)


def join(*parts):
    return call(join_kernel, [(sum(part.shape[0] for part in parts), parts[0].shape[1])], *parts)[0]


def on_device(states, routing, route_weight, norm_gain, gate_proj, up_proj, down_proj):
    owners = lax.axis_size("expert")
    row_dev, dim = states.shape[1:]
    passes_count = routing.shape[1]
    top, *middle = upper_flips(owners)

    gate, up = load(gate_proj, up_proj)
    block = prepare(owners // GROUP, states, routing, route_weight)
    other = exchange(block, top, 0)
    other, gate, up = lax.optimization_barrier((other, gate, up))
    pair, raw = call(first_kernel, [(2 * row_dev, dim + LANES), (2 * row_dev, dim)], block, other, norm_gain)
    pair, down_hbm = lax.optimization_barrier((pair, down_proj))
    (down,) = load(down_hbm)
    own, tail = states[0], None
    for step_no in range(passes_count):
        rows_a = pair
        for flips in middle:
            rows_a = join(rows_a, exchange(rows_a, flips, 0))
        mine = [rows_a] + [exchange(rows_a, flips, 0) for flips in SQUARE]
        near = rows_a
        if step_no == 0:
            near, down = lax.optimization_barrier((near, down))
        fars = [exchange(rows, CORE, 0) for rows in [near] + mine[1:]]
        outs, tail = mlp(step_no, mine + fars, tail, gate, up, down)

        kept, sent = outs[:4], [exchange(rows, CORE, 0) for rows in outs[4:]]
        parts = [kept[0], sent[0]]
        for place in (3, 1, 2):
            parts.append(exchange(add(kept[place], sent[place]), SQUARE[place - 1], 0))
        for flips in middle[::-1]:
            low, high = split(*parts)
            parts = [low, exchange(high, flips, 0)]
        if step_no < passes_count - 1:
            total = add(*parts)
            rest = exchange(raw, STAY, 1)
            more = step_no < passes_count - 2
            pair, own, *raws = call(
                meet_kernel, [(2 * row_dev, dim), (row_dev, dim)] + [(2 * row_dev, dim)] * more,
                rest, exchange(total, STAY, 1), exchange(total, top, 1), norm_gain,
                scratch_shapes=[] if more else [pltpu.VMEM((2 * row_dev, dim), jnp.bfloat16)],
            )
            raw = raws[0] if more else None
        else:
            low, high = split(*parts)
            rest = exchange(own, STAY, 1)
            own = add(rest, exchange(high, top, 1), exchange(low, STAY, 1))
    return own[None]


def solution(mesh):
    return jax.shard_map(
        on_device,
        mesh=mesh,
        in_specs=(
            P("segment", "expert", None),
            P("segment", None, "expert", None),
            P("segment", None, "expert", None),
            P("segment", None),
            P("segment", None, "expert"),
            P("segment", None, "expert"),
            P("segment", "expert", None),
        ),
        out_specs=P("segment", "expert", None),
        check_vma=False,
    )
```

```python
import functools

import jax
import jax.numpy as jnp
from jax import lax
from jax.experimental import pallas as pl
from jax.experimental.pallas import tpu as pltpu
from jax.sharding import PartitionSpec as P

GROUP = 4
LANES = 128
CHUNK = 1024
VMEM_LIMIT = 16 * 1024 * 1024
VMEM = pl.BlockSpec(memory_space=pltpu.VMEM)


def exchange(value, flips, hop):
    segments, owners = lax.axis_size("segment"), lax.axis_size("expert")
    if flips == (0, 0) and hop % segments == 0:
        return value
    pairs = []
    for seg in range(segments):
        for own in range(owners):
            target = (seg + hop) % segments * owners + (own ^ flips[own % 2])
            pairs.append((seg * owners + own, target))
    return lax.ppermute(value, ("segment", "expert"), pairs)


def upper_flips(owners):
    return [(1 << place,) * 2 for place in range(owners.bit_length() - 2, 2, -1)]


CORE = (1, 1)
SQUARE = ((2, 2), (4, 4), (6, 6))
STAY = (0, 0)


def spans(dim):
    return [slice(start, min(start + CHUNK, dim)) for start in range(0, dim, CHUNK)]


def call(kernel, outs, *args, **more):
    return pl.pallas_call(
        kernel,
        out_shape=[jax.ShapeDtypeStruct(shape, jnp.bfloat16) for shape in outs],
        in_specs=more.pop("in_specs", [VMEM] * len(args)),
        out_specs=[VMEM] * len(outs),
        compiler_params=pltpu.CompilerParams(vmem_limit_bytes=VMEM_LIMIT),
        **more,
    )(*args)


def load_kernel(count, *refs):
    sems = refs[-1]
    copies = [pltpu.make_async_copy(refs[place], refs[count + place], sems.at[place]) for place in range(count)]
    for copy in copies:
        copy.start()
    for copy in copies:
        copy.wait()


def load(*weights):
    count = len(weights)
    return pl.pallas_call(
        functools.partial(load_kernel, count),
        out_shape=[pltpu.VMEM(w.shape, w.dtype) for w in weights],
        in_specs=[pl.BlockSpec(memory_space=pltpu.HBM)] * count,
        out_specs=[VMEM] * count,
        scratch_shapes=[pltpu.SemaphoreType.DMA((count,))],
        compiler_params=pltpu.CompilerParams(vmem_limit_bytes=VMEM_LIMIT),
        cost_estimate=pl.CostEstimate(
            flops=0, bytes_accessed=sum(2 * w.size for w in weights), transcendentals=0
        ),
    )(*[pltpu.with_memory_space_constraint(w, pltpu.HBM) for w in weights])


def prepare_kernel(experts, states_hbm, routing_hbm, weight_hbm, out_ref, states_ref, routing_ref, weight_ref, sems):
    pairs = ((routing_hbm, routing_ref), (weight_hbm, weight_ref), (states_hbm, states_ref))
    copies = [pltpu.make_async_copy(source, target, sems.at[place]) for place, (source, target) in enumerate(pairs)]
    for copy in copies:
        copy.start()
    rows, dim = states_ref.shape[1:]
    copies[0].wait()
    copies[1].wait()
    lane = lax.broadcasted_iota(jnp.int32, (rows, LANES), 1).astype(jnp.float32)
    diagonal = lax.broadcasted_iota(jnp.int32, (rows, rows), 0) == lax.broadcasted_iota(jnp.int32, (rows, rows), 1)

    def upright(line):
        return jnp.sum(jnp.where(diagonal, line.astype(jnp.float32), 0.0), axis=1, keepdims=True)

    total = jnp.zeros((rows, LANES), jnp.float32)
    for step in range(routing_ref.shape[1]):
        for k in range(routing_ref.shape[2]):
            column = upright(routing_ref[0, step, k:k + 1, :]) + step * experts
            total += jnp.where(lane == column, upright(weight_ref[0, step, k:k + 1, :]), 0.0)
    out_ref[:, dim:] = total.astype(jnp.bfloat16)
    copies[2].wait()
    for span in spans(dim):
        out_ref[:, span] = states_ref[0, :, span]


def prepare(experts, states, routing, weight):
    args = [states, jnp.swapaxes(routing, 2, 3), jnp.swapaxes(weight, 2, 3)]
    rows, dim = states.shape[1:]
    (block,) = call(
        functools.partial(prepare_kernel, experts), [(rows, dim + LANES)],
        *[pltpu.with_memory_space_constraint(x, pltpu.HBM) for x in args],
        in_specs=[pl.BlockSpec(memory_space=pltpu.HBM)] * 3,
        scratch_shapes=[pltpu.VMEM(x.shape, x.dtype) for x in args] + [pltpu.SemaphoreType.DMA((3,))],
    )
    return block


def join_kernel(*refs):
    *parts, out_ref = refs
    for span in spans(out_ref.shape[1]):
        rows = [part[:, span].astype(jnp.float32) for part in parts]
        out_ref[:, span] = jnp.concatenate(rows, axis=0).astype(jnp.bfloat16)


def add_kernel(*refs):
    *parts, out_ref = refs
    for span in spans(out_ref.shape[1]):
        out_ref[:, span] = sum(part[:, span].astype(jnp.float32) for part in parts).astype(jnp.bfloat16)


def split_kernel(count, *refs):
    parts, outs = refs[:-count], refs[-count:]
    rows = outs[0].shape[0]
    for span in spans(outs[0].shape[1]):
        total = sum(part[:, span].astype(jnp.float32) for part in parts)
        for place, out_ref in enumerate(outs):
            out_ref[:, span] = total[place * rows:(place + 1) * rows].astype(jnp.bfloat16)


def normalise(raw_ref, gain_ref, out_ref):
    rows, dim = raw_ref.shape
    square = jnp.zeros((rows, LANES), jnp.float32)
    for start in range(0, dim, LANES):
        piece = raw_ref[:, start:start + LANES].astype(jnp.float32)
        square += piece * piece
    inv = lax.rsqrt(jnp.sum(square, axis=1, keepdims=True) / dim + 1e-06)
    for span in spans(dim):
        scaled = raw_ref[:, span].astype(jnp.float32) * inv * gain_ref[:, span]
        out_ref[:, span] = scaled.astype(jnp.bfloat16)


def first_kernel(own_ref, far_ref, gain_ref, out_ref, raw_ref):
    dim = raw_ref.shape[1]
    for span in spans(dim):
        rows = [ref[:, span].astype(jnp.float32) for ref in (own_ref, far_ref)]
        raw_ref[:, span] = jnp.concatenate(rows, axis=0).astype(jnp.bfloat16)
    tails = [ref[:, dim:].astype(jnp.float32) for ref in (own_ref, far_ref)]
    out_ref[:, dim:] = jnp.concatenate(tails, axis=0).astype(jnp.bfloat16)
    normalise(raw_ref, gain_ref, out_ref)


def meet_kernel(rest_ref, near_ref, far_ref, gain_ref, out_ref, own_ref, raw_ref):
    half = own_ref.shape[0]
    for span in spans(out_ref.shape[1]):
        far = far_ref[:, span].astype(jnp.float32)
        total = rest_ref[:, span].astype(jnp.float32) + near_ref[:, span].astype(jnp.float32)
        total = (total + jnp.concatenate([far[half:], far[:half]], axis=0)).astype(jnp.bfloat16)
        raw_ref[:, span] = total
        own_ref[:, span] = total[:half]
    normalise(raw_ref, gain_ref, out_ref)


def mlp_kernel(step_no, *refs):
    x_refs, refs = refs[:8], refs[8:]
    if step_no > 0:
        tail_ref, refs = refs[0], refs[1:]
    (gate_ref, up_ref, down_ref), outs, refs = refs[:3], refs[3:11], refs[11:]
    part = outs[0].shape[0]
    dim, hidden = gate_ref.shape[1:]
    experts = lax.axis_size("expert") // GROUP
    column = step_no * experts + lax.axis_index("expert") // GROUP
    lane = lax.broadcasted_iota(jnp.int32, (part, LANES), 1)
    weights = []
    for place, ref in enumerate(x_refs):
        band = slice(place * part, (place + 1) * part)
        if step_no == 0:
            tail = ref[:, dim:]
            refs[0][band, :] = tail
        else:
            tail = tail_ref[band, :]
        chosen = jnp.where(lane == column, tail.astype(jnp.float32), 0.0)
        weights.append(jnp.sum(chosen, axis=1, keepdims=True))
    gated = jnp.zeros((8 * part, hidden), jnp.float32)
    up_part = jnp.zeros((8 * part, hidden), jnp.float32)
    for span in spans(dim):
        rows = jnp.concatenate([ref[:, span] for ref in x_refs], axis=0)
        gated += jnp.dot(rows, gate_ref[0, span, :], preferred_element_type=jnp.float32)
        up_part += jnp.dot(rows, up_ref[0, span, :], preferred_element_type=jnp.float32)
    inner = (gated / (1.0 + jnp.exp(-gated)) * up_part).astype(jnp.bfloat16)
    for span in spans(dim):
        terms = jnp.dot(inner, down_ref[0, :, span], preferred_element_type=jnp.float32)
        for place, out_ref in enumerate(outs):
            weight = weights[place]
            mine = terms[place * part:(place + 1) * part]
            out_ref[:, span] = jnp.where(weight > 0.0, weight * mine, 0.0).astype(jnp.bfloat16)


def mlp(step_no, xs, tail, gate, up, down):
    dim, hidden = gate.shape[1:]
    part = xs[0].shape[0]
    gate, up, down = [pltpu.with_memory_space_constraint(w, pltpu.VMEM) for w in (gate, up, down)]
    first = step_no == 0
    args = list(xs) + ([] if first else [tail]) + [gate, up, down]
    result = call(
        functools.partial(mlp_kernel, step_no), [(part, dim)] * 8 + [(8 * part, LANES)] * first, *args,
        cost_estimate=pl.CostEstimate(
            flops=48 * part * dim * hidden, bytes_accessed=6 * dim * hidden, transcendentals=0
        ),
    )
    return result[:8], result[8] if first else tail


def add(*parts):
    rows = parts[0].shape[0]
    dim = parts[-1].shape[1]
    return call(add_kernel, [(rows, dim)], *parts)[0]


def split(*parts):
    rows, dim = parts[0].shape
    return call(functools.partial(split_kernel, 2), [(rows // 2, dim)] * 2, *parts)


def join(*parts):
    return call(join_kernel, [(sum(part.shape[0] for part in parts), parts[0].shape[1])], *parts)[0]


def on_device(states, routing, route_weight, norm_gain, gate_proj, up_proj, down_proj):
    owners = lax.axis_size("expert")
    row_dev, dim = states.shape[1:]
    passes_count = routing.shape[1]
    top, *middle = upper_flips(owners)

    (gate,) = load(gate_proj)
    block = prepare(owners // GROUP, states, routing, route_weight)
    other = exchange(block, top, 0)
    other, gate = lax.optimization_barrier((other, gate))
    pair, raw = call(first_kernel, [(2 * row_dev, dim + LANES), (2 * row_dev, dim)], block, other, norm_gain)
    pair, up_hbm, down_hbm = lax.optimization_barrier((pair, up_proj, down_proj))
    up, down = load(up_hbm, down_hbm)
    own, tail = states[0], None
    for step_no in range(passes_count):
        rows_a = pair
        for flips in middle:
            rows_a = join(rows_a, exchange(rows_a, flips, 0))
        mine = [rows_a] + [exchange(rows_a, flips, 0) for flips in SQUARE]
        near = rows_a
        if step_no == 0:
            near, up, down = lax.optimization_barrier((near, up, down))
        fars = [exchange(rows, CORE, 0) for rows in [near] + mine[1:]]
        outs, tail = mlp(step_no, mine + fars, tail, gate, up, down)

        kept, sent = outs[:4], [exchange(rows, CORE, 0) for rows in outs[4:]]
        parts = [kept[0], sent[0]]
        for place in (3, 2, 1):
            parts.append(exchange(add(kept[place], sent[place]), SQUARE[place - 1], 0))
        for flips in middle[::-1]:
            low, high = split(*parts)
            parts = [low, exchange(high, flips, 0)]
        if step_no < passes_count - 1:
            total = add(*parts)
            rest = exchange(raw, STAY, 1)
            more = step_no < passes_count - 2
            pair, own, *raws = call(
                meet_kernel, [(2 * row_dev, dim), (row_dev, dim)] + [(2 * row_dev, dim)] * more,
                rest, exchange(total, STAY, 1), exchange(total, top, 1), norm_gain,
                scratch_shapes=[] if more else [pltpu.VMEM((2 * row_dev, dim), jnp.bfloat16)],
            )
            raw = raws[0] if more else None
        else:
            low, high = split(*parts)
            rest = exchange(own, STAY, 1)
            own = add(rest, exchange(high, top, 1), exchange(low, STAY, 1))
    return own[None]


def solution(mesh):
    return jax.shard_map(
        on_device,
        mesh=mesh,
        in_specs=(
            P("segment", "expert", None),
            P("segment", None, "expert", None),
            P("segment", None, "expert", None),
            P("segment", None),
            P("segment", None, "expert"),
            P("segment", None, "expert"),
            P("segment", "expert", None),
        ),
        out_specs=P("segment", "expert", None),
        check_vma=False,
    )
```

```python
import functools

import jax
import jax.numpy as jnp
from jax import lax
from jax.experimental import pallas as pl
from jax.experimental.pallas import tpu as pltpu
from jax.sharding import PartitionSpec as P

GROUP = 4
LANES = 128
CHUNK = 1024
VMEM_LIMIT = 16 * 1024 * 1024
VMEM = pl.BlockSpec(memory_space=pltpu.VMEM)


def exchange(value, flips, hop):
    segments, owners = lax.axis_size("segment"), lax.axis_size("expert")
    if flips == (0, 0) and hop % segments == 0:
        return value
    pairs = []
    for seg in range(segments):
        for own in range(owners):
            target = (seg + hop) % segments * owners + (own ^ flips[own % 2])
            pairs.append((seg * owners + own, target))
    return lax.ppermute(value, ("segment", "expert"), pairs)


def upper_flips(owners):
    return [(1 << place,) * 2 for place in range(owners.bit_length() - 2, 2, -1)]


CORE = (1, 1)
SQUARE = ((2, 2), (4, 4), (6, 6))
STAY = (0, 0)


def spans(dim):
    return [slice(start, min(start + CHUNK, dim)) for start in range(0, dim, CHUNK)]


def call(kernel, outs, *args, **more):
    return pl.pallas_call(
        kernel,
        out_shape=[jax.ShapeDtypeStruct(shape, jnp.bfloat16) for shape in outs],
        in_specs=more.pop("in_specs", [VMEM] * len(args)),
        out_specs=[VMEM] * len(outs),
        compiler_params=pltpu.CompilerParams(vmem_limit_bytes=VMEM_LIMIT),
        **more,
    )(*args)


def load_kernel(count, *refs):
    sems = refs[-1]
    copies = [pltpu.make_async_copy(refs[place], refs[count + place], sems.at[place]) for place in range(count)]
    for copy in copies:
        copy.start()
    for copy in copies:
        copy.wait()


def load(*weights):
    count = len(weights)
    return pl.pallas_call(
        functools.partial(load_kernel, count),
        out_shape=[pltpu.VMEM(w.shape, w.dtype) for w in weights],
        in_specs=[pl.BlockSpec(memory_space=pltpu.HBM)] * count,
        out_specs=[VMEM] * count,
        scratch_shapes=[pltpu.SemaphoreType.DMA((count,))],
        compiler_params=pltpu.CompilerParams(vmem_limit_bytes=VMEM_LIMIT),
        cost_estimate=pl.CostEstimate(
            flops=0, bytes_accessed=sum(2 * w.size for w in weights), transcendentals=0
        ),
    )(*[pltpu.with_memory_space_constraint(w, pltpu.HBM) for w in weights])


def prepare_kernel(experts, states_hbm, routing_hbm, weight_hbm, out_ref, states_ref, routing_ref, weight_ref, sems):
    pairs = ((routing_hbm, routing_ref), (weight_hbm, weight_ref), (states_hbm, states_ref))
    copies = [pltpu.make_async_copy(source, target, sems.at[place]) for place, (source, target) in enumerate(pairs)]
    for copy in copies:
        copy.start()
    rows, dim = states_ref.shape[1:]
    copies[0].wait()
    copies[1].wait()
    lane = lax.broadcasted_iota(jnp.int32, (rows, LANES), 1).astype(jnp.float32)
    diagonal = lax.broadcasted_iota(jnp.int32, (rows, rows), 0) == lax.broadcasted_iota(jnp.int32, (rows, rows), 1)

    def upright(line):
        return jnp.sum(jnp.where(diagonal, line.astype(jnp.float32), 0.0), axis=1, keepdims=True)

    total = jnp.zeros((rows, LANES), jnp.float32)
    for step in range(routing_ref.shape[1]):
        for k in range(routing_ref.shape[2]):
            column = upright(routing_ref[0, step, k:k + 1, :]) + step * experts
            total += jnp.where(lane == column, upright(weight_ref[0, step, k:k + 1, :]), 0.0)
    out_ref[:, dim:] = total.astype(jnp.bfloat16)
    copies[2].wait()
    for span in spans(dim):
        out_ref[:, span] = states_ref[0, :, span]


def prepare(experts, states, routing, weight):
    args = [states, jnp.swapaxes(routing, 2, 3), jnp.swapaxes(weight, 2, 3)]
    rows, dim = states.shape[1:]
    (block,) = call(
        functools.partial(prepare_kernel, experts), [(rows, dim + LANES)],
        *[pltpu.with_memory_space_constraint(x, pltpu.HBM) for x in args],
        in_specs=[pl.BlockSpec(memory_space=pltpu.HBM)] * 3,
        scratch_shapes=[pltpu.VMEM(x.shape, x.dtype) for x in args] + [pltpu.SemaphoreType.DMA((3,))],
    )
    return block


def join_kernel(*refs):
    *parts, out_ref = refs
    for span in spans(out_ref.shape[1]):
        rows = [part[:, span].astype(jnp.float32) for part in parts]
        out_ref[:, span] = jnp.concatenate(rows, axis=0).astype(jnp.bfloat16)


def add_kernel(*refs):
    *parts, out_ref = refs
    for span in spans(out_ref.shape[1]):
        out_ref[:, span] = sum(part[:, span].astype(jnp.float32) for part in parts).astype(jnp.bfloat16)


def total_kernel(own_ref, *refs):
    *parts, out_ref = refs
    half = own_ref.shape[0]
    for span in spans(out_ref.shape[1]):
        total = sum(part[:, span].astype(jnp.float32) for part in parts)
        own = own_ref[:, span].astype(jnp.float32)
        out_ref[:, span] = jnp.concatenate([total[:half] + own, total[half:]], axis=0).astype(jnp.bfloat16)


def last_kernel(own_ref, *refs):
    *parts, low_ref, high_ref = refs
    half = own_ref.shape[0]
    for span in spans(low_ref.shape[1]):
        total = sum(part[:, span].astype(jnp.float32) for part in parts)
        low_ref[:, span] = (total[:half] + own_ref[:, span].astype(jnp.float32)).astype(jnp.bfloat16)
        high_ref[:, span] = total[half:].astype(jnp.bfloat16)


def split_kernel(count, *refs):
    parts, outs = refs[:-count], refs[-count:]
    rows = outs[0].shape[0]
    for span in spans(outs[0].shape[1]):
        total = sum(part[:, span].astype(jnp.float32) for part in parts)
        for place, out_ref in enumerate(outs):
            out_ref[:, span] = total[place * rows:(place + 1) * rows].astype(jnp.bfloat16)


def normalise(raw_ref, gain_ref, out_ref):
    rows, dim = raw_ref.shape
    square = jnp.zeros((rows, LANES), jnp.float32)
    for start in range(0, dim, LANES):
        piece = raw_ref[:, start:start + LANES].astype(jnp.float32)
        square += piece * piece
    inv = lax.rsqrt(jnp.sum(square, axis=1, keepdims=True) / dim + 1e-06)
    for span in spans(dim):
        scaled = raw_ref[:, span].astype(jnp.float32) * inv * gain_ref[:, span]
        out_ref[:, span] = scaled.astype(jnp.bfloat16)


def first_kernel(own_ref, far_ref, gain_ref, out_ref, raw_ref):
    dim = raw_ref.shape[1]
    for span in spans(dim):
        rows = [ref[:, span].astype(jnp.float32) for ref in (own_ref, far_ref)]
        raw_ref[:, span] = jnp.concatenate(rows, axis=0).astype(jnp.bfloat16)
    tails = [ref[:, dim:].astype(jnp.float32) for ref in (own_ref, far_ref)]
    out_ref[:, dim:] = jnp.concatenate(tails, axis=0).astype(jnp.bfloat16)
    normalise(raw_ref, gain_ref, out_ref)


def meet_kernel(near_ref, far_ref, gain_ref, out_ref, own_ref, raw_ref):
    half = own_ref.shape[0]
    for span in spans(out_ref.shape[1]):
        far = far_ref[:, span].astype(jnp.float32)
        total = near_ref[:, span].astype(jnp.float32) + jnp.concatenate([far[half:], far[:half]], axis=0)
        total = total.astype(jnp.bfloat16)
        raw_ref[:, span] = total
        own_ref[:, span] = total[:half]
    normalise(raw_ref, gain_ref, out_ref)


def mlp_kernel(step_no, *refs):
    x_refs, refs = refs[:8], refs[8:]
    if step_no > 0:
        tail_ref, refs = refs[0], refs[1:]
    (gate_ref, up_ref, down_ref), outs, refs = refs[:3], refs[3:11], refs[11:]
    part = outs[0].shape[0]
    dim, hidden = gate_ref.shape[1:]
    experts = lax.axis_size("expert") // GROUP
    column = step_no * experts + lax.axis_index("expert") // GROUP
    lane = lax.broadcasted_iota(jnp.int32, (part, LANES), 1)
    weights = []
    for place, ref in enumerate(x_refs):
        band = slice(place * part, (place + 1) * part)
        if step_no == 0:
            tail = ref[:, dim:]
            refs[0][band, :] = tail
        else:
            tail = tail_ref[band, :]
        chosen = jnp.where(lane == column, tail.astype(jnp.float32), 0.0)
        weights.append(jnp.sum(chosen, axis=1, keepdims=True))
    gated = jnp.zeros((8 * part, hidden), jnp.float32)
    up_part = jnp.zeros((8 * part, hidden), jnp.float32)
    for span in spans(dim):
        rows = jnp.concatenate([ref[:, span] for ref in x_refs], axis=0)
        gated += jnp.dot(rows, gate_ref[0, span, :], preferred_element_type=jnp.float32)
        up_part += jnp.dot(rows, up_ref[0, span, :], preferred_element_type=jnp.float32)
    inner = (gated / (1.0 + jnp.exp(-gated)) * up_part).astype(jnp.bfloat16)
    for span in spans(dim):
        terms = jnp.dot(inner, down_ref[0, :, span], preferred_element_type=jnp.float32)
        for place, out_ref in enumerate(outs):
            weight = weights[place]
            mine = terms[place * part:(place + 1) * part]
            out_ref[:, span] = jnp.where(weight > 0.0, weight * mine, 0.0).astype(jnp.bfloat16)


def mlp(step_no, xs, tail, gate, up, down):
    dim, hidden = gate.shape[1:]
    part = xs[0].shape[0]
    gate, up, down = [pltpu.with_memory_space_constraint(w, pltpu.VMEM) for w in (gate, up, down)]
    first = step_no == 0
    args = list(xs) + ([] if first else [tail]) + [gate, up, down]
    result = call(
        functools.partial(mlp_kernel, step_no), [(part, dim)] * 8 + [(8 * part, LANES)] * first, *args,
        cost_estimate=pl.CostEstimate(
            flops=48 * part * dim * hidden, bytes_accessed=6 * dim * hidden, transcendentals=0
        ),
    )
    return result[:8], result[8] if first else tail


def add(*parts):
    rows = parts[0].shape[0]
    dim = parts[-1].shape[1]
    return call(add_kernel, [(rows, dim)], *parts)[0]


def split(*parts):
    rows, dim = parts[0].shape
    return call(functools.partial(split_kernel, 2), [(rows // 2, dim)] * 2, *parts)


def join(*parts):
    return call(join_kernel, [(sum(part.shape[0] for part in parts), parts[0].shape[1])], *parts)[0]


def on_device(states, routing, route_weight, norm_gain, gate_proj, up_proj, down_proj):
    owners = lax.axis_size("expert")
    row_dev, dim = states.shape[1:]
    passes_count = routing.shape[1]
    top, *middle = upper_flips(owners)

    (gate,) = load(gate_proj)
    block = prepare(owners // GROUP, states, routing, route_weight)
    other = exchange(block, top, 0)
    other, gate = lax.optimization_barrier((other, gate))
    pair_rows = pltpu.VMEM((2 * row_dev, dim), jnp.bfloat16)
    (pair,) = call(
        first_kernel, [(2 * row_dev, dim + LANES)], block, other, norm_gain, scratch_shapes=[pair_rows]
    )
    pair, up_hbm, down_hbm = lax.optimization_barrier((pair, up_proj, down_proj))
    up, down = load(up_hbm, down_hbm)
    own, tail = states[0], None
    for step_no in range(passes_count):
        rows_a = pair
        for flips in middle:
            rows_a = join(rows_a, exchange(rows_a, flips, 0))
        mine = [rows_a] + [exchange(rows_a, flips, 0) for flips in SQUARE]
        near = rows_a
        if step_no == 0:
            near, up, down = lax.optimization_barrier((near, up, down))
        fars = [exchange(rows, CORE, 0) for rows in [near] + mine[1:]]
        outs, tail = mlp(step_no, mine + fars, tail, gate, up, down)

        kept, sent = outs[:4], [exchange(rows, CORE, 0) for rows in outs[4:]]
        parts = [kept[0], sent[0]]
        for place in (3, 2, 1):
            parts.append(exchange(add(kept[place], sent[place]), SQUARE[place - 1], 0))
        for flips in middle[::-1]:
            low, high = split(*parts)
            parts = [low, exchange(high, flips, 0)]
        if step_no < passes_count - 1:
            (total,) = call(total_kernel, [(2 * row_dev, dim)], own, *parts)
            pair, own = call(
                meet_kernel, [(2 * row_dev, dim), (row_dev, dim)],
                exchange(total, STAY, 1), exchange(total, top, 1), norm_gain, scratch_shapes=[pair_rows],
            )
        else:
            low, high = call(last_kernel, [(row_dev, dim)] * 2, own, *parts)
            own = add(exchange(high, top, 1), exchange(low, STAY, 1))
    return own[None]


def solution(mesh):
    return jax.shard_map(
        on_device,
        mesh=mesh,
        in_specs=(
            P("segment", "expert", None),
            P("segment", None, "expert", None),
            P("segment", None, "expert", None),
            P("segment", None),
            P("segment", None, "expert"),
            P("segment", None, "expert"),
            P("segment", "expert", None),
        ),
        out_specs=P("segment", "expert", None),
        check_vma=False,
    )
```

```python
import functools

import jax
import jax.numpy as jnp
from jax import lax
from jax.experimental import pallas as pl
from jax.experimental.pallas import tpu as pltpu
from jax.sharding import PartitionSpec as P

GROUP = 4
LANES = 128
CHUNK = 1024
VMEM_LIMIT = 16 * 1024 * 1024
VMEM = pl.BlockSpec(memory_space=pltpu.VMEM)


def exchange(value, flips, hop):
    segments, owners = lax.axis_size("segment"), lax.axis_size("expert")
    if flips == (0, 0) and hop % segments == 0:
        return value
    pairs = []
    for seg in range(segments):
        for own in range(owners):
            target = (seg + hop) % segments * owners + (own ^ flips[own % 2])
            pairs.append((seg * owners + own, target))
    return lax.ppermute(value, ("segment", "expert"), pairs)


def upper_flips(owners):
    return [(1 << place,) * 2 for place in range(owners.bit_length() - 2, 2, -1)]


CORE = (1, 1)
SQUARE = ((2, 2), (4, 4), (6, 6))
STAY = (0, 0)


def spans(dim):
    return [slice(start, min(start + CHUNK, dim)) for start in range(0, dim, CHUNK)]


def call(kernel, outs, *args, **more):
    return pl.pallas_call(
        kernel,
        out_shape=[jax.ShapeDtypeStruct(shape, jnp.bfloat16) for shape in outs],
        in_specs=more.pop("in_specs", [VMEM] * len(args)),
        out_specs=[VMEM] * len(outs),
        compiler_params=pltpu.CompilerParams(vmem_limit_bytes=VMEM_LIMIT),
        **more,
    )(*args)


def load_kernel(count, *refs):
    sems = refs[-1]
    copies = [pltpu.make_async_copy(refs[place], refs[count + place], sems.at[place]) for place in range(count)]
    for copy in copies:
        copy.start()
    for copy in copies:
        copy.wait()


def load(*weights):
    count = len(weights)
    return pl.pallas_call(
        functools.partial(load_kernel, count),
        out_shape=[pltpu.VMEM(w.shape, w.dtype) for w in weights],
        in_specs=[pl.BlockSpec(memory_space=pltpu.HBM)] * count,
        out_specs=[VMEM] * count,
        scratch_shapes=[pltpu.SemaphoreType.DMA((count,))],
        compiler_params=pltpu.CompilerParams(vmem_limit_bytes=VMEM_LIMIT),
        cost_estimate=pl.CostEstimate(
            flops=0, bytes_accessed=sum(2 * w.size for w in weights), transcendentals=0
        ),
    )(*[pltpu.with_memory_space_constraint(w, pltpu.HBM) for w in weights])


def prepare_kernel(experts, states_hbm, routing_hbm, weight_hbm, out_ref, states_ref, routing_ref, weight_ref, sems):
    pairs = ((routing_hbm, routing_ref), (weight_hbm, weight_ref), (states_hbm, states_ref))
    copies = [pltpu.make_async_copy(source, target, sems.at[place]) for place, (source, target) in enumerate(pairs)]
    for copy in copies:
        copy.start()
    rows, dim = states_ref.shape[1:]
    copies[0].wait()
    copies[1].wait()
    lane = lax.broadcasted_iota(jnp.int32, (rows, LANES), 1).astype(jnp.float32)
    diagonal = lax.broadcasted_iota(jnp.int32, (rows, rows), 0) == lax.broadcasted_iota(jnp.int32, (rows, rows), 1)

    def upright(line):
        return jnp.sum(jnp.where(diagonal, line.astype(jnp.float32), 0.0), axis=1, keepdims=True)

    total = jnp.zeros((rows, LANES), jnp.float32)
    for step in range(routing_ref.shape[1]):
        for k in range(routing_ref.shape[2]):
            column = upright(routing_ref[0, step, k:k + 1, :]) + step * experts
            total += jnp.where(lane == column, upright(weight_ref[0, step, k:k + 1, :]), 0.0)
    out_ref[:, dim:] = total.astype(jnp.bfloat16)
    copies[2].wait()
    for span in spans(dim):
        out_ref[:, span] = states_ref[0, :, span]


def prepare(experts, states, routing, weight):
    args = [states, jnp.swapaxes(routing, 2, 3), jnp.swapaxes(weight, 2, 3)]
    rows, dim = states.shape[1:]
    (block,) = call(
        functools.partial(prepare_kernel, experts), [(rows, dim + LANES)],
        *[pltpu.with_memory_space_constraint(x, pltpu.HBM) for x in args],
        in_specs=[pl.BlockSpec(memory_space=pltpu.HBM)] * 3,
        scratch_shapes=[pltpu.VMEM(x.shape, x.dtype) for x in args] + [pltpu.SemaphoreType.DMA((3,))],
    )
    return block


def join_kernel(*refs):
    *parts, out_ref = refs
    for span in spans(out_ref.shape[1]):
        rows = [part[:, span].astype(jnp.float32) for part in parts]
        out_ref[:, span] = jnp.concatenate(rows, axis=0).astype(jnp.bfloat16)


def add_kernel(*refs):
    *parts, out_ref = refs
    for span in spans(out_ref.shape[1]):
        out_ref[:, span] = sum(part[:, span].astype(jnp.float32) for part in parts).astype(jnp.bfloat16)


def split_kernel(count, *refs):
    parts, outs = refs[:-count], refs[-count:]
    rows = outs[0].shape[0]
    for span in spans(outs[0].shape[1]):
        total = sum(part[:, span].astype(jnp.float32) for part in parts)
        for place, out_ref in enumerate(outs):
            out_ref[:, span] = total[place * rows:(place + 1) * rows].astype(jnp.bfloat16)


def squares(piece):
    piece = piece.astype(jnp.float32)
    return sum(piece[:, start:start + LANES] * piece[:, start:start + LANES] for start in range(0, piece.shape[1], LANES))


def normalise(raw_ref, square, gain_ref, out_ref):
    dim = raw_ref.shape[1]
    inv = lax.rsqrt(jnp.sum(square, axis=1, keepdims=True) / dim + 1e-06)
    for span in spans(dim):
        scaled = raw_ref[:, span].astype(jnp.float32) * inv * gain_ref[:, span]
        out_ref[:, span] = scaled.astype(jnp.bfloat16)


def first_kernel(own_ref, far_ref, gain_ref, out_ref, raw_ref):
    dim = raw_ref.shape[1]
    square = 0.0
    for span in spans(dim):
        rows = [ref[:, span].astype(jnp.float32) for ref in (own_ref, far_ref)]
        joined = jnp.concatenate(rows, axis=0)
        square += squares(joined)
        raw_ref[:, span] = joined.astype(jnp.bfloat16)
    tails = [ref[:, dim:].astype(jnp.float32) for ref in (own_ref, far_ref)]
    out_ref[:, dim:] = jnp.concatenate(tails, axis=0).astype(jnp.bfloat16)
    normalise(raw_ref, square, gain_ref, out_ref)


def meet_kernel(rest_ref, near_ref, far_ref, gain_ref, out_ref, own_ref, raw_ref):
    half = own_ref.shape[0]
    square = 0.0
    for span in spans(out_ref.shape[1]):
        far = far_ref[:, span].astype(jnp.float32)
        total = rest_ref[:, span].astype(jnp.float32) + near_ref[:, span].astype(jnp.float32)
        total = (total + jnp.concatenate([far[half:], far[:half]], axis=0)).astype(jnp.bfloat16)
        square += squares(total)
        raw_ref[:, span] = total
        own_ref[:, span] = total[:half]
    normalise(raw_ref, square, gain_ref, out_ref)


def mlp_kernel(step_no, *refs):
    x_refs, refs = refs[:8], refs[8:]
    if step_no > 0:
        tail_ref, refs = refs[0], refs[1:]
    (gate_ref, up_ref, down_ref), outs, refs = refs[:3], refs[3:11], refs[11:]
    part = outs[0].shape[0]
    dim, hidden = gate_ref.shape[1:]
    experts = lax.axis_size("expert") // GROUP
    column = step_no * experts + lax.axis_index("expert") // GROUP
    lane = lax.broadcasted_iota(jnp.int32, (part, LANES), 1)
    weights = []
    for place, ref in enumerate(x_refs):
        band = slice(place * part, (place + 1) * part)
        if step_no == 0:
            tail = ref[:, dim:]
            refs[0][band, :] = tail
        else:
            tail = tail_ref[band, :]
        chosen = jnp.where(lane == column, tail.astype(jnp.float32), 0.0)
        weights.append(jnp.sum(chosen, axis=1, keepdims=True))
    gated = jnp.zeros((8 * part, hidden), jnp.float32)
    up_part = jnp.zeros((8 * part, hidden), jnp.float32)
    for span in spans(dim):
        rows = jnp.concatenate([ref[:, span] for ref in x_refs], axis=0)
        gated += jnp.dot(rows, gate_ref[0, span, :], preferred_element_type=jnp.float32)
        up_part += jnp.dot(rows, up_ref[0, span, :], preferred_element_type=jnp.float32)
    inner = (gated / (1.0 + jnp.exp(-gated)) * up_part).astype(jnp.bfloat16)
    for span in spans(dim):
        terms = jnp.dot(inner, down_ref[0, :, span], preferred_element_type=jnp.float32)
        for place, out_ref in enumerate(outs):
            weight = weights[place]
            mine = terms[place * part:(place + 1) * part]
            out_ref[:, span] = jnp.where(weight > 0.0, weight * mine, 0.0).astype(jnp.bfloat16)


def mlp(step_no, xs, tail, gate, up, down):
    dim, hidden = gate.shape[1:]
    part = xs[0].shape[0]
    gate, up, down = [pltpu.with_memory_space_constraint(w, pltpu.VMEM) for w in (gate, up, down)]
    first = step_no == 0
    args = list(xs) + ([] if first else [tail]) + [gate, up, down]
    result = call(
        functools.partial(mlp_kernel, step_no), [(part, dim)] * 8 + [(8 * part, LANES)] * first, *args,
        cost_estimate=pl.CostEstimate(
            flops=48 * part * dim * hidden, bytes_accessed=6 * dim * hidden, transcendentals=0
        ),
    )
    return result[:8], result[8] if first else tail


def add(*parts):
    rows = parts[0].shape[0]
    dim = parts[-1].shape[1]
    return call(add_kernel, [(rows, dim)], *parts)[0]


def split(*parts):
    rows, dim = parts[0].shape
    return call(functools.partial(split_kernel, 2), [(rows // 2, dim)] * 2, *parts)


def join(*parts):
    return call(join_kernel, [(sum(part.shape[0] for part in parts), parts[0].shape[1])], *parts)[0]


def on_device(states, routing, route_weight, norm_gain, gate_proj, up_proj, down_proj):
    owners = lax.axis_size("expert")
    row_dev, dim = states.shape[1:]
    passes_count = routing.shape[1]
    top, *middle = upper_flips(owners)

    (gate,) = load(gate_proj)
    block = prepare(owners // GROUP, states, routing, route_weight)
    other = exchange(block, top, 0)
    other, gate = lax.optimization_barrier((other, gate))
    pair, raw = call(first_kernel, [(2 * row_dev, dim + LANES), (2 * row_dev, dim)], block, other, norm_gain)
    pair, up_hbm, down_hbm = lax.optimization_barrier((pair, up_proj, down_proj))
    up, down = load(up_hbm, down_hbm)
    own, tail = states[0], None
    for step_no in range(passes_count):
        rows_a = pair
        for flips in middle:
            rows_a = join(rows_a, exchange(rows_a, flips, 0))
        mine = [rows_a] + [exchange(rows_a, flips, 0) for flips in SQUARE]
        near = rows_a
        if step_no == 0:
            near, up, down = lax.optimization_barrier((near, up, down))
        fars = [exchange(rows, CORE, 0) for rows in [near] + mine[1:]]
        outs, tail = mlp(step_no, mine + fars, tail, gate, up, down)

        kept, sent = outs[:4], [exchange(rows, CORE, 0) for rows in outs[4:]]
        parts = [kept[0], sent[0]]
        for place in (3, 2, 1):
            parts.append(exchange(add(kept[place], sent[place]), SQUARE[place - 1], 0))
        for flips in middle[::-1]:
            low, high = split(*parts)
            parts = [low, exchange(high, flips, 0)]
        if step_no < passes_count - 1:
            total = add(*parts)
            rest = exchange(raw, STAY, 1)
            more = step_no < passes_count - 2
            pair, own, *raws = call(
                meet_kernel, [(2 * row_dev, dim), (row_dev, dim)] + [(2 * row_dev, dim)] * more,
                rest, exchange(total, STAY, 1), exchange(total, top, 1), norm_gain,
                scratch_shapes=[] if more else [pltpu.VMEM((2 * row_dev, dim), jnp.bfloat16)],
            )
            raw = raws[0] if more else None
        else:
            low, high = split(*parts)
            rest = exchange(own, STAY, 1)
            own = add(rest, exchange(high, top, 1), exchange(low, STAY, 1))
    return own[None]


def solution(mesh):
    return jax.shard_map(
        on_device,
        mesh=mesh,
        in_specs=(
            P("segment", "expert", None),
            P("segment", None, "expert", None),
            P("segment", None, "expert", None),
            P("segment", None),
            P("segment", None, "expert"),
            P("segment", None, "expert"),
            P("segment", "expert", None),
        ),
        out_specs=P("segment", "expert", None),
        check_vma=False,
    )
```

```python
import functools

import jax
import jax.numpy as jnp
from jax import lax
from jax.experimental import pallas as pl
from jax.experimental.pallas import tpu as pltpu
from jax.sharding import PartitionSpec as P

GROUP = 4
LANES = 128
CHUNK = 1792
VMEM_LIMIT = 16 * 1024 * 1024
VMEM = pl.BlockSpec(memory_space=pltpu.VMEM)


def exchange(value, flips, hop):
    segments, owners = lax.axis_size("segment"), lax.axis_size("expert")
    if flips == (0, 0) and hop % segments == 0:
        return value
    pairs = []
    for seg in range(segments):
        for own in range(owners):
            target = (seg + hop) % segments * owners + (own ^ flips[own % 2])
            pairs.append((seg * owners + own, target))
    return lax.ppermute(value, ("segment", "expert"), pairs)


def upper_flips(owners):
    return [(1 << place,) * 2 for place in range(owners.bit_length() - 2, 2, -1)]


CORE = (1, 1)
SQUARE = ((2, 2), (4, 4), (6, 6))
STAY = (0, 0)


def spans(dim):
    return [slice(start, min(start + CHUNK, dim)) for start in range(0, dim, CHUNK)]


def call(kernel, outs, *args, **more):
    return pl.pallas_call(
        kernel,
        out_shape=[jax.ShapeDtypeStruct(shape, jnp.bfloat16) for shape in outs],
        in_specs=more.pop("in_specs", [VMEM] * len(args)),
        out_specs=[VMEM] * len(outs),
        compiler_params=pltpu.CompilerParams(vmem_limit_bytes=VMEM_LIMIT),
        **more,
    )(*args)


def load_kernel(count, *refs):
    sems = refs[-1]
    copies = [pltpu.make_async_copy(refs[place], refs[count + place], sems.at[place]) for place in range(count)]
    for copy in copies:
        copy.start()
    for copy in copies:
        copy.wait()


def load(*weights):
    count = len(weights)
    return pl.pallas_call(
        functools.partial(load_kernel, count),
        out_shape=[pltpu.VMEM(w.shape, w.dtype) for w in weights],
        in_specs=[pl.BlockSpec(memory_space=pltpu.HBM)] * count,
        out_specs=[VMEM] * count,
        scratch_shapes=[pltpu.SemaphoreType.DMA((count,))],
        compiler_params=pltpu.CompilerParams(vmem_limit_bytes=VMEM_LIMIT),
        cost_estimate=pl.CostEstimate(
            flops=0, bytes_accessed=sum(2 * w.size for w in weights), transcendentals=0
        ),
    )(*[pltpu.with_memory_space_constraint(w, pltpu.HBM) for w in weights])


def prepare_kernel(experts, states_hbm, routing_hbm, weight_hbm, out_ref, states_ref, routing_ref, weight_ref, sems):
    pairs = ((routing_hbm, routing_ref), (weight_hbm, weight_ref), (states_hbm, states_ref))
    copies = [pltpu.make_async_copy(source, target, sems.at[place]) for place, (source, target) in enumerate(pairs)]
    for copy in copies:
        copy.start()
    rows, dim = states_ref.shape[1:]
    copies[0].wait()
    copies[1].wait()
    lane = lax.broadcasted_iota(jnp.int32, (rows, LANES), 1).astype(jnp.float32)
    diagonal = lax.broadcasted_iota(jnp.int32, (rows, rows), 0) == lax.broadcasted_iota(jnp.int32, (rows, rows), 1)

    def upright(line):
        return jnp.sum(jnp.where(diagonal, line.astype(jnp.float32), 0.0), axis=1, keepdims=True)

    total = jnp.zeros((rows, LANES), jnp.float32)
    for step in range(routing_ref.shape[1]):
        for k in range(routing_ref.shape[2]):
            column = upright(routing_ref[0, step, k:k + 1, :]) + step * experts
            total += jnp.where(lane == column, upright(weight_ref[0, step, k:k + 1, :]), 0.0)
    out_ref[:, dim:] = total.astype(jnp.bfloat16)
    copies[2].wait()
    for span in spans(dim):
        out_ref[:, span] = states_ref[0, :, span]


def prepare(experts, states, routing, weight):
    args = [states, jnp.swapaxes(routing, 2, 3), jnp.swapaxes(weight, 2, 3)]
    rows, dim = states.shape[1:]
    (block,) = call(
        functools.partial(prepare_kernel, experts), [(rows, dim + LANES)],
        *[pltpu.with_memory_space_constraint(x, pltpu.HBM) for x in args],
        in_specs=[pl.BlockSpec(memory_space=pltpu.HBM)] * 3,
        scratch_shapes=[pltpu.VMEM(x.shape, x.dtype) for x in args] + [pltpu.SemaphoreType.DMA((3,))],
    )
    return block


def join_kernel(*refs):
    *parts, out_ref = refs
    for span in spans(out_ref.shape[1]):
        rows = [part[:, span].astype(jnp.float32) for part in parts]
        out_ref[:, span] = jnp.concatenate(rows, axis=0).astype(jnp.bfloat16)


def add_kernel(*refs):
    *parts, out_ref = refs
    for span in spans(out_ref.shape[1]):
        out_ref[:, span] = sum(part[:, span].astype(jnp.float32) for part in parts).astype(jnp.bfloat16)


def split_kernel(count, *refs):
    parts, outs = refs[:-count], refs[-count:]
    rows = outs[0].shape[0]
    for span in spans(outs[0].shape[1]):
        total = sum(part[:, span].astype(jnp.float32) for part in parts)
        for place, out_ref in enumerate(outs):
            out_ref[:, span] = total[place * rows:(place + 1) * rows].astype(jnp.bfloat16)


def squares(piece):
    piece = piece.astype(jnp.float32)
    return sum(piece[:, start:start + LANES] * piece[:, start:start + LANES] for start in range(0, piece.shape[1], LANES))


def normalise(raw_ref, square, gain_ref, out_ref):
    dim = raw_ref.shape[1]
    inv = lax.rsqrt(jnp.sum(square, axis=1, keepdims=True) / dim + 1e-06)
    for span in spans(dim):
        scaled = raw_ref[:, span].astype(jnp.float32) * inv * gain_ref[:, span]
        out_ref[:, span] = scaled.astype(jnp.bfloat16)


def first_kernel(own_ref, far_ref, gain_ref, out_ref, raw_ref):
    dim = raw_ref.shape[1]
    square = 0.0
    for span in spans(dim):
        rows = [ref[:, span].astype(jnp.float32) for ref in (own_ref, far_ref)]
        joined = jnp.concatenate(rows, axis=0)
        square += squares(joined)
        raw_ref[:, span] = joined.astype(jnp.bfloat16)
    tails = [ref[:, dim:].astype(jnp.float32) for ref in (own_ref, far_ref)]
    out_ref[:, dim:] = jnp.concatenate(tails, axis=0).astype(jnp.bfloat16)
    normalise(raw_ref, square, gain_ref, out_ref)


def meet_kernel(rest_ref, near_ref, far_ref, gain_ref, out_ref, own_ref, raw_ref):
    half = own_ref.shape[0]
    square = 0.0
    for span in spans(out_ref.shape[1]):
        far = far_ref[:, span].astype(jnp.float32)
        total = rest_ref[:, span].astype(jnp.float32) + near_ref[:, span].astype(jnp.float32)
        total = (total + jnp.concatenate([far[half:], far[:half]], axis=0)).astype(jnp.bfloat16)
        square += squares(total)
        raw_ref[:, span] = total
        own_ref[:, span] = total[:half]
    normalise(raw_ref, square, gain_ref, out_ref)


def mlp_kernel(step_no, *refs):
    x_refs, refs = refs[:8], refs[8:]
    if step_no > 0:
        tail_ref, refs = refs[0], refs[1:]
    (gate_ref, up_ref, down_ref), outs, refs = refs[:3], refs[3:11], refs[11:]
    part = outs[0].shape[0]
    dim, hidden = gate_ref.shape[1:]
    experts = lax.axis_size("expert") // GROUP
    column = step_no * experts + lax.axis_index("expert") // GROUP
    lane = lax.broadcasted_iota(jnp.int32, (part, LANES), 1)
    weights = []
    for place, ref in enumerate(x_refs):
        band = slice(place * part, (place + 1) * part)
        if step_no == 0:
            tail = ref[:, dim:]
            refs[0][band, :] = tail
        else:
            tail = tail_ref[band, :]
        chosen = jnp.where(lane == column, tail.astype(jnp.float32), 0.0)
        weights.append(jnp.sum(chosen, axis=1, keepdims=True))
    gated = jnp.zeros((8 * part, hidden), jnp.float32)
    up_part = jnp.zeros((8 * part, hidden), jnp.float32)
    for span in spans(dim):
        rows = jnp.concatenate([ref[:, span] for ref in x_refs], axis=0)
        gated += jnp.dot(rows, gate_ref[0, span, :], preferred_element_type=jnp.float32)
        up_part += jnp.dot(rows, up_ref[0, span, :], preferred_element_type=jnp.float32)
    inner = (gated / (1.0 + jnp.exp(-gated)) * up_part).astype(jnp.bfloat16)
    for span in spans(dim):
        terms = jnp.dot(inner, down_ref[0, :, span], preferred_element_type=jnp.float32)
        for place, out_ref in enumerate(outs):
            weight = weights[place]
            mine = terms[place * part:(place + 1) * part]
            out_ref[:, span] = jnp.where(weight > 0.0, weight * mine, 0.0).astype(jnp.bfloat16)


def mlp(step_no, xs, tail, gate, up, down):
    dim, hidden = gate.shape[1:]
    part = xs[0].shape[0]
    gate, up, down = [pltpu.with_memory_space_constraint(w, pltpu.VMEM) for w in (gate, up, down)]
    first = step_no == 0
    args = list(xs) + ([] if first else [tail]) + [gate, up, down]
    result = call(
        functools.partial(mlp_kernel, step_no), [(part, dim)] * 8 + [(8 * part, LANES)] * first, *args,
        cost_estimate=pl.CostEstimate(
            flops=48 * part * dim * hidden, bytes_accessed=6 * dim * hidden, transcendentals=0
        ),
    )
    return result[:8], result[8] if first else tail


def add(*parts):
    rows = parts[0].shape[0]
    dim = parts[-1].shape[1]
    return call(add_kernel, [(rows, dim)], *parts)[0]


def split(*parts):
    rows, dim = parts[0].shape
    return call(functools.partial(split_kernel, 2), [(rows // 2, dim)] * 2, *parts)


def join(*parts):
    return call(join_kernel, [(sum(part.shape[0] for part in parts), parts[0].shape[1])], *parts)[0]


def on_device(states, routing, route_weight, norm_gain, gate_proj, up_proj, down_proj):
    owners = lax.axis_size("expert")
    row_dev, dim = states.shape[1:]
    passes_count = routing.shape[1]
    top, *middle = upper_flips(owners)

    (gate,) = load(gate_proj)
    block = prepare(owners // GROUP, states, routing, route_weight)
    other = exchange(block, top, 0)
    other, gate = lax.optimization_barrier((other, gate))
    pair, raw = call(first_kernel, [(2 * row_dev, dim + LANES), (2 * row_dev, dim)], block, other, norm_gain)
    pair, up_hbm, down_hbm = lax.optimization_barrier((pair, up_proj, down_proj))
    up, down = load(up_hbm, down_hbm)
    own, tail = states[0], None
    for step_no in range(passes_count):
        rows_a = pair
        for flips in middle:
            rows_a = join(rows_a, exchange(rows_a, flips, 0))
        mine = [rows_a] + [exchange(rows_a, flips, 0) for flips in SQUARE]
        near = rows_a
        if step_no == 0:
            near, up, down = lax.optimization_barrier((near, up, down))
        fars = [exchange(rows, CORE, 0) for rows in [near] + mine[1:]]
        outs, tail = mlp(step_no, mine + fars, tail, gate, up, down)

        kept, sent = outs[:4], [exchange(rows, CORE, 0) for rows in outs[4:]]
        parts = [kept[0], sent[0]]
        for place in (3, 2, 1):
            parts.append(exchange(add(kept[place], sent[place]), SQUARE[place - 1], 0))
        for flips in middle[::-1]:
            low, high = split(*parts)
            parts = [low, exchange(high, flips, 0)]
        if step_no < passes_count - 1:
            total = add(*parts)
            rest = exchange(raw, STAY, 1)
            more = step_no < passes_count - 2
            pair, own, *raws = call(
                meet_kernel, [(2 * row_dev, dim), (row_dev, dim)] + [(2 * row_dev, dim)] * more,
                rest, exchange(total, STAY, 1), exchange(total, top, 1), norm_gain,
                scratch_shapes=[] if more else [pltpu.VMEM((2 * row_dev, dim), jnp.bfloat16)],
            )
            raw = raws[0] if more else None
        else:
            low, high = split(*parts)
            rest = exchange(own, STAY, 1)
            own = add(rest, exchange(high, top, 1), exchange(low, STAY, 1))
    return own[None]


def solution(mesh):
    return jax.shard_map(
        on_device,
        mesh=mesh,
        in_specs=(
            P("segment", "expert", None),
            P("segment", None, "expert", None),
            P("segment", None, "expert", None),
            P("segment", None),
            P("segment", None, "expert"),
            P("segment", None, "expert"),
            P("segment", "expert", None),
        ),
        out_specs=P("segment", "expert", None),
        check_vma=False,
    )
```
